256 devices in a mesh: seg: 8 (over z), tile: 32 (over x, y, core).
Axes of the slice: x: 4, y: 4, z: 8, core: 2. Of those that a mesh axis runs over, the one named last changes fastest.
Arguments:
- samples: bfloat16 [8, 4096, 2048], P('seg', 'tile'), may hold values from -512 to 512
- pair_list: int32 [2, 8192], P(None, 'tile'), may hold values from 0 to 4095, as said below
- sensor_home: int32 [4096], replicated, may hold values from 0 to 4095, as said below
Outputs:
- correlations: bfloat16 [2048, 8192], P('seg', 'tile')
The draws below stay inside these ranges and needn't reach their ends.
Inputs may be any that keep to these rules, and one draw needn't show every extreme that they name: `pair_list`: row 0 and row 1 name the two sensors of a pair, never the same one. Among the pairs of one index of tile (256 consecutive columns), the sensors whose stored rows lie in one block of 128 consecutive rows are at most 8 different ones. `sensor_home`: each number appears once.
All inputs are finite; a program needn't handle non-finite values.
Results may differ from the reference program's by a relative error of at most 0.019.
Values may be sent and summed in bfloat16 or wider, within the bound.
No kernel may reach another device: no remote copies, remote signals or barrier semaphores. Data moves between devices by JAX's collectives and lax.ppermute only.
A program may use at most 192 MiB of HBM per device.

```python
import math
import jax
import jax.numpy as jnp
from jax import lax

NFFT = 4096
SEG_LEN = 2048
NF = 2048
BAND = 64
NLAG = 2048
CAP = 8
SENS_DEV = 128
PAIR_DEV = 256
SEGS = 8
SENSORS = 4096
PAIRS = 8192


tone_count = 8


def shared_home(key):
    return jax.random.permutation(jax.random.fold_in(key, 101), SENSORS).astype(jnp.int32)


def draw_sensor_home(key, part):
    home_rows = shared_home(key)
    return home_rows


def draw_pair_list(key, part):
    home_rows = shared_home(key)
    key = jax.random.fold_in(key, 7)
    key_list = jax.random.split(key, 8)
    holders = SENSORS // SENS_DEV
    indices = jnp.arange(holders, dtype=jnp.int32)
    counts = jax.random.randint(key_list[0], (holders, holders), 0, CAP + 1)
    hot_owner = jax.random.randint(key_list[1], (), 0, holders)
    hot_tile = jax.random.randint(key_list[2], (), 0, holders)
    counts = jnp.where(indices[None, :] == hot_owner, CAP, counts)
    counts = jnp.where(indices[:, None] == hot_tile, CAP, counts)
    picked = jax.vmap(lambda k: jax.random.permutation(k, SENS_DEV)[:CAP])(jax.random.split(key_list[3], holders * holders))
    picked = picked.reshape(holders, holders, CAP).astype(jnp.int32)
    stored = (picked + (indices * SENS_DEV)[None, :, None]).reshape(holders, holders * CAP)
    slot_idx = jnp.arange(CAP, dtype=jnp.int32)
    is_live = (slot_idx[None, None, :] < counts[:, :, None]).reshape(holders, holders * CAP)
    mixing = jax.vmap(lambda k: jax.random.permutation(k, holders * CAP))(jax.random.split(key_list[4], holders)).astype(jnp.int32)
    scores = jnp.where(is_live, 0, holders * CAP) + mixing
    ordering = jnp.argsort(scores, axis=1)
    compact = jnp.take_along_axis(stored, ordering, axis=1)
    live_count = jnp.sum(is_live.astype(jnp.int32), axis=1)[:, None]
    pair_idx = jnp.arange(PAIR_DEV, dtype=jnp.int32)[None, :]
    first_draw = jax.random.randint(key_list[5], (holders, PAIR_DEV), 0, 1 << 20)
    second_draw = jax.random.randint(key_list[6], (holders, PAIR_DEV), 0, 1 << 20)
    rand_first = first_draw % live_count
    rand_second = (rand_first + 1 + second_draw % (live_count - 1)) % live_count
    covering = 2 * pair_idx < live_count
    pos_first = jnp.where(covering, 2 * pair_idx % live_count, rand_first)
    pos_second = jnp.where(covering, (2 * pair_idx + 1) % live_count, rand_second)
    shuffle = jax.vmap(lambda k: jax.random.permutation(k, PAIR_DEV))(jax.random.split(key_list[7], holders)).astype(jnp.int32)
    pos_first = jnp.take_along_axis(pos_first, shuffle, axis=1)
    pos_second = jnp.take_along_axis(pos_second, shuffle, axis=1)
    row_first = jnp.take_along_axis(compact, pos_first, axis=1)
    row_second = jnp.take_along_axis(compact, pos_second, axis=1)
    inverse = jnp.zeros((SENSORS,), jnp.int32).at[home_rows].set(jnp.arange(SENSORS, dtype=jnp.int32))
    return jnp.stack([inverse[row_first].reshape(-1), inverse[row_second].reshape(-1)]).astype(jnp.int32)


def draw_samples(key, part):
    key = jax.random.fold_in(key, 11)
    key_list = jax.random.split(key, 5)
    full_shape = (SEGS, SENSORS, SEG_LEN)
    sample_idx = jnp.arange(SEG_LEN, dtype=jnp.int32)
    noise_part = jnp.clip(jax.random.normal(key_list[0], full_shape, jnp.float32), -6.0, 6.0)
    gains = jnp.exp(jax.random.uniform(key_list[1], (SEGS, SENSORS, 1), jnp.float32, 0.0, math.log(10.0)))
    tone_bins = jax.random.randint(key_list[2], (SEGS, SENSORS, tone_count), 1, NF)
    tone_amps = jnp.exp(jax.random.uniform(key_list[3], (SEGS, SENSORS, tone_count), jnp.float32, math.log(0.2), math.log(2.0)))
    phases = jax.random.uniform(key_list[4], (SEGS, SENSORS, tone_count), jnp.float32, -math.pi, math.pi)
    summed_wave = noise_part
    for tone_idx in range(tone_count):
        cycle_idx = tone_bins[:, :, tone_idx:tone_idx + 1] * sample_idx % NFFT
        summed_wave = summed_wave + tone_amps[:, :, tone_idx:tone_idx + 1] * jnp.cos(cycle_idx.astype(jnp.float32) * (2.0 * math.pi / NFFT) + phases[:, :, tone_idx:tone_idx + 1])
    values = gains * summed_wave
    return jnp.clip(values, -512.0, 512.0).astype(jnp.bfloat16)


def setup_inputs(seed: int = 0) -> dict:
    seeds = jax.random.split(jax.random.key(seed), 4)
    return {
        "samples": draw_samples(jax.random.fold_in(seeds[3], 71), 0),
        "pair_list": draw_pair_list(jax.random.fold_in(seeds[3], 71), 0),
        "sensor_home": draw_sensor_home(jax.random.fold_in(seeds[3], 71), 0),
    }


def reference(samples, pair_list, sensor_home):
    rows_of = jnp.take(sensor_home, pair_list, axis=0)

    def add_segment(totals, seg_samples):
        spectrum = jnp.fft.rfft(seg_samples.astype(jnp.float32), n=NFFT, axis=1)[:, :NF]
        real_part = jnp.real(spectrum)
        imag_part = jnp.imag(spectrum)
        sensor_count = real_part.shape[0]
        real_band = real_part.reshape(sensor_count, NF // BAND, BAND)
        imag_band = imag_part.reshape(sensor_count, NF // BAND, BAND)
        band_power = lax.optimization_barrier(jnp.mean(real_band * real_band + imag_band * imag_band, axis=2, keepdims=True)) + 1e-05
        band_norm = jnp.sqrt(band_power)
        white_re = (real_band / band_norm).reshape(sensor_count, NF).astype(jnp.bfloat16)
        white_im = (imag_band / band_norm).reshape(sensor_count, NF).astype(jnp.bfloat16)
        re_first = jnp.take(white_re, rows_of[0], axis=0).astype(jnp.float32)
        im_first = jnp.take(white_im, rows_of[0], axis=0).astype(jnp.float32)
        re_second = jnp.take(white_re, rows_of[1], axis=0).astype(jnp.float32)
        im_second = jnp.take(white_im, rows_of[1], axis=0).astype(jnp.float32)
        new_re = totals[0] + (re_first * re_second + im_first * im_second)
        new_im = totals[1] + (im_first * re_second - re_first * im_second)
        return ((new_re, new_im), None)
    zero_rows = jnp.zeros((PAIRS, NF), jnp.float32)
    (stack_re, stack_im), _ = lax.scan(add_segment, (zero_rows, zero_rows), samples)
    packed = lax.complex(stack_re, stack_im)
    nyquist = jnp.zeros((PAIRS, 1), packed.dtype)
    series = jnp.fft.irfft(jnp.concatenate([packed, nyquist], axis=1), n=NFFT, axis=1)
    series = series * math.sqrt(NFFT / SEGS)
    lagged = jnp.concatenate([series[:, NFFT - NLAG // 2:], series[:, :NLAG // 2]], axis=1)
    return lagged.T.astype(jnp.bfloat16)
```

```python
import functools
import math

import jax
import jax.numpy as jnp
import numpy as np
from jax import lax
from jax.experimental import pallas as pl
from jax.experimental.pallas import tpu as pltpu
from jax.sharding import PartitionSpec as P

NFFT = 4096
NF = 2048
BAND = 64
NLAG = 2048
CAP = 8
RADIX = 32
LANES = 128
HALF = RADIX // 2
F32 = jnp.float32
BF16 = jnp.bfloat16


def _bins():
    k2 = np.arange(NF // RADIX)
    low = [np.arange(HALF), np.concatenate([[HALF], RADIX - np.arange(1, HALF)])]
    return np.concatenate([c[:, None] + RADIX * k2[None, :] for c in low], axis=1)


def _forward_tables():
    bins = _bins()
    n2 = np.arange(LANES)
    half = NF // RADIX
    tables = np.zeros((HALF, 2 * LANES, 2 * LANES))
    for j in range(HALF):
        angle = -2.0 * np.pi * ((n2[:, None] * bins[j][None, :]) % NFFT) / NFFT
        c, s = np.cos(angle), np.sin(angle)
        a, b = slice(0, half), slice(half, LANES)
        top, low = tables[j, :LANES], tables[j, LANES:]
        re, im = slice(0, LANES), slice(LANES, 2 * LANES)
        if j == 0:
            top[:, re][:, a], top[:, im][:, a] = c[:, a], s[:, a]
            low[:, re][:, b], low[:, im][:, b] = c[:, b], s[:, b]
        else:
            sign = np.where(np.arange(LANES) < half, 1.0, -1.0)[None, :]
            top[:, re], top[:, im] = c, s
            low[:, re], low[:, im] = -sign * s, sign * c
    return tables


def _inverse_tables(segments):
    bins = _bins()
    t2 = np.arange(LANES)
    half = NF // RADIX
    tables = np.zeros((HALF, 2 * LANES, 2 * LANES))
    for j in range(HALF):
        weight = np.where(bins[j] == 0, 1.0, 2.0) / math.sqrt(NFFT * segments)
        angle = 2.0 * np.pi * ((bins[j][:, None] * t2[None, :]) % NFFT) / NFFT
        wave = weight[:, None] * np.exp(1j * angle)
        if j == 0:
            for part, cols in ((slice(0, half), slice(0, LANES)), (slice(half, LANES), slice(LANES, 2 * LANES))):
                tables[0, :LANES, cols][part] = wave.real[part]
                tables[0, LANES:, cols][part] = -wave.imag[part]
        else:
            turn = (-1j) ** j
            first = (np.arange(LANES) < half)[:, None]
            of_re = turn * np.where(first, wave, np.conj(wave))
            of_im = turn * np.where(first, 1j * wave, np.conj(1j * wave))
            tables[j, :LANES, :LANES], tables[j, :LANES, LANES:] = of_re.real, of_re.imag
            tables[j, LANES:, :LANES], tables[j, LANES:, LANES:] = of_im.real, of_im.imag
    return tables


def _split(table):
    high = table.astype(BF16)
    low = (table - high.astype(np.float64)).astype(BF16)
    return high, low


def _band_table():
    lane = np.arange(LANES) % (NF // RADIX) // (BAND // RADIX)
    return (lane[:, None] == lane[None, :]).astype(np.float32) / BAND


def _turn(z, k, n, sign):
    re, im = z
    k = k % n
    if k == 0:
        return z
    if 4 * k == n:
        return (-im, re) if sign > 0 else (im, -re)
    if 2 * k == n:
        return (-re, -im)
    if 8 * k == n:
        r = math.sqrt(0.5)
        return ((re - im) * r, (re + im) * r) if sign > 0 else ((re + im) * r, (im - re) * r)
    c, s = math.cos(2 * math.pi * k / n), sign * math.sin(2 * math.pi * k / n)
    return (re * c - im * s, re * s + im * c)


def _add(a, b):
    return (a[0] + b[0], a[1] + b[1])


def _sub(a, b):
    return (a[0] - b[0], a[1] - b[1])


def _dft(z, sign):
    n = len(z)
    if n == 1:
        return list(z)
    half = n // 2
    even = _dft([_add(z[i], z[i + half]) for i in range(half)], sign)
    odd = _dft([_turn(_sub(z[i], z[i + half]), i, n, sign) for i in range(half)], sign)
    return [v for pair in zip(even, odd) for v in pair]


def _odd_bins(x):
    half = len(x) // 2
    z = [_turn((x[n], -x[n + half]), n, 4 * half, -1) if n else (x[0], -x[half]) for n in range(half)]
    return _dft(z, -1)


def _place_odd(out, d, n):
    for q, v in enumerate(d):
        k = 4 * q + 1
        if 2 * k <= n:
            out[k] = v
        else:
            out[n - k] = (v[0], -v[1])


def _rdft(x):
    n = len(x)
    if n == 2:
        return [(x[0] + x[1], None), (x[0] - x[1], None)]
    half = n // 2
    out = [None] * (half + 1)
    out[::2] = _rdft([x[i] + x[i + half] for i in range(half)])
    if n == 4:
        out[1] = (x[0] - x[2], x[3] - x[1])
    else:
        _place_odd(out, _odd_bins([x[i] - x[i + half] for i in range(half)]), n)
    return out


def _forward32(x):
    out = [None] * (HALF + 1)
    out[::2] = _rdft(x)
    _place_odd(out, _odd_bins(x), RADIX)
    return out


def _odd_adjoint(u, n):
    count = n // 4
    d = []
    for q in range(count):
        k = 4 * q + 1
        d.append(u[k] if 2 * k <= n else (u[n - k][0], -u[n - k][1]))
    z = _dft(d, 1)
    y = [_turn(z[i], i, n, 1) for i in range(count)]
    return [v[0] for v in y] + [-v[1] for v in y]


def _rdft_adjoint(u):
    n = 2 * (len(u) - 1)
    if n == 2:
        return [u[0][0] + u[1][0], u[0][0] - u[1][0]]
    a = _rdft_adjoint(u[::2])
    if n == 4:
        b = [u[1][0], -u[1][1]]
    else:
        b = _odd_adjoint(u, n)
    return [p + q for p, q in zip(a, b)] + [p - q for p, q in zip(a, b)]


def _inverse32(u):
    a = _rdft_adjoint(u[::2])
    b = _odd_adjoint(u, RADIX)
    return [p + q for p, q in zip(a, b)]


def _dot(a, b, dims=((1,), (0,))):
    return lax.dot_general(a, b, (dims, ((), ())), preferred_element_type=F32)


def _one_hot(index, rows):
    return (lax.broadcasted_iota(jnp.int32, (rows, index.shape[1]), 0) == index).astype(F32)


def request_kernel(holders, pair_ref, home_ref, want_ref, slot_ref, where_ref):
    pairs = jnp.concatenate([pair_ref[0:1, :], pair_ref[1:2, :]], axis=1)
    home = home_ref[...]
    high = _one_hot(pairs // LANES, home.shape[0]).astype(BF16)
    low = _one_hot(pairs % LANES, LANES)
    first = ((0,), (0,))
    owner = jnp.sum(_dot((home // LANES).astype(F32).astype(BF16), high, first) * low, axis=0, keepdims=True)
    place = jnp.sum(_dot((home % LANES).astype(F32).astype(BF16), high, first) * low, axis=0, keepdims=True)
    owner = owner.astype(jnp.int32)
    place = place.astype(jnp.int32)
    where_ref[0:1, :] = owner
    where_ref[1:2, :] = place
    owners = _one_hot(owner, holders).astype(BF16)
    places = _one_hot(place, LANES).astype(BF16)
    needed = jnp.minimum(_dot(owners, places, ((1,), (1,))), 1.0)
    row = lax.broadcasted_iota(jnp.int32, (LANES, LANES), 0)
    col = lax.broadcasted_iota(jnp.int32, (LANES, LANES), 1)
    slot = _dot(needed.astype(BF16), (row < col).astype(F32).astype(BF16))
    slot_ref[...] = slot
    marked = jnp.where(needed > 0.0, slot, -1.0)
    slots = lax.broadcasted_iota(jnp.int32, (CAP, LANES), 0).astype(F32)
    for holder in range(holders):
        want_ref[holder] = (marked[holder : holder + 1, :] == slots).astype(F32).astype(BF16)


def position_kernel(slot_ref, where_ref, pick_ref):
    owner = where_ref[0:1, :]
    place = where_ref[1:2, :]
    holders = slot_ref.shape[0]
    slot = jnp.minimum(slot_ref[...], CAP - 1.0)
    of_pair = _dot(slot.astype(BF16), _one_hot(owner, holders).astype(BF16), ((0,), (0,)))
    slot = jnp.sum(of_pair * _one_hot(place, LANES), axis=0, keepdims=True)
    position = owner * CAP + slot.astype(jnp.int32)
    pick_ref[...] = _one_hot(position, holders * CAP).T.astype(BF16)


ROWS = 16


def correlate_kernel(
    x_ref, pick_ref, band_ref, high_hbm, low_hbm, inverse_hbm,
    out_ref,
    high_ref, low_ref, inverse_ref, yh_ref, yl_ref, spec_ref, power_ref, u_ref, sems,
):
    copies = [
        pltpu.make_async_copy(src, dst, sems.at[i])
        for i, (src, dst) in enumerate(
            ((high_hbm, high_ref), (low_hbm, low_ref), (inverse_hbm, inverse_ref))
        )
    ]
    for copy in copies:
        copy.start()
    row_count = x_ref.shape[0]
    pair_count = pick_ref.shape[0] // 2
    re, im = slice(0, LANES), slice(LANES, 2 * LANES)

    def put(j, rows, cols, value):
        high = value.astype(BF16)
        yh_ref[j, rows, cols] = high
        yl_ref[j, rows, cols] = (value - high.astype(F32)).astype(BF16)

    @pl.loop(0, row_count // ROWS)
    def _(i):
        rows = pl.ds(pl.multiple_of(i * ROWS, ROWS), ROWS)
        x = [x_ref[rows, n * LANES : (n + 1) * LANES].astype(F32) for n in range(HALF)]
        y = _forward32(x)
        put(0, rows, re, y[0][0])
        put(0, rows, im, y[HALF][0])
        for j in range(1, HALF):
            put(j, rows, re, y[j][0])
            put(j, rows, im, y[j][1])

    copies[0].wait()
    copies[1].wait()
    power_ref[...] = jnp.zeros_like(power_ref)

    @pl.loop(0, HALF)
    def _(j):
        spec = _dot(yh_ref[j], high_ref[j]) + _dot(yh_ref[j], low_ref[j]) + _dot(yl_ref[j], high_ref[j])
        spec_ref[j] = spec
        power_ref[...] += spec[:, re] * spec[:, re] + spec[:, im] * spec[:, im]

    power = lax.dot_general(
        power_ref[...], band_ref[...], (((1,), (0,)), ((), ())),
        precision=lax.Precision.HIGHEST, preferred_element_type=F32,
    )
    power_ref[...] = 1.0 / jnp.sqrt(power + 1e-05)
    copies[2].wait()

    @pl.loop(0, HALF)
    def _(j):
        scale = power_ref[...]
        white = jnp.concatenate(
            [(spec_ref[j, :, re] * scale).astype(BF16), (spec_ref[j, :, im] * scale).astype(BF16)], axis=1
        )
        ends = _dot(pick_ref[...], white)
        a, c = ends[:pair_count], ends[pair_count:]
        cross = jnp.concatenate(
            [
                (a[:, re] * c[:, re] + a[:, im] * c[:, im]).astype(BF16),
                (a[:, im] * c[:, re] - a[:, re] * c[:, im]).astype(BF16),
            ],
            axis=1,
        )
        u_ref[j] = _dot(cross, inverse_ref[j])

    blocks = out_ref.shape[0]
    width = out_ref.shape[2] // LANES

    @pl.loop(0, pair_count // ROWS)
    def _(i):
        rows = pl.ds(pl.multiple_of(i * ROWS, ROWS), ROWS)
        u = [(u_ref[0, rows, re], None)]
        u += [(u_ref[j, rows, re], u_ref[j, rows, im]) for j in range(1, HALF)]
        u += [(u_ref[0, rows, im], None)]
        lags = _inverse32(u)
        for s in range(blocks):
            for h in range(width):
                out_ref[s, rows, h * LANES : (h + 1) * LANES] = lags[s * width + h].astype(BF16)


def sum_kernel(parts_ref, out_ref):
    total = parts_ref[0].astype(F32)
    for s in range(1, parts_ref.shape[0]):
        total = total + parts_ref[s].astype(F32)
    out_ref[...] = total.T.astype(BF16)


VMEM = pl.BlockSpec(memory_space=pltpu.VMEM)
ANY = pl.BlockSpec(memory_space=pl.ANY)


def shards(samples, pair_list, sensor_home):
    tiles = lax.axis_size("tile")
    segments = lax.axis_size("seg")
    local = samples[0]
    sens_dev, seg_len = local.shape
    pair_dev = pair_list.shape[1]
    rows = tiles * CAP
    shape = jax.ShapeDtypeStruct
    want, slot, where = pl.pallas_call(
        functools.partial(request_kernel, tiles),
        out_shape=(
            shape((tiles, CAP, sens_dev), BF16),
            shape((tiles, sens_dev), F32),
            shape((2, 2 * pair_dev), jnp.int32),
        ),
        in_specs=[VMEM] * 2,
        out_specs=(VMEM,) * 3,
        name="request",
    )(pair_list, sensor_home.reshape(-1, LANES))
    asked = lax.all_to_all(want, "tile", split_axis=0, concat_axis=0, tiled=True)
    pick = pl.pallas_call(
        position_kernel,
        out_shape=shape((2 * pair_dev, rows), BF16),
        in_specs=[VMEM] * 2,
        out_specs=VMEM,
        name="position",
    )(slot, where)
    outgoing = jnp.dot(asked.reshape(rows, sens_dev), local, preferred_element_type=F32).astype(BF16)
    arrived = lax.all_to_all(
        outgoing.reshape(tiles, CAP, seg_len), "tile", split_axis=0, concat_axis=0, tiled=True
    )
    high, low = _split(_forward_tables())
    inverse = _inverse_tables(segments).astype(BF16)
    block = (HALF, 2 * LANES, 2 * LANES)
    partial = pl.pallas_call(
        correlate_kernel,
        out_shape=shape((segments, pair_dev, NLAG // segments), BF16),
        in_specs=[VMEM, VMEM, VMEM, ANY, ANY, ANY],
        out_specs=VMEM,
        scratch_shapes=[
            pltpu.VMEM(block, BF16),
            pltpu.VMEM(block, BF16),
            pltpu.VMEM(block, BF16),
            pltpu.VMEM((HALF, rows, 2 * LANES), BF16),
            pltpu.VMEM((HALF, rows, 2 * LANES), BF16),
            pltpu.VMEM((HALF, rows, 2 * LANES), F32),
            pltpu.VMEM((rows, LANES), F32),
            pltpu.VMEM((HALF, pair_dev, 2 * LANES), F32),
            pltpu.SemaphoreType.DMA((3,)),
        ],
        compiler_params=pltpu.CompilerParams(vmem_limit_bytes=40 * 1024 * 1024),
        name="correlate",
    )(arrived.reshape(rows, seg_len), pick, jnp.asarray(_band_table()), jnp.asarray(high), jnp.asarray(low), jnp.asarray(inverse))
    parts = lax.all_to_all(partial, "seg", split_axis=0, concat_axis=0, tiled=True)
    return pl.pallas_call(
        sum_kernel,
        out_shape=shape((NLAG // segments, pair_dev), BF16),
        in_specs=[VMEM],
        out_specs=VMEM,
        name="stack",
    )(parts)


def solution(mesh):
    return jax.shard_map(
        shards,
        mesh=mesh,
        in_specs=(P("seg", "tile", None), P(None, "tile"), P()),
        out_specs=P("seg", "tile"),
        check_vma=False,
    )
```

```python
import functools
import math

import jax
import jax.numpy as jnp
import numpy as np
from jax import lax
from jax.experimental import pallas as pl
from jax.experimental.pallas import tpu as pltpu
from jax.sharding import PartitionSpec as P

NFFT = 4096
NF = 2048
BAND = 64
NLAG = 2048
CAP = 8
RADIX = 32
LANES = 128
HALF = RADIX // 2
F32 = jnp.float32
BF16 = jnp.bfloat16


def _bins():
    k2 = np.arange(NF // RADIX)
    low = [np.arange(HALF), np.concatenate([[HALF], RADIX - np.arange(1, HALF)])]
    return np.concatenate([c[:, None] + RADIX * k2[None, :] for c in low], axis=1)


def _forward_tables():
    bins = _bins()
    n2 = np.arange(LANES)
    half = NF // RADIX
    tables = np.zeros((HALF, 2 * LANES, 2 * LANES))
    for j in range(HALF):
        angle = -2.0 * np.pi * ((n2[:, None] * bins[j][None, :]) % NFFT) / NFFT
        c, s = np.cos(angle), np.sin(angle)
        a, b = slice(0, half), slice(half, LANES)
        top, low = tables[j, :LANES], tables[j, LANES:]
        re, im = slice(0, LANES), slice(LANES, 2 * LANES)
        if j == 0:
            top[:, re][:, a], top[:, im][:, a] = c[:, a], s[:, a]
            low[:, re][:, b], low[:, im][:, b] = c[:, b], s[:, b]
        else:
            sign = np.where(np.arange(LANES) < half, 1.0, -1.0)[None, :]
            top[:, re], top[:, im] = c, s
            low[:, re], low[:, im] = -sign * s, sign * c
    return tables


def _inverse_tables(segments):
    bins = _bins()
    t2 = np.arange(LANES)
    half = NF // RADIX
    tables = np.zeros((HALF, 2 * LANES, 2 * LANES))
    for j in range(HALF):
        weight = np.where(bins[j] == 0, 1.0, 2.0) / math.sqrt(NFFT * segments)
        angle = 2.0 * np.pi * ((bins[j][:, None] * t2[None, :]) % NFFT) / NFFT
        wave = weight[:, None] * np.exp(1j * angle)
        if j == 0:
            for part, cols in ((slice(0, half), slice(0, LANES)), (slice(half, LANES), slice(LANES, 2 * LANES))):
                tables[0, :LANES, cols][part] = wave.real[part]
                tables[0, LANES:, cols][part] = -wave.imag[part]
        else:
            turn = (-1j) ** j
            first = (np.arange(LANES) < half)[:, None]
            of_re = turn * np.where(first, wave, np.conj(wave))
            of_im = turn * np.where(first, 1j * wave, np.conj(1j * wave))
            tables[j, :LANES, :LANES], tables[j, :LANES, LANES:] = of_re.real, of_re.imag
            tables[j, LANES:, :LANES], tables[j, LANES:, LANES:] = of_im.real, of_im.imag
    return tables


def _split(table):
    high = table.astype(BF16)
    low = (table - high.astype(np.float64)).astype(BF16)
    return high, low


def _turn(z, k, n, sign):
    re, im = z
    k = k % n
    if k == 0:
        return z
    if 4 * k == n:
        return (-im, re) if sign > 0 else (im, -re)
    if 2 * k == n:
        return (-re, -im)
    if 8 * k == n:
        r = math.sqrt(0.5)
        return ((re - im) * r, (re + im) * r) if sign > 0 else ((re + im) * r, (im - re) * r)
    c, s = math.cos(2 * math.pi * k / n), sign * math.sin(2 * math.pi * k / n)
    return (re * c - im * s, re * s + im * c)


def _add(a, b):
    return (a[0] + b[0], a[1] + b[1])


def _sub(a, b):
    return (a[0] - b[0], a[1] - b[1])


def _dft(z, sign):
    n = len(z)
    if n == 1:
        return list(z)
    half = n // 2
    even = _dft([_add(z[i], z[i + half]) for i in range(half)], sign)
    odd = _dft([_turn(_sub(z[i], z[i + half]), i, n, sign) for i in range(half)], sign)
    return [v for pair in zip(even, odd) for v in pair]


def _odd_bins(x):
    half = len(x) // 2
    z = [_turn((x[n], -x[n + half]), n, 4 * half, -1) if n else (x[0], -x[half]) for n in range(half)]
    return _dft(z, -1)


def _place_odd(out, d, n):
    for q, v in enumerate(d):
        k = 4 * q + 1
        if 2 * k <= n:
            out[k] = v
        else:
            out[n - k] = (v[0], -v[1])


def _rdft(x):
    n = len(x)
    if n == 2:
        return [(x[0] + x[1], None), (x[0] - x[1], None)]
    half = n // 2
    out = [None] * (half + 1)
    out[::2] = _rdft([x[i] + x[i + half] for i in range(half)])
    if n == 4:
        out[1] = (x[0] - x[2], x[3] - x[1])
    else:
        _place_odd(out, _odd_bins([x[i] - x[i + half] for i in range(half)]), n)
    return out


def _forward32(x):
    out = [None] * (HALF + 1)
    out[::2] = _rdft(x)
    _place_odd(out, _odd_bins(x), RADIX)
    return out


def _odd_adjoint(u, n):
    count = n // 4
    d = []
    for q in range(count):
        k = 4 * q + 1
        d.append(u[k] if 2 * k <= n else (u[n - k][0], -u[n - k][1]))
    z = _dft(d, 1)
    y = [_turn(z[i], i, n, 1) for i in range(count)]
    return [v[0] for v in y] + [-v[1] for v in y]


def _rdft_adjoint(u):
    n = 2 * (len(u) - 1)
    if n == 2:
        return [u[0][0] + u[1][0], u[0][0] - u[1][0]]
    a = _rdft_adjoint(u[::2])
    if n == 4:
        b = [u[1][0], -u[1][1]]
    else:
        b = _odd_adjoint(u, n)
    return [p + q for p, q in zip(a, b)] + [p - q for p, q in zip(a, b)]


def _inverse32(u):
    a = _rdft_adjoint(u[::2])
    b = _odd_adjoint(u, RADIX)
    return [p + q for p, q in zip(a, b)]


def _dot(a, b, dims=((1,), (0,))):
    return lax.dot_general(a, b, (dims, ((), ())), preferred_element_type=F32)


def _band_mean(power):
    row = lax.broadcasted_iota(jnp.int32, (LANES, LANES), 0) % (NF // RADIX) // (BAND // RADIX)
    col = lax.broadcasted_iota(jnp.int32, (LANES, LANES), 1) % (NF // RADIX) // (BAND // RADIX)
    share = jnp.where(row == col, 1.0 / BAND, 0.0)
    return lax.dot_general(
        power, share, (((1,), (0,)), ((), ())), precision=lax.Precision.HIGHEST, preferred_element_type=F32
    )


def _one_hot(index, rows):
    return (lax.broadcasted_iota(jnp.int32, (rows, index.shape[1]), 0) == index).astype(F32)


def request_kernel(holders, pair_hbm, home_hbm, want_ref, slot_ref, where_ref, pair_ref, home_ref, sems):
    copies = [
        pltpu.make_async_copy(pair_hbm, pair_ref, sems.at[0]),
        pltpu.make_async_copy(home_hbm, home_ref, sems.at[1]),
    ]
    for copy in copies:
        copy.start()
    for copy in copies:
        copy.wait()
    pairs = jnp.concatenate([pair_ref[0:1, :], pair_ref[1:2, :]], axis=1)
    home = home_ref[...]
    high = _one_hot(pairs // LANES, home.shape[0]).astype(BF16)
    low = _one_hot(pairs % LANES, LANES)
    first = ((0,), (0,))
    owner = jnp.sum(_dot((home // LANES).astype(F32).astype(BF16), high, first) * low, axis=0, keepdims=True)
    place = jnp.sum(_dot((home % LANES).astype(F32).astype(BF16), high, first) * low, axis=0, keepdims=True)
    owner = owner.astype(jnp.int32)
    place = place.astype(jnp.int32)
    where_ref[0:1, :] = owner
    where_ref[1:2, :] = place
    owners = _one_hot(owner, holders).astype(BF16)
    places = _one_hot(place, LANES).astype(BF16)
    needed = jnp.minimum(_dot(owners, places, ((1,), (1,))), 1.0)
    row = lax.broadcasted_iota(jnp.int32, (LANES, LANES), 0)
    col = lax.broadcasted_iota(jnp.int32, (LANES, LANES), 1)
    slot = _dot(needed.astype(BF16), (row < col).astype(F32).astype(BF16))
    slot_ref[...] = slot
    marked = jnp.where(needed > 0.0, slot, -1.0)
    slots = lax.broadcasted_iota(jnp.int32, (CAP, LANES), 0).astype(F32)
    for holder in range(holders):
        want_ref[holder] = (marked[holder : holder + 1, :] == slots).astype(F32).astype(BF16)


def position_kernel(slot_ref, where_ref, pick_ref):
    owner = where_ref[0:1, :]
    place = where_ref[1:2, :]
    holders = slot_ref.shape[0]
    slot = jnp.minimum(slot_ref[...], CAP - 1.0)
    of_pair = _dot(slot.astype(BF16), _one_hot(owner, holders).astype(BF16), ((0,), (0,)))
    slot = jnp.sum(of_pair * _one_hot(place, LANES), axis=0, keepdims=True)
    position = owner * CAP + slot.astype(jnp.int32)
    pick_ref[...] = _one_hot(position, holders * CAP).T.astype(BF16)


ROWS = 16


def correlate_kernel(
    x_ref, pick_ref, table_hbm,
    lags_ref, far_ref,
    table_ref, yh_ref, yl_ref, spec_ref, power_ref, u_ref, sems,
):
    row_count = x_ref.shape[0]
    pair_count = pick_ref.shape[0] // 2
    re, im = slice(0, LANES), slice(LANES, 2 * LANES)
    group = table_ref.shape[0] // sems.shape[0]
    copies = []
    for i in range(sems.shape[0]):
        part = pl.ds(i * group, group)
        copies.append(pltpu.make_async_copy(table_hbm.at[part], table_ref.at[part], sems.at[i]))
        copies[i].start()

    def put(j, rows, cols, value):
        high = value.astype(BF16)
        yh_ref[j, rows, cols] = high
        yl_ref[j, rows, cols] = (value - high.astype(F32)).astype(BF16)

    @pl.loop(0, row_count // ROWS)
    def _(i):
        rows = pl.ds(pl.multiple_of(i * ROWS, ROWS), ROWS)
        x = [x_ref[rows, n * LANES : (n + 1) * LANES].astype(F32) for n in range(HALF)]
        y = _forward32(x)
        put(0, rows, re, y[0][0])
        put(0, rows, im, y[HALF][0])
        for j in range(1, HALF):
            put(j, rows, re, y[j][0])
            put(j, rows, im, y[j][1])

    for j in range(HALF):
        if 2 * j % group == 0:
            copies[2 * j // group].wait()
        high, low = table_ref[2 * j], table_ref[2 * j + 1]
        spec = _dot(yh_ref[j], high) + _dot(yh_ref[j], low) + _dot(yl_ref[j], high)
        spec_ref[j] = spec
        power = spec[:, re] * spec[:, re] + spec[:, im] * spec[:, im]
        power_ref[...] = power if j == 0 else power_ref[...] + power

    power_ref[...] = 1.0 / jnp.sqrt(_band_mean(power_ref[...]) + 1e-05)

    for copy in copies[2 * HALF // group :]:
        copy.wait()

    def ends_of(j):
        scale = power_ref[...]
        white = jnp.concatenate(
            [(spec_ref[j, :, re] * scale).astype(BF16), (spec_ref[j, :, im] * scale).astype(BF16)], axis=1
        )
        return _dot(pick_ref[...], white)

    ahead = ends_of(0)
    for j in range(HALF):
        ends = ahead
        if j + 1 < HALF:
            ahead = ends_of(j + 1)
        a, c = ends[:pair_count], ends[pair_count:]
        cross = jnp.concatenate(
            [
                (a[:, re] * c[:, re] + a[:, im] * c[:, im]).astype(BF16),
                (a[:, im] * c[:, re] - a[:, re] * c[:, im]).astype(BF16),
            ],
            axis=1,
        )
        u_ref[j] = _dot(cross, table_ref[2 * HALF + j])

    me = lax.axis_index("seg")
    blocks = lags_ref.shape[0]
    width = lags_ref.shape[2] // LANES

    @pl.loop(0, pair_count // ROWS)
    def _(i):
        rows = pl.ds(pl.multiple_of(i * ROWS, ROWS), ROWS)
        u = [(u_ref[0, rows, re], None)]
        u += [(u_ref[j, rows, re], u_ref[j, rows, im]) for j in range(1, HALF)]
        u += [(u_ref[0, rows, im], None)]
        lags = _inverse32(u)
        for s in range(blocks):
            place = lax.rem(s - me + blocks, blocks)
            for h in range(width):
                lags_ref[place, rows, h * LANES : (h + 1) * LANES] = lags[s * width + h].astype(BF16)

    far_ref[...] = lags_ref[blocks // 2]


def pack_kernel(lags_ref, up_ref, down_ref, keep_ref):
    up_ref[0], up_ref[1] = lags_ref[3], lags_ref[1]
    down_ref[0], down_ref[1] = lags_ref[5], lags_ref[7]
    keep_ref[0], keep_ref[1], keep_ref[2] = lags_ref[2], lags_ref[6], lags_ref[0]


def relay_kernel(keep_ref, up_ref, down_ref, far_ref, up_out_ref, down_out_ref):
    even = lax.axis_index("tile") % 2 == 0
    far = far_ref[...].astype(F32)
    up = keep_ref[0].astype(F32) + up_ref[0].astype(F32) + jnp.where(even, far, 0.0)
    down = keep_ref[1].astype(F32) + down_ref[0].astype(F32) + jnp.where(even, 0.0, far)
    up_out_ref[...] = up.astype(BF16)
    down_out_ref[...] = down.astype(BF16)


def sum_kernel(keep_ref, up_ref, down_ref, far_up_ref, far_down_ref, out_ref):
    total = keep_ref[2].astype(F32) + up_ref[1].astype(F32) + down_ref[1].astype(F32)
    total = total + far_up_ref[...].astype(F32) + far_down_ref[...].astype(F32)
    out_ref[...] = total.T.astype(BF16)


VMEM = pl.BlockSpec(memory_space=pltpu.VMEM)
ANY = pl.BlockSpec(memory_space=pl.ANY)
MIB = 1024 * 1024


def _call(kernel, name, inputs, outputs, args, scratch=(), limit=4, cost=None):
    return pl.pallas_call(
        kernel,
        out_shape=outputs,
        in_specs=inputs,
        out_specs=(VMEM,) * len(outputs),
        scratch_shapes=scratch,
        compiler_params=pltpu.CompilerParams(vmem_limit_bytes=limit * MIB),
        cost_estimate=cost,
        name=name,
    )(*args)


def _in_hbm(value):
    return pltpu.with_memory_space_constraint(value, pltpu.HBM)


def shards(samples, pair_list, sensor_home):
    tiles = lax.axis_size("tile")
    segments = lax.axis_size("seg")
    local = samples[0]
    sens_dev, seg_len = local.shape
    pair_dev = pair_list.shape[1]
    rows = tiles * CAP
    lags = NLAG // segments
    shape = jax.ShapeDtypeStruct
    home = sensor_home.reshape(-1, LANES)
    want, slot, where = _call(
        functools.partial(request_kernel, tiles),
        "request",
        [ANY] * 2,
        (
            shape((tiles, CAP, sens_dev), BF16),
            shape((tiles, sens_dev), F32),
            shape((2, 2 * pair_dev), jnp.int32),
        ),
        (_in_hbm(pair_list), _in_hbm(home)),
        [
            pltpu.VMEM(pair_list.shape, jnp.int32),
            pltpu.VMEM(home.shape, jnp.int32),
            pltpu.SemaphoreType.DMA((2,)),
        ],
    )
    asked = lax.all_to_all(want, "tile", split_axis=0, concat_axis=0, tiled=True)
    (pick,) = _call(
        position_kernel, "position", [VMEM] * 2, (shape((2 * pair_dev, rows), BF16),), (slot, where)
    )
    asked, pick = lax.optimization_barrier((asked, pick))
    outgoing = jnp.dot(asked.reshape(rows, sens_dev), local, preferred_element_type=F32).astype(BF16)
    arrived = lax.all_to_all(
        outgoing.reshape(tiles, CAP, seg_len), "tile", split_axis=0, concat_axis=0, tiled=True
    )
    high, low = _split(_forward_tables())
    tables = np.stack([high, low], axis=1).reshape(2 * HALF, 2 * LANES, 2 * LANES)
    inverse = _inverse_tables(segments).astype(BF16)
    tables = np.concatenate([tables, inverse])
    lag_block = (pair_dev, lags)
    blocks, far = _call(
        correlate_kernel,
        "correlate",
        [VMEM] * 2 + [ANY],
        (pltpu.VMEM((segments,) + lag_block, BF16), pltpu.VMEM(lag_block, BF16)),
        (arrived.reshape(rows, seg_len), pick, _in_hbm(jnp.asarray(tables))),
        [
            pltpu.VMEM(tables.shape, BF16),
            pltpu.VMEM((HALF, rows, 2 * LANES), BF16),
            pltpu.VMEM((HALF, rows, 2 * LANES), BF16),
            pltpu.VMEM((HALF, rows, 2 * LANES), F32),
            pltpu.VMEM((rows, LANES), F32),
            pltpu.VMEM((HALF, pair_dev, 2 * LANES), F32),
            pltpu.SemaphoreType.DMA((12,)),
        ],
        limit=40,
    )
    up, down, keep = _call(
        pack_kernel,
        "pack",
        [VMEM],
        tuple(pltpu.VMEM((n,) + lag_block, BF16) for n in (2, 2, 3)),
        (blocks,),
        cost=pl.CostEstimate(flops=5_000_000_000, bytes_accessed=10_000_000, transcendentals=0),
    )

    def shift(value, even, odd):
        ring = [
            (s * tiles + t, (s + (odd if t % 2 else even)) % segments * tiles + t)
            for s in range(segments)
            for t in range(tiles)
        ]
        return lax.ppermute(value, ("seg", "tile"), ring)

    up, down = shift(up, 1, 1), shift(down, -1, -1)
    far = shift(far, 2, -2)
    on_up, on_down = _call(
        relay_kernel,
        "relay",
        [VMEM] * 4,
        (pltpu.VMEM(lag_block, BF16),) * 2,
        (keep, up, down, far),
    )
    on_up, on_down = shift(on_up, 2, 2), shift(on_down, -2, -2)
    (out,) = _call(
        sum_kernel,
        "stack",
        [VMEM] * 5,
        (shape((lags, pair_dev), BF16),),
        (keep, up, down, on_up, on_down),
    )
    return out


def solution(mesh):
    return jax.shard_map(
        shards,
        mesh=mesh,
        in_specs=(P("seg", "tile", None), P(None, "tile"), P()),
        out_specs=P("seg", "tile"),
        check_vma=False,
    )
```

```python
import functools
import math

import jax
import jax.numpy as jnp
import numpy as np
from jax import lax
from jax.experimental import pallas as pl
from jax.experimental.pallas import tpu as pltpu
from jax.sharding import PartitionSpec as P

NFFT = 4096
NF = 2048
BAND = 64
NLAG = 2048
CAP = 8
RADIX = 32
LANES = 128
HALF = RADIX // 2
F32 = jnp.float32
BF16 = jnp.bfloat16


def _bins():
    k2 = np.arange(NF // RADIX)
    low = [np.arange(HALF), np.concatenate([[HALF], RADIX - np.arange(1, HALF)])]
    return np.concatenate([c[:, None] + RADIX * k2[None, :] for c in low], axis=1)


def _forward_tables():
    bins = _bins()
    n2 = np.arange(LANES)
    half = NF // RADIX
    tables = np.zeros((HALF, 2 * LANES, 2 * LANES))
    for j in range(HALF):
        angle = -2.0 * np.pi * ((n2[:, None] * bins[j][None, :]) % NFFT) / NFFT
        c, s = np.cos(angle), np.sin(angle)
        a, b = slice(0, half), slice(half, LANES)
        top, low = tables[j, :LANES], tables[j, LANES:]
        re, im = slice(0, LANES), slice(LANES, 2 * LANES)
        if j == 0:
            top[:, re][:, a], top[:, im][:, a] = c[:, a], s[:, a]
            low[:, re][:, b], low[:, im][:, b] = c[:, b], s[:, b]
        else:
            sign = np.where(np.arange(LANES) < half, 1.0, -1.0)[None, :]
            top[:, re], top[:, im] = c, s
            low[:, re], low[:, im] = -sign * s, sign * c
    return tables


def _inverse_tables(segments):
    bins = _bins()
    t2 = np.arange(LANES)
    half = NF // RADIX
    tables = np.zeros((HALF, 2 * LANES, 2 * LANES))
    for j in range(HALF):
        weight = np.where(bins[j] == 0, 1.0, 2.0) / math.sqrt(NFFT * segments)
        angle = 2.0 * np.pi * ((bins[j][:, None] * t2[None, :]) % NFFT) / NFFT
        wave = weight[:, None] * np.exp(1j * angle)
        if j == 0:
            for part, cols in ((slice(0, half), slice(0, LANES)), (slice(half, LANES), slice(LANES, 2 * LANES))):
                tables[0, :LANES, cols][part] = wave.real[part]
                tables[0, LANES:, cols][part] = -wave.imag[part]
        else:
            turn = (-1j) ** j
            first = (np.arange(LANES) < half)[:, None]
            of_re = turn * np.where(first, wave, np.conj(wave))
            of_im = turn * np.where(first, 1j * wave, np.conj(1j * wave))
            tables[j, :LANES, :LANES], tables[j, :LANES, LANES:] = of_re.real, of_re.imag
            tables[j, LANES:, :LANES], tables[j, LANES:, LANES:] = of_im.real, of_im.imag
    return tables


def _upper_halves(tables, inverse):
    upper = tables[:, :LANES].copy()
    upper[0] += tables[0, LANES:]
    inverse_upper = inverse[:, :LANES].copy()
    folded = inverse[0, :, :LANES] + inverse[0, :, LANES:]
    inverse_upper[0] = np.concatenate([folded[:LANES], folded[LANES:]], axis=1)
    return upper, inverse_upper


def _forward_whole(j, upper):
    c, s = upper[:, :LANES], upper[:, LANES:]
    first = lax.broadcasted_iota(jnp.int32, c.shape, 1) < NF // RADIX
    none = jnp.zeros_like(c)
    if j == 0:
        above = [jnp.where(first, c, none), jnp.where(first, s, none)]
        below = [jnp.where(first, none, c), jnp.where(first, none, s)]
    else:
        above = [c, s]
        below = [jnp.where(first, -s, s), jnp.where(first, c, -c)]
    return jnp.concatenate([jnp.concatenate(above, axis=1), jnp.concatenate(below, axis=1)], axis=0)


def _inverse_whole(j, upper):
    half = NF // RADIX
    a, b = upper[:, :LANES], upper[:, LANES:]
    none = jnp.zeros_like(a[:half])
    if j == 0:
        parts = [(a[:half], none), (none, a[half:]), (b[:half], none), (none, b[half:])]
    else:
        parts = [(a[:half], b[:half]), (a[half:], b[half:]), (-b[:half], a[:half]), (b[half:], -a[half:])]
    return jnp.concatenate([jnp.concatenate(p, axis=1) for p in parts], axis=0)


def _split(table):
    high = table.astype(BF16)
    low = (table - high.astype(np.float64)).astype(BF16)
    return high, low


def _turn(z, k, n, sign):
    re, im = z
    k = k % n
    if k == 0:
        return z
    if 4 * k == n:
        return (-im, re) if sign > 0 else (im, -re)
    if 2 * k == n:
        return (-re, -im)
    if 8 * k == n:
        r = math.sqrt(0.5)
        return ((re - im) * r, (re + im) * r) if sign > 0 else ((re + im) * r, (im - re) * r)
    c, s = math.cos(2 * math.pi * k / n), sign * math.sin(2 * math.pi * k / n)
    return (re * c - im * s, re * s + im * c)


def _add(a, b):
    return (a[0] + b[0], a[1] + b[1])


def _sub(a, b):
    return (a[0] - b[0], a[1] - b[1])


def _dft(z, sign):
    n = len(z)
    if n == 1:
        return list(z)
    half = n // 2
    even = _dft([_add(z[i], z[i + half]) for i in range(half)], sign)
    odd = _dft([_turn(_sub(z[i], z[i + half]), i, n, sign) for i in range(half)], sign)
    return [v for pair in zip(even, odd) for v in pair]


def _odd_bins(x):
    half = len(x) // 2
    z = [_turn((x[n], -x[n + half]), n, 4 * half, -1) if n else (x[0], -x[half]) for n in range(half)]
    return _dft(z, -1)


def _place_odd(out, d, n):
    for q, v in enumerate(d):
        k = 4 * q + 1
        if 2 * k <= n:
            out[k] = v
        else:
            out[n - k] = (v[0], -v[1])


def _rdft(x):
    n = len(x)
    if n == 2:
        return [(x[0] + x[1], None), (x[0] - x[1], None)]
    half = n // 2
    out = [None] * (half + 1)
    out[::2] = _rdft([x[i] + x[i + half] for i in range(half)])
    if n == 4:
        out[1] = (x[0] - x[2], x[3] - x[1])
    else:
        _place_odd(out, _odd_bins([x[i] - x[i + half] for i in range(half)]), n)
    return out


def _forward32(x):
    out = [None] * (HALF + 1)
    out[::2] = _rdft(x)
    _place_odd(out, _odd_bins(x), RADIX)
    return out


def _odd_adjoint(u, n):
    count = n // 4
    d = []
    for q in range(count):
        k = 4 * q + 1
        d.append(u[k] if 2 * k <= n else (u[n - k][0], -u[n - k][1]))
    z = _dft(d, 1)
    y = [_turn(z[i], i, n, 1) for i in range(count)]
    return [v[0] for v in y] + [-v[1] for v in y]


def _rdft_adjoint(u):
    n = 2 * (len(u) - 1)
    if n == 2:
        return [u[0][0] + u[1][0], u[0][0] - u[1][0]]
    a = _rdft_adjoint(u[::2])
    if n == 4:
        b = [u[1][0], -u[1][1]]
    else:
        b = _odd_adjoint(u, n)
    return [p + q for p, q in zip(a, b)] + [p - q for p, q in zip(a, b)]


def _inverse32(u):
    a = _rdft_adjoint(u[::2])
    b = _odd_adjoint(u, RADIX)
    return [p + q for p, q in zip(a, b)]


def _dot(a, b, dims=((1,), (0,))):
    return lax.dot_general(a, b, (dims, ((), ())), preferred_element_type=F32)


def _band_mean(power):
    row = lax.broadcasted_iota(jnp.int32, (LANES, LANES), 0) % (NF // RADIX) // (BAND // RADIX)
    col = lax.broadcasted_iota(jnp.int32, (LANES, LANES), 1) % (NF // RADIX) // (BAND // RADIX)
    share = jnp.where(row == col, 1.0 / BAND, 0.0)
    return lax.dot_general(
        power, share, (((1,), (0,)), ((), ())), precision=lax.Precision.HIGHEST, preferred_element_type=F32
    )


def _one_hot(index, rows):
    return (lax.broadcasted_iota(jnp.int32, (rows, index.shape[1]), 0) == index).astype(F32)


def request_kernel(holders, pair_hbm, home_hbm, want_ref, slot_ref, where_ref, pair_ref, home_ref, sems):
    copies = [
        pltpu.make_async_copy(pair_hbm, pair_ref, sems.at[0]),
        pltpu.make_async_copy(home_hbm, home_ref, sems.at[1]),
    ]
    for copy in copies:
        copy.start()
    for copy in copies:
        copy.wait()
    pairs = jnp.concatenate([pair_ref[0:1, :], pair_ref[1:2, :]], axis=1)
    home = home_ref[...]
    high = _one_hot(pairs // LANES, home.shape[0]).astype(BF16)
    low = _one_hot(pairs % LANES, LANES)
    first = ((0,), (0,))
    owner = jnp.sum(_dot((home // LANES).astype(F32).astype(BF16), high, first) * low, axis=0, keepdims=True)
    place = jnp.sum(_dot((home % LANES).astype(F32).astype(BF16), high, first) * low, axis=0, keepdims=True)
    owner = owner.astype(jnp.int32)
    place = place.astype(jnp.int32)
    where_ref[0:1, :] = owner
    where_ref[1:2, :] = place
    owners = _one_hot(owner, holders).astype(BF16)
    places = _one_hot(place, LANES).astype(BF16)
    needed = jnp.minimum(_dot(owners, places, ((1,), (1,))), 1.0)
    row = lax.broadcasted_iota(jnp.int32, (LANES, LANES), 0)
    col = lax.broadcasted_iota(jnp.int32, (LANES, LANES), 1)
    slot = _dot(needed.astype(BF16), (row < col).astype(F32).astype(BF16))
    slot_ref[...] = slot
    marked = jnp.where(needed > 0.0, slot, -1.0)
    slots = lax.broadcasted_iota(jnp.int32, (CAP, LANES), 0).astype(F32)
    for holder in range(holders):
        want_ref[holder] = (marked[holder : holder + 1, :] == slots).astype(F32).astype(BF16)


def position_kernel(slot_ref, where_ref, pick_ref):
    owner = where_ref[0:1, :]
    place = where_ref[1:2, :]
    holders = slot_ref.shape[0]
    slot = jnp.minimum(slot_ref[...], CAP - 1.0)
    of_pair = _dot(slot.astype(BF16), _one_hot(owner, holders).astype(BF16), ((0,), (0,)))
    slot = jnp.sum(of_pair * _one_hot(place, LANES), axis=0, keepdims=True)
    position = owner * CAP + slot.astype(jnp.int32)
    pick_ref[...] = _one_hot(position, holders * CAP).T.astype(BF16)


ROWS = 16


def transform_kernel(x_ref, table_hbm, yh_ref, yl_ref, table_ref, sem):
    copy = pltpu.make_async_copy(table_hbm, table_ref, sem.at[0])
    copy.start()
    row_count = x_ref.shape[0]
    re, im = slice(0, LANES), slice(LANES, 2 * LANES)

    def put(j, rows, cols, value):
        high = value.astype(BF16)
        yh_ref[j, rows, cols] = high
        yl_ref[j, rows, cols] = (value - high.astype(F32)).astype(BF16)

    @pl.loop(0, row_count // ROWS)
    def _(i):
        rows = pl.ds(pl.multiple_of(i * ROWS, ROWS), ROWS)
        x = [x_ref[rows, n * LANES : (n + 1) * LANES].astype(F32) for n in range(HALF)]
        y = _forward32(x)
        put(0, rows, re, y[0][0])
        put(0, rows, im, y[HALF][0])
        for j in range(1, HALF):
            put(j, rows, re, y[j][0])
            put(j, rows, im, y[j][1])

    copy.wait()


def correlate_kernel(yh_ref, yl_ref, table_ref, pick_ref, lags_ref, spec_ref, power_ref, u_ref):
    pair_count = pick_ref.shape[0] // 2
    re, im = slice(0, LANES), slice(LANES, 2 * LANES)
    for j in range(HALF):
        high, low = _forward_whole(j, table_ref[2 * j]), _forward_whole(j, table_ref[2 * j + 1])
        spec = _dot(yh_ref[j], high) + _dot(yh_ref[j], low) + _dot(yl_ref[j], high)
        spec_ref[j] = spec
        power = spec[:, re] * spec[:, re] + spec[:, im] * spec[:, im]
        power_ref[...] = power if j == 0 else power_ref[...] + power

    power_ref[...] = 1.0 / jnp.sqrt(_band_mean(power_ref[...]) + 1e-05)

    def ends_of(j):
        scale = power_ref[...]
        white = jnp.concatenate(
            [(spec_ref[j, :, re] * scale).astype(BF16), (spec_ref[j, :, im] * scale).astype(BF16)], axis=1
        )
        return _dot(pick_ref[...], white)

    ahead = ends_of(0)
    for j in range(HALF):
        ends = ahead
        if j + 1 < HALF:
            ahead = ends_of(j + 1)
        a, c = ends[:pair_count], ends[pair_count:]
        cross = jnp.concatenate(
            [
                (a[:, re] * c[:, re] + a[:, im] * c[:, im]).astype(BF16),
                (a[:, im] * c[:, re] - a[:, re] * c[:, im]).astype(BF16),
            ],
            axis=1,
        )
        u_ref[j] = _dot(cross, _inverse_whole(j, table_ref[2 * HALF + j]))

    me = lax.axis_index("seg")
    even = lax.axis_index("tile") % 2 == 0
    blocks = lags_ref.shape[0]
    width = lags_ref.shape[2] // LANES

    @pl.loop(0, pair_count // ROWS)
    def _(i):
        rows = pl.ds(pl.multiple_of(i * ROWS, ROWS), ROWS)
        u = [(u_ref[0, rows, re], None)]
        u += [(u_ref[j, rows, re], u_ref[j, rows, im]) for j in range(1, HALF)]
        u += [(u_ref[0, rows, im], None)]
        lags = _inverse32(u)
        for s in range(blocks):
            place = lax.rem(jnp.where(even, s - me, me - s) + blocks, blocks)
            for h in range(width):
                lags_ref[place, rows, h * LANES : (h + 1) * LANES] = lags[s * width + h].astype(BF16)


def pack_kernel(lags_ref, far_ref, ahead_ref, back_ref, ahead1_ref, back1_ref, keep_ref):
    far_ref[...] = lags_ref[4]
    ahead_ref[...], back_ref[...] = lags_ref[3], lags_ref[5]
    ahead1_ref[...], back1_ref[...] = lags_ref[1], lags_ref[7]
    keep_ref[0], keep_ref[1], keep_ref[2] = lags_ref[0], lags_ref[2], lags_ref[6]


def relay_kernel(keep_ref, far_ref, ahead_ref, back_ref, ahead_out_ref, back_out_ref):
    ahead = keep_ref[1].astype(F32) + far_ref[...].astype(F32) + ahead_ref[...].astype(F32)
    back = keep_ref[2].astype(F32) + back_ref[...].astype(F32)
    ahead_out_ref[...] = ahead.astype(BF16)
    back_out_ref[...] = back.astype(BF16)


def sum_kernel(keep_ref, ahead_ref, back_ref, ahead2_ref, back2_ref, out_ref):
    total = keep_ref[0].astype(F32) + ahead_ref[...].astype(F32) + back_ref[...].astype(F32)
    total = total + ahead2_ref[...].astype(F32) + back2_ref[...].astype(F32)
    out_ref[...] = total.T.astype(BF16)


VMEM = pl.BlockSpec(memory_space=pltpu.VMEM)
ANY = pl.BlockSpec(memory_space=pl.ANY)
MIB = 1024 * 1024


def _call(kernel, name, inputs, outputs, args, scratch=(), limit=4):
    return pl.pallas_call(
        kernel,
        out_shape=outputs,
        in_specs=inputs,
        out_specs=(VMEM,) * len(outputs),
        scratch_shapes=scratch,
        compiler_params=pltpu.CompilerParams(vmem_limit_bytes=limit * MIB),
        name=name,
    )(*args)


def _in_hbm(value):
    return pltpu.with_memory_space_constraint(value, pltpu.HBM)


def shards(samples, pair_list, sensor_home):
    tiles = lax.axis_size("tile")
    segments = lax.axis_size("seg")
    local = samples[0]
    sens_dev, seg_len = local.shape
    pair_dev = pair_list.shape[1]
    rows = tiles * CAP
    lags = NLAG // segments
    shape = jax.ShapeDtypeStruct
    home = sensor_home.reshape(-1, LANES)
    want, slot, where = _call(
        functools.partial(request_kernel, tiles),
        "request",
        [ANY] * 2,
        (
            shape((tiles, CAP, sens_dev), BF16),
            shape((tiles, sens_dev), F32),
            shape((2, 2 * pair_dev), jnp.int32),
        ),
        (_in_hbm(pair_list), _in_hbm(home)),
        [
            pltpu.VMEM(pair_list.shape, jnp.int32),
            pltpu.VMEM(home.shape, jnp.int32),
            pltpu.SemaphoreType.DMA((2,)),
        ],
    )
    asked = lax.all_to_all(want, "tile", split_axis=0, concat_axis=0, tiled=True)
    (pick,) = _call(
        position_kernel, "position", [VMEM] * 2, (shape((2 * pair_dev, rows), BF16),), (slot, where)
    )
    asked, pick = lax.optimization_barrier((asked, pick))
    outgoing = jnp.dot(asked.reshape(rows, sens_dev), local, preferred_element_type=F32).astype(BF16)
    arrived = lax.all_to_all(
        outgoing.reshape(tiles, CAP, seg_len), "tile", split_axis=0, concat_axis=0, tiled=True
    )
    forward, inverse = _upper_halves(_forward_tables(), _inverse_tables(segments))
    tables = np.stack(_split(forward), axis=1).reshape(2 * HALF, LANES, 2 * LANES)
    tables = np.concatenate([tables, inverse.astype(BF16)])
    lag_block = (pair_dev, lags)
    spectra = pltpu.VMEM((HALF, rows, 2 * LANES), BF16)
    yh, yl, tables = _call(
        transform_kernel,
        "transform",
        [VMEM, ANY],
        (spectra, spectra, pltpu.VMEM(tables.shape, BF16)),
        (arrived.reshape(rows, seg_len), _in_hbm(jnp.asarray(tables))),
        [pltpu.SemaphoreType.DMA((1,))],
        limit=16,
    )
    (blocks,) = _call(
        correlate_kernel,
        "correlate",
        [VMEM] * 4,
        (pltpu.VMEM((segments,) + lag_block, BF16),),
        (yh, yl, tables, pick),
        [
            pltpu.VMEM((HALF, rows, 2 * LANES), F32),
            pltpu.VMEM((rows, LANES), F32),
            pltpu.VMEM((HALF, pair_dev, 2 * LANES), F32),
        ],
        limit=24,
    )
    far, ahead, back, ahead1, back1, keep = _call(
        pack_kernel,
        "pack",
        [VMEM],
        tuple(pltpu.VMEM(n + lag_block, BF16) for n in ((), (), (), (), (), (3,))),
        (blocks,),
    )

    def shift(value, steps):
        ring = [
            (s * tiles + t, (s + (-steps if t % 2 else steps)) % segments * tiles + t)
            for s in range(segments)
            for t in range(tiles)
        ]
        return lax.ppermute(value, ("seg", "tile"), ring)

    far, ahead, back = shift(far, 2), shift(ahead, 1), shift(back, -1)
    ahead1, back1 = shift(ahead1, 1), shift(back1, -1)
    ahead2, back2 = _call(
        relay_kernel,
        "relay",
        [VMEM] * 4,
        (pltpu.VMEM(lag_block, BF16),) * 2,
        (keep, far, ahead, back),
    )
    ahead2, back2 = shift(ahead2, 2), shift(back2, -2)
    (out,) = _call(
        sum_kernel,
        "stack",
        [VMEM] * 5,
        (shape((lags, pair_dev), BF16),),
        (keep, ahead1, back1, ahead2, back2),
    )
    return out


def solution(mesh):
    return jax.shard_map(
        shards,
        mesh=mesh,
        in_specs=(P("seg", "tile", None), P(None, "tile"), P()),
        out_specs=P("seg", "tile"),
        check_vma=False,
    )
```

```python
import functools
import math

import jax
import jax.numpy as jnp
import numpy as np
from jax import lax
from jax.experimental import pallas as pl
from jax.experimental.pallas import tpu as pltpu
from jax.sharding import PartitionSpec as P

NFFT = 4096
NF = 2048
BAND = 64
NLAG = 2048
CAP = 8
RADIX = 32
LANES = 128
HALF = RADIX // 2
F32 = jnp.float32
BF16 = jnp.bfloat16


def _bins():
    k2 = np.arange(NF // RADIX)
    low = [np.arange(HALF), np.concatenate([[HALF], RADIX - np.arange(1, HALF)])]
    return np.concatenate([c[:, None] + RADIX * k2[None, :] for c in low], axis=1)


def _forward_tables():
    bins = _bins()
    n2 = np.arange(LANES)
    half = NF // RADIX
    tables = np.zeros((HALF, 2 * LANES, 2 * LANES))
    for j in range(HALF):
        angle = -2.0 * np.pi * ((n2[:, None] * bins[j][None, :]) % NFFT) / NFFT
        c, s = np.cos(angle), np.sin(angle)
        a, b = slice(0, half), slice(half, LANES)
        top, low = tables[j, :LANES], tables[j, LANES:]
        re, im = slice(0, LANES), slice(LANES, 2 * LANES)
        if j == 0:
            top[:, re][:, a], top[:, im][:, a] = c[:, a], s[:, a]
            low[:, re][:, b], low[:, im][:, b] = c[:, b], s[:, b]
        else:
            sign = np.where(np.arange(LANES) < half, 1.0, -1.0)[None, :]
            top[:, re], top[:, im] = c, s
            low[:, re], low[:, im] = -sign * s, sign * c
    return tables


def _inverse_tables(segments):
    bins = _bins()
    t2 = np.arange(LANES)
    half = NF // RADIX
    tables = np.zeros((HALF, 2 * LANES, 2 * LANES))
    for j in range(HALF):
        weight = np.where(bins[j] == 0, 1.0, 2.0) / math.sqrt(NFFT * segments)
        angle = 2.0 * np.pi * ((bins[j][:, None] * t2[None, :]) % NFFT) / NFFT
        wave = weight[:, None] * np.exp(1j * angle)
        if j == 0:
            for part, cols in ((slice(0, half), slice(0, LANES)), (slice(half, LANES), slice(LANES, 2 * LANES))):
                tables[0, :LANES, cols][part] = wave.real[part]
                tables[0, LANES:, cols][part] = -wave.imag[part]
        else:
            turn = (-1j) ** j
            first = (np.arange(LANES) < half)[:, None]
            of_re = turn * np.where(first, wave, np.conj(wave))
            of_im = turn * np.where(first, 1j * wave, np.conj(1j * wave))
            tables[j, :LANES, :LANES], tables[j, :LANES, LANES:] = of_re.real, of_re.imag
            tables[j, LANES:, :LANES], tables[j, LANES:, LANES:] = of_im.real, of_im.imag
    return tables


def _upper_halves(tables, inverse):
    upper = tables[:, :LANES].copy()
    upper[0] += tables[0, LANES:]
    inverse_upper = inverse[:, :LANES].copy()
    folded = inverse[0, :, :LANES] + inverse[0, :, LANES:]
    inverse_upper[0] = np.concatenate([folded[:LANES], folded[LANES:]], axis=1)
    return upper, inverse_upper


def _forward_whole(j, upper):
    c, s = upper[:, :LANES], upper[:, LANES:]
    first = lax.broadcasted_iota(jnp.int32, c.shape, 1) < NF // RADIX
    none = jnp.zeros_like(c)
    if j == 0:
        above = [jnp.where(first, c, none), jnp.where(first, s, none)]
        below = [jnp.where(first, none, c), jnp.where(first, none, s)]
    else:
        above = [c, s]
        below = [jnp.where(first, -s, s), jnp.where(first, c, -c)]
    return jnp.concatenate([jnp.concatenate(above, axis=1), jnp.concatenate(below, axis=1)], axis=0)


def _inverse_whole(j, upper):
    half = NF // RADIX
    a, b = upper[:, :LANES], upper[:, LANES:]
    none = jnp.zeros_like(a[:half])
    if j == 0:
        parts = [(a[:half], none), (none, a[half:]), (b[:half], none), (none, b[half:])]
    else:
        parts = [(a[:half], b[:half]), (a[half:], b[half:]), (-b[:half], a[:half]), (b[half:], -a[half:])]
    return jnp.concatenate([jnp.concatenate(p, axis=1) for p in parts], axis=0)


def _split(table):
    high = table.astype(BF16)
    low = (table - high.astype(np.float64)).astype(BF16)
    return high, low


def _turn(z, k, n, sign):
    re, im = z
    k = k % n
    if k == 0:
        return z
    if 4 * k == n:
        return (-im, re) if sign > 0 else (im, -re)
    if 2 * k == n:
        return (-re, -im)
    if 8 * k == n:
        r = math.sqrt(0.5)
        return ((re - im) * r, (re + im) * r) if sign > 0 else ((re + im) * r, (im - re) * r)
    c, s = math.cos(2 * math.pi * k / n), sign * math.sin(2 * math.pi * k / n)
    return (re * c - im * s, re * s + im * c)


def _add(a, b):
    return (a[0] + b[0], a[1] + b[1])


def _sub(a, b):
    return (a[0] - b[0], a[1] - b[1])


def _dft(z, sign):
    n = len(z)
    if n == 1:
        return list(z)
    half = n // 2
    even = _dft([_add(z[i], z[i + half]) for i in range(half)], sign)
    odd = _dft([_turn(_sub(z[i], z[i + half]), i, n, sign) for i in range(half)], sign)
    return [v for pair in zip(even, odd) for v in pair]


def _odd_bins(x):
    half = len(x) // 2
    z = [_turn((x[n], -x[n + half]), n, 4 * half, -1) if n else (x[0], -x[half]) for n in range(half)]
    return _dft(z, -1)


def _place_odd(out, d, n):
    for q, v in enumerate(d):
        k = 4 * q + 1
        if 2 * k <= n:
            out[k] = v
        else:
            out[n - k] = (v[0], -v[1])


def _rdft(x):
    n = len(x)
    if n == 2:
        return [(x[0] + x[1], None), (x[0] - x[1], None)]
    half = n // 2
    out = [None] * (half + 1)
    out[::2] = _rdft([x[i] + x[i + half] for i in range(half)])
    if n == 4:
        out[1] = (x[0] - x[2], x[3] - x[1])
    else:
        _place_odd(out, _odd_bins([x[i] - x[i + half] for i in range(half)]), n)
    return out


def _forward32(x):
    out = [None] * (HALF + 1)
    out[::2] = _rdft(x)
    _place_odd(out, _odd_bins(x), RADIX)
    return out


def _odd_adjoint(u, n):
    count = n // 4
    d = []
    for q in range(count):
        k = 4 * q + 1
        d.append(u[k] if 2 * k <= n else (u[n - k][0], -u[n - k][1]))
    z = _dft(d, 1)
    y = [_turn(z[i], i, n, 1) for i in range(count)]
    return [v[0] for v in y] + [-v[1] for v in y]


def _rdft_adjoint(u):
    n = 2 * (len(u) - 1)
    if n == 2:
        return [u[0][0] + u[1][0], u[0][0] - u[1][0]]
    a = _rdft_adjoint(u[::2])
    if n == 4:
        b = [u[1][0], -u[1][1]]
    else:
        b = _odd_adjoint(u, n)
    return [p + q for p, q in zip(a, b)] + [p - q for p, q in zip(a, b)]


def _inverse32(u):
    a = _rdft_adjoint(u[::2])
    b = _odd_adjoint(u, RADIX)
    return [p + q for p, q in zip(a, b)]


def _dot(a, b, dims=((1,), (0,))):
    return lax.dot_general(a, b, (dims, ((), ())), preferred_element_type=F32)


def _band_mean(power):
    row = lax.broadcasted_iota(jnp.int32, (LANES, LANES), 0) % (NF // RADIX) // (BAND // RADIX)
    col = lax.broadcasted_iota(jnp.int32, (LANES, LANES), 1) % (NF // RADIX) // (BAND // RADIX)
    share = jnp.where(row == col, 1.0 / BAND, 0.0).astype(BF16)
    high = power.astype(BF16)
    low = (power - high.astype(F32)).astype(BF16)
    return _dot(high, share) + _dot(low, share)


def _one_hot(index, rows):
    return (lax.broadcasted_iota(jnp.int32, (rows, index.shape[1]), 0) == index).astype(F32)


def request_kernel(holders, pair_hbm, home_hbm, want_ref, slot_ref, where_ref, pair_ref, home_ref, sems):
    copies = [
        pltpu.make_async_copy(pair_hbm, pair_ref, sems.at[0]),
        pltpu.make_async_copy(home_hbm, home_ref, sems.at[1]),
    ]
    for copy in copies:
        copy.start()
    for copy in copies:
        copy.wait()
    pairs = jnp.concatenate([pair_ref[0:1, :], pair_ref[1:2, :]], axis=1)
    home = home_ref[...]
    high = _one_hot(pairs // LANES, home.shape[0]).astype(BF16)
    low = _one_hot(pairs % LANES, LANES)
    first = ((0,), (0,))
    owner = jnp.sum(_dot((home // LANES).astype(F32).astype(BF16), high, first) * low, axis=0, keepdims=True)
    place = jnp.sum(_dot((home % LANES).astype(F32).astype(BF16), high, first) * low, axis=0, keepdims=True)
    owner = owner.astype(jnp.int32)
    place = place.astype(jnp.int32)
    where_ref[0:1, :] = owner
    where_ref[1:2, :] = place
    owners = _one_hot(owner, holders).astype(BF16)
    places = _one_hot(place, LANES).astype(BF16)
    needed = jnp.minimum(_dot(owners, places, ((1,), (1,))), 1.0)
    row = lax.broadcasted_iota(jnp.int32, (LANES, LANES), 0)
    col = lax.broadcasted_iota(jnp.int32, (LANES, LANES), 1)
    slot = _dot(needed.astype(BF16), (row < col).astype(F32).astype(BF16))
    slot_ref[...] = slot
    marked = jnp.where(needed > 0.0, slot, -1.0)
    slots = lax.broadcasted_iota(jnp.int32, (CAP, LANES), 0).astype(F32)
    for holder in range(holders):
        want_ref[holder] = (marked[holder : holder + 1, :] == slots).astype(F32).astype(BF16)


def position_kernel(slot_ref, where_ref, table_hbm, pick_ref, table_ref, sem):
    copy = pltpu.make_async_copy(table_hbm, table_ref, sem.at[0])
    copy.start()
    owner = where_ref[0:1, :]
    place = where_ref[1:2, :]
    holders = slot_ref.shape[0]
    slot = jnp.minimum(slot_ref[...], CAP - 1.0)
    of_pair = _dot(slot.astype(BF16), _one_hot(owner, holders).astype(BF16), ((0,), (0,)))
    slot = jnp.sum(of_pair * _one_hot(place, LANES), axis=0, keepdims=True)
    position = owner * CAP + slot.astype(jnp.int32)
    pick_ref[...] = _one_hot(position, holders * CAP).T.astype(BF16)
    copy.wait()


ROWS = 16


def transform_kernel(x_ref, table_hbm, yh_ref, yl_ref, table_ref, sem):
    copy = pltpu.make_async_copy(table_hbm, table_ref, sem.at[0])
    copy.start()
    row_count = x_ref.shape[0]
    re, im = slice(0, LANES), slice(LANES, 2 * LANES)

    def put(j, rows, cols, value):
        high = value.astype(BF16)
        yh_ref[j, rows, cols] = high
        yl_ref[j, rows, cols] = (value - high.astype(F32)).astype(BF16)

    @pl.loop(0, row_count // ROWS)
    def _(i):
        rows = pl.ds(pl.multiple_of(i * ROWS, ROWS), ROWS)
        x = [x_ref[rows, n * LANES : (n + 1) * LANES].astype(F32) for n in range(HALF)]
        y = _forward32(x)
        put(0, rows, re, y[0][0])
        put(0, rows, im, y[HALF][0])
        for j in range(1, HALF):
            put(j, rows, re, y[j][0])
            put(j, rows, im, y[j][1])

    copy.wait()


def correlate_kernel(yh_ref, yl_ref, table_ref, inverse_ref, pick_ref, lags_ref, spec_ref, power_ref, u_ref):
    pair_count = pick_ref.shape[0] // 2
    re, im = slice(0, LANES), slice(LANES, 2 * LANES)
    for j in range(HALF):
        high, low = _forward_whole(j, table_ref[2 * j]), _forward_whole(j, table_ref[2 * j + 1])
        spec = _dot(yh_ref[j], high) + _dot(yh_ref[j], low) + _dot(yl_ref[j], high)
        spec_ref[j] = spec
        power = spec[:, re] * spec[:, re] + spec[:, im] * spec[:, im]
        power_ref[...] = power if j == 0 else power_ref[...] + power

    power_ref[...] = 1.0 / jnp.sqrt(_band_mean(power_ref[...]) + 1e-05)

    def ends_of(j):
        scale = power_ref[...]
        white = jnp.concatenate(
            [(spec_ref[j, :, re] * scale).astype(BF16), (spec_ref[j, :, im] * scale).astype(BF16)], axis=1
        )
        return _dot(pick_ref[...], white)

    queue = [ends_of(0), ends_of(1)]
    for j in range(HALF):
        ends = queue.pop(0)
        if j + 2 < HALF:
            queue.append(ends_of(j + 2))
        a, c = ends[:pair_count], ends[pair_count:]
        cross = jnp.concatenate(
            [
                (a[:, re] * c[:, re] + a[:, im] * c[:, im]).astype(BF16),
                (a[:, im] * c[:, re] - a[:, re] * c[:, im]).astype(BF16),
            ],
            axis=1,
        )
        u_ref[j] = _dot(cross, _inverse_whole(j, inverse_ref[j]))

    me = lax.axis_index("seg")
    even = lax.axis_index("tile") % 2 == 0
    blocks = lags_ref.shape[0]
    width = lags_ref.shape[2] // LANES

    @pl.loop(0, pair_count // ROWS)
    def _(i):
        rows = pl.ds(pl.multiple_of(i * ROWS, ROWS), ROWS)
        u = [(u_ref[0, rows, re], None)]
        u += [(u_ref[j, rows, re], u_ref[j, rows, im]) for j in range(1, HALF)]
        u += [(u_ref[0, rows, im], None)]
        lags = _inverse32(u)
        for s in range(blocks):
            place = lax.rem(jnp.where(even, s - me, me - s) + blocks, blocks)
            for h in range(width):
                lags_ref[place, rows, h * LANES : (h + 1) * LANES] = lags[s * width + h].astype(BF16)


def pack_kernel(lags_ref, far_ref, ahead_ref, back_ref, ahead1_ref, back1_ref, keep_ref):
    far_ref[...] = lags_ref[4]
    ahead_ref[...], back_ref[...] = lags_ref[3], lags_ref[5]
    ahead1_ref[...], back1_ref[...] = lags_ref[1], lags_ref[7]
    keep_ref[0], keep_ref[1], keep_ref[2] = lags_ref[0], lags_ref[2], lags_ref[6]


def relay_kernel(keep_ref, far_ref, ahead_ref, back_ref, ahead_out_ref, back_out_ref):
    ahead = keep_ref[1].astype(F32) + far_ref[...].astype(F32) + ahead_ref[...].astype(F32)
    back = keep_ref[2].astype(F32) + back_ref[...].astype(F32)
    ahead_out_ref[...] = ahead.astype(BF16)
    back_out_ref[...] = back.astype(BF16)


def sum_kernel(keep_ref, ahead_ref, back_ref, ahead2_ref, back2_ref, out_ref):
    total = keep_ref[0].astype(F32) + ahead_ref[...].astype(F32) + back_ref[...].astype(F32)
    total = total + ahead2_ref[...].astype(F32) + back2_ref[...].astype(F32)
    out_ref[...] = total.T.astype(BF16)


VMEM = pl.BlockSpec(memory_space=pltpu.VMEM)
ANY = pl.BlockSpec(memory_space=pl.ANY)
MIB = 1024 * 1024


def _call(kernel, name, inputs, outputs, args, scratch=(), limit=4):
    return pl.pallas_call(
        kernel,
        out_shape=outputs,
        in_specs=inputs,
        out_specs=(VMEM,) * len(outputs),
        scratch_shapes=scratch,
        compiler_params=pltpu.CompilerParams(vmem_limit_bytes=limit * MIB),
        name=name,
    )(*args)


def _in_hbm(value):
    return pltpu.with_memory_space_constraint(value, pltpu.HBM)


def shards(samples, pair_list, sensor_home):
    tiles = lax.axis_size("tile")
    segments = lax.axis_size("seg")
    local = samples[0]
    sens_dev, seg_len = local.shape
    pair_dev = pair_list.shape[1]
    rows = tiles * CAP
    lags = NLAG // segments
    shape = jax.ShapeDtypeStruct
    home = sensor_home.reshape(-1, LANES)
    want, slot, where = _call(
        functools.partial(request_kernel, tiles),
        "request",
        [ANY] * 2,
        (
            shape((tiles, CAP, sens_dev), BF16),
            shape((tiles, sens_dev), F32),
            shape((2, 2 * pair_dev), jnp.int32),
        ),
        (_in_hbm(pair_list), _in_hbm(home)),
        [
            pltpu.VMEM(pair_list.shape, jnp.int32),
            pltpu.VMEM(home.shape, jnp.int32),
            pltpu.SemaphoreType.DMA((2,)),
        ],
    )
    asked = lax.all_to_all(want, "tile", split_axis=0, concat_axis=0, tiled=True)
    forward, inverse = _upper_halves(_forward_tables(), _inverse_tables(segments))
    forward = np.stack(_split(forward), axis=1).reshape(2 * HALF, LANES, 2 * LANES)
    inverse = jnp.asarray(inverse.astype(BF16))
    pick, inverse = _call(
        position_kernel,
        "position",
        [VMEM] * 2 + [ANY],
        (pltpu.VMEM((2 * pair_dev, rows), BF16), pltpu.VMEM(inverse.shape, BF16)),
        (slot, where, _in_hbm(inverse)),
        [pltpu.SemaphoreType.DMA((1,))],
    )
    asked, pick = lax.optimization_barrier((asked, pick))
    outgoing = jnp.dot(asked.reshape(rows, sens_dev), local, preferred_element_type=F32).astype(BF16)
    arrived = lax.all_to_all(
        outgoing.reshape(tiles, CAP, seg_len), "tile", split_axis=0, concat_axis=0, tiled=True
    )
    lag_block = (pair_dev, lags)
    spectra = pltpu.VMEM((HALF, rows, 2 * LANES), BF16)
    yh, yl, forward = _call(
        transform_kernel,
        "transform",
        [VMEM, ANY],
        (spectra, spectra, pltpu.VMEM(forward.shape, BF16)),
        (arrived.reshape(rows, seg_len), _in_hbm(jnp.asarray(forward))),
        [pltpu.SemaphoreType.DMA((1,))],
        limit=16,
    )
    (blocks,) = _call(
        correlate_kernel,
        "correlate",
        [VMEM] * 5,
        (pltpu.VMEM((segments,) + lag_block, BF16),),
        (yh, yl, forward, inverse, pick),
        [
            pltpu.VMEM((HALF, rows, 2 * LANES), F32),
            pltpu.VMEM((rows, LANES), F32),
            pltpu.VMEM((HALF, pair_dev, 2 * LANES), F32),
        ],
        limit=24,
    )
    far, ahead, back, ahead1, back1, keep = _call(
        pack_kernel,
        "pack",
        [VMEM],
        tuple(pltpu.VMEM(n + lag_block, BF16) for n in ((), (), (), (), (), (3,))),
        (blocks,),
    )

    def shift(value, steps):
        ring = [
            (s * tiles + t, (s + (-steps if t % 2 else steps)) % segments * tiles + t)
            for s in range(segments)
            for t in range(tiles)
        ]
        return lax.ppermute(value, ("seg", "tile"), ring)

    far, ahead, back = shift(far, 2), shift(ahead, 1), shift(back, -1)
    ahead1, back1 = shift(ahead1, 1), shift(back1, -1)
    ahead2, back2 = _call(
        relay_kernel,
        "relay",
        [VMEM] * 4,
        (pltpu.VMEM(lag_block, BF16),) * 2,
        (keep, far, ahead, back),
    )
    ahead2, back2 = shift(ahead2, 2), shift(back2, -2)
    (out,) = _call(
        sum_kernel,
        "stack",
        [VMEM] * 5,
        (shape((lags, pair_dev), BF16),),
        (keep, ahead1, back1, ahead2, back2),
    )
    return out


def solution(mesh):
    return jax.shard_map(
        shards,
        mesh=mesh,
        in_specs=(P("seg", "tile", None), P(None, "tile"), P()),
        out_specs=P("seg", "tile"),
        check_vma=False,
    )
```

```python
import functools
import math

import jax
import jax.numpy as jnp
import numpy as np
from jax import lax
from jax.experimental import pallas as pl
from jax.experimental.pallas import tpu as pltpu
from jax.sharding import PartitionSpec as P

NFFT = 4096
NF = 2048
BAND = 64
NLAG = 2048
CAP = 8
RADIX = 32
LANES = 128
HALF = RADIX // 2
F32 = jnp.float32
BF16 = jnp.bfloat16


def _bins():
    k2 = np.arange(NF // RADIX)
    low = [np.arange(HALF), np.concatenate([[HALF], RADIX - np.arange(1, HALF)])]
    return np.concatenate([c[:, None] + RADIX * k2[None, :] for c in low], axis=1)


def _forward_tables():
    bins = _bins()
    n2 = np.arange(LANES)
    half = NF // RADIX
    tables = np.zeros((HALF, 2 * LANES, 2 * LANES))
    for j in range(HALF):
        angle = -2.0 * np.pi * ((n2[:, None] * bins[j][None, :]) % NFFT) / NFFT
        c, s = np.cos(angle), np.sin(angle)
        a, b = slice(0, half), slice(half, LANES)
        top, low = tables[j, :LANES], tables[j, LANES:]
        re, im = slice(0, LANES), slice(LANES, 2 * LANES)
        if j == 0:
            top[:, re][:, a], top[:, im][:, a] = c[:, a], s[:, a]
            low[:, re][:, b], low[:, im][:, b] = c[:, b], s[:, b]
        else:
            sign = np.where(np.arange(LANES) < half, 1.0, -1.0)[None, :]
            top[:, re], top[:, im] = c, s
            low[:, re], low[:, im] = -sign * s, sign * c
    return tables


def _inverse_tables(segments):
    bins = _bins()
    t2 = np.arange(LANES)
    half = NF // RADIX
    tables = np.zeros((HALF, 2 * LANES, 2 * LANES))
    for j in range(HALF):
        weight = np.where(bins[j] == 0, 1.0, 2.0) / math.sqrt(NFFT * segments)
        angle = 2.0 * np.pi * ((bins[j][:, None] * t2[None, :]) % NFFT) / NFFT
        wave = weight[:, None] * np.exp(1j * angle)
        if j == 0:
            for part, cols in ((slice(0, half), slice(0, LANES)), (slice(half, LANES), slice(LANES, 2 * LANES))):
                tables[0, :LANES, cols][part] = wave.real[part]
                tables[0, LANES:, cols][part] = -wave.imag[part]
        else:
            turn = (-1j) ** j
            first = (np.arange(LANES) < half)[:, None]
            of_re = turn * np.where(first, wave, np.conj(wave))
            of_im = turn * np.where(first, 1j * wave, np.conj(1j * wave))
            tables[j, :LANES, :LANES], tables[j, :LANES, LANES:] = of_re.real, of_re.imag
            tables[j, LANES:, :LANES], tables[j, LANES:, LANES:] = of_im.real, of_im.imag
    return tables


def _upper_halves(tables, inverse):
    upper = tables[:, :LANES].copy()
    upper[0] += tables[0, LANES:]
    inverse_upper = inverse[:, :LANES].copy()
    folded = inverse[0, :, :LANES] + inverse[0, :, LANES:]
    inverse_upper[0] = np.concatenate([folded[:LANES], folded[LANES:]], axis=1)
    return upper, inverse_upper


def _forward_whole(j, upper):
    c, s = upper[:, :LANES], upper[:, LANES:]
    first = lax.broadcasted_iota(jnp.int32, c.shape, 1) < NF // RADIX
    none = jnp.zeros_like(c)
    if j == 0:
        above = [jnp.where(first, c, none), jnp.where(first, s, none)]
        below = [jnp.where(first, none, c), jnp.where(first, none, s)]
    else:
        above = [c, s]
        below = [jnp.where(first, -s, s), jnp.where(first, c, -c)]
    return jnp.concatenate([jnp.concatenate(above, axis=1), jnp.concatenate(below, axis=1)], axis=0)


def _inverse_whole(j, upper):
    half = NF // RADIX
    a, b = upper[:, :LANES], upper[:, LANES:]
    none = jnp.zeros_like(a[:half])
    if j == 0:
        parts = [(a[:half], none), (none, a[half:]), (b[:half], none), (none, b[half:])]
    else:
        parts = [(a[:half], b[:half]), (a[half:], b[half:]), (-b[:half], a[:half]), (b[half:], -a[half:])]
    return jnp.concatenate([jnp.concatenate(p, axis=1) for p in parts], axis=0)


def _split(table):
    high = table.astype(BF16)
    low = (table - high.astype(np.float64)).astype(BF16)
    return high, low


def _turn(z, k, n, sign):
    re, im = z
    k = k % n
    if k == 0:
        return z
    if 4 * k == n:
        return (-im, re) if sign > 0 else (im, -re)
    if 2 * k == n:
        return (-re, -im)
    if 8 * k == n:
        r = math.sqrt(0.5)
        return ((re - im) * r, (re + im) * r) if sign > 0 else ((re + im) * r, (im - re) * r)
    c, s = math.cos(2 * math.pi * k / n), sign * math.sin(2 * math.pi * k / n)
    return (re * c - im * s, re * s + im * c)


def _add(a, b):
    return (a[0] + b[0], a[1] + b[1])


def _sub(a, b):
    return (a[0] - b[0], a[1] - b[1])


def _dft(z, sign):
    n = len(z)
    if n == 1:
        return list(z)
    half = n // 2
    even = _dft([_add(z[i], z[i + half]) for i in range(half)], sign)
    odd = _dft([_turn(_sub(z[i], z[i + half]), i, n, sign) for i in range(half)], sign)
    return [v for pair in zip(even, odd) for v in pair]


def _odd_bins(x):
    half = len(x) // 2
    z = [_turn((x[n], -x[n + half]), n, 4 * half, -1) if n else (x[0], -x[half]) for n in range(half)]
    return _dft(z, -1)


def _place_odd(out, d, n):
    for q, v in enumerate(d):
        k = 4 * q + 1
        if 2 * k <= n:
            out[k] = v
        else:
            out[n - k] = (v[0], -v[1])


def _rdft(x):
    n = len(x)
    if n == 2:
        return [(x[0] + x[1], None), (x[0] - x[1], None)]
    half = n // 2
    out = [None] * (half + 1)
    out[::2] = _rdft([x[i] + x[i + half] for i in range(half)])
    if n == 4:
        out[1] = (x[0] - x[2], x[3] - x[1])
    else:
        _place_odd(out, _odd_bins([x[i] - x[i + half] for i in range(half)]), n)
    return out


def _forward32(x):
    out = [None] * (HALF + 1)
    out[::2] = _rdft(x)
    _place_odd(out, _odd_bins(x), RADIX)
    return out


def _odd_adjoint(u, n):
    count = n // 4
    d = []
    for q in range(count):
        k = 4 * q + 1
        d.append(u[k] if 2 * k <= n else (u[n - k][0], -u[n - k][1]))
    z = _dft(d, 1)
    y = [_turn(z[i], i, n, 1) for i in range(count)]
    return [v[0] for v in y] + [-v[1] for v in y]


def _rdft_adjoint(u):
    n = 2 * (len(u) - 1)
    if n == 2:
        return [u[0][0] + u[1][0], u[0][0] - u[1][0]]
    a = _rdft_adjoint(u[::2])
    if n == 4:
        b = [u[1][0], -u[1][1]]
    else:
        b = _odd_adjoint(u, n)
    return [p + q for p, q in zip(a, b)] + [p - q for p, q in zip(a, b)]


def _inverse32(u):
    a = _rdft_adjoint(u[::2])
    b = _odd_adjoint(u, RADIX)
    return [p + q for p, q in zip(a, b)]


def _dot(a, b, dims=((1,), (0,))):
    return lax.dot_general(a, b, (dims, ((), ())), preferred_element_type=F32)


def _band_mean(power):
    row = lax.broadcasted_iota(jnp.int32, (LANES, LANES), 0) % (NF // RADIX) // (BAND // RADIX)
    col = lax.broadcasted_iota(jnp.int32, (LANES, LANES), 1) % (NF // RADIX) // (BAND // RADIX)
    share = jnp.where(row == col, 1.0 / BAND, 0.0).astype(BF16)
    high = power.astype(BF16)
    low = (power - high.astype(F32)).astype(BF16)
    return _dot(high, share) + _dot(low, share)


def _one_hot(index, rows):
    return (lax.broadcasted_iota(jnp.int32, (rows, index.shape[1]), 0) == index).astype(F32)


def request_kernel(holders, pair_hbm, home_hbm, want_ref, slot_ref, where_ref, pair_ref, home_ref, sems):
    copies = [
        pltpu.make_async_copy(pair_hbm, pair_ref, sems.at[0]),
        pltpu.make_async_copy(home_hbm, home_ref, sems.at[1]),
    ]
    for copy in copies:
        copy.start()
    for copy in copies:
        copy.wait()
    pairs = jnp.concatenate([pair_ref[0:1, :], pair_ref[1:2, :]], axis=1)
    home = home_ref[...]
    high = _one_hot(pairs // LANES, home.shape[0])
    low = _one_hot(pairs % LANES, LANES).astype(BF16)
    stored = jnp.concatenate([home // LANES, home % LANES], axis=0).astype(F32).astype(BF16)
    columns = _dot(stored, low)
    owner = jnp.sum(columns[: home.shape[0]] * high, axis=0, keepdims=True).astype(jnp.int32)
    place = jnp.sum(columns[home.shape[0] :] * high, axis=0, keepdims=True).astype(jnp.int32)
    where_ref[0:1, :] = owner
    where_ref[1:2, :] = place
    owners = _one_hot(owner, holders).astype(BF16)
    places = _one_hot(place, LANES).astype(BF16)
    needed = jnp.minimum(_dot(owners, places, ((1,), (1,))), 1.0)
    row = lax.broadcasted_iota(jnp.int32, (LANES, LANES), 0)
    col = lax.broadcasted_iota(jnp.int32, (LANES, LANES), 1)
    slot = _dot(needed.astype(BF16), (row < col).astype(F32).astype(BF16))
    slot_ref[...] = slot
    marked = jnp.where(needed > 0.0, slot, -1.0)
    slots = lax.broadcasted_iota(jnp.int32, (CAP, LANES), 0).astype(F32)
    for holder in range(holders):
        want_ref[holder] = (marked[holder : holder + 1, :] == slots).astype(F32).astype(BF16)


def position_kernel(slot_ref, where_ref, table_hbm, pick_ref, table_ref, sem):
    copy = pltpu.make_async_copy(table_hbm, table_ref, sem.at[0])
    copy.start()
    owner = where_ref[0:1, :]
    place = where_ref[1:2, :]
    holders = slot_ref.shape[0]
    slot = jnp.minimum(slot_ref[...], CAP - 1.0)
    of_pair = _dot(slot.astype(BF16), _one_hot(owner, holders).astype(BF16), ((0,), (0,)))
    slot = jnp.sum(of_pair * _one_hot(place, LANES), axis=0, keepdims=True)
    position = owner * CAP + slot.astype(jnp.int32)
    pick_ref[...] = _one_hot(position, holders * CAP).T.astype(BF16)
    copy.wait()


ROWS = 16


def transform_kernel(x_ref, table_hbm, yh_ref, yl_ref, table_ref, sem):
    copy = pltpu.make_async_copy(table_hbm, table_ref, sem.at[0])
    copy.start()
    row_count = x_ref.shape[0]
    re, im = slice(0, LANES), slice(LANES, 2 * LANES)

    def put(j, rows, cols, value):
        high = value.astype(BF16)
        yh_ref[j, rows, cols] = high
        yl_ref[j, rows, cols] = (value - high.astype(F32)).astype(BF16)

    @pl.loop(0, row_count // ROWS)
    def _(i):
        rows = pl.ds(pl.multiple_of(i * ROWS, ROWS), ROWS)
        x = [x_ref[rows, n * LANES : (n + 1) * LANES].astype(F32) for n in range(HALF)]
        y = _forward32(x)
        put(0, rows, re, y[0][0])
        put(0, rows, im, y[HALF][0])
        for j in range(1, HALF):
            put(j, rows, re, y[j][0])
            put(j, rows, im, y[j][1])

    copy.wait()


def correlate_kernel(yh_ref, yl_ref, table_ref, inverse_ref, pick_ref, lags_ref, spec_ref, power_ref, u_ref, cross_ref):
    pair_count = pick_ref.shape[0] // 2
    re, im = slice(0, LANES), slice(LANES, 2 * LANES)
    for j in range(HALF):
        high, low = _forward_whole(j, table_ref[2 * j]), _forward_whole(j, table_ref[2 * j + 1])
        spec = _dot(yh_ref[j], high) + _dot(yh_ref[j], low) + _dot(yl_ref[j], high)
        spec_ref[j] = spec
        power = spec[:, re] * spec[:, re] + spec[:, im] * spec[:, im]
        power_ref[...] = power if j == 0 else power_ref[...] + power

    power_ref[...] = 1.0 / jnp.sqrt(_band_mean(power_ref[...]) + 1e-05)

    def ends_of(j):
        scale = power_ref[...]
        white = jnp.concatenate(
            [(spec_ref[j, :, re] * scale).astype(BF16), (spec_ref[j, :, im] * scale).astype(BF16)], axis=1
        )
        return _dot(pick_ref[...], white)

    half = pair_count // 2
    queue = [ends_of(0), ends_of(1)]
    for j in range(HALF):
        ends = queue.pop(0)
        if j + 2 < HALF:
            queue.append(ends_of(j + 2))
        a, c = ends[:pair_count], ends[pair_count:]
        cross = jnp.concatenate(
            [
                (a[:, re] * c[:, re] + a[:, im] * c[:, im]).astype(BF16),
                (a[:, im] * c[:, re] - a[:, re] * c[:, im]).astype(BF16),
            ],
            axis=1,
        )
        u_ref[j, :half] = _dot(cross[:half], _inverse_whole(j, inverse_ref[j]))
        cross_ref[j] = cross[half:]

    me = lax.axis_index("seg")
    even = lax.axis_index("tile") % 2 == 0
    blocks = lags_ref.shape[0]
    width = lags_ref.shape[2] // LANES

    def lags_of(rows):
        u = [(u_ref[0, rows, re], None)]
        u += [(u_ref[j, rows, re], u_ref[j, rows, im]) for j in range(1, HALF)]
        u += [(u_ref[0, rows, im], None)]
        lags = _inverse32(u)
        for s in range(blocks):
            place = lax.rem(jnp.where(even, s - me, me - s) + blocks, blocks)
            for h in range(width):
                lags_ref[place, rows, h * LANES : (h + 1) * LANES] = lags[s * width + h].astype(BF16)

    steps = half // ROWS
    for j in range(HALF):
        u_ref[j, half:] = _dot(cross_ref[j], _inverse_whole(j, inverse_ref[j]))
        for i in range(j * steps // HALF, (j + 1) * steps // HALF):
            lags_of(slice(i * ROWS, (i + 1) * ROWS))

    @pl.loop(steps, pair_count // ROWS)
    def _(i):
        lags_of(pl.ds(pl.multiple_of(i * ROWS, ROWS), ROWS))


def pack_kernel(lags_ref, far_ref, ahead_ref, back_ref, ahead1_ref, back1_ref, keep_ref):
    far_ref[...] = lags_ref[4]
    ahead_ref[...], back_ref[...] = lags_ref[3], lags_ref[5]
    ahead1_ref[...], back1_ref[...] = lags_ref[1], lags_ref[7]
    keep_ref[0], keep_ref[1], keep_ref[2] = lags_ref[0], lags_ref[2], lags_ref[6]


def relay_kernel(keep_ref, far_ref, ahead_ref, back_ref, ahead_out_ref, back_out_ref):
    ahead = keep_ref[1].astype(F32) + far_ref[...].astype(F32) + ahead_ref[...].astype(F32)
    back = keep_ref[2].astype(F32) + back_ref[...].astype(F32)
    ahead_out_ref[...] = ahead.astype(BF16)
    back_out_ref[...] = back.astype(BF16)


def sum_kernel(keep_ref, ahead_ref, back_ref, ahead2_ref, back2_ref, out_hbm, out_ref, sems):
    half = out_ref.shape[0] // 2
    copies = []
    for i in range(2):
        part = slice(i * half, (i + 1) * half)
        total = keep_ref[0, :, part].astype(F32) + ahead_ref[:, part].astype(F32) + back_ref[:, part].astype(F32)
        total = total + ahead2_ref[:, part].astype(F32) + back2_ref[:, part].astype(F32)
        out_ref[part] = total.T.astype(BF16)
        copies.append(pltpu.make_async_copy(out_ref.at[part], out_hbm.at[part], sems.at[i]))
        copies[i].start()
    for copy in copies:
        copy.wait()


VMEM = pl.BlockSpec(memory_space=pltpu.VMEM)
ANY = pl.BlockSpec(memory_space=pl.ANY)
MIB = 1024 * 1024


def _call(kernel, name, inputs, outputs, args, scratch=(), limit=4, place=VMEM):
    return pl.pallas_call(
        kernel,
        out_shape=outputs,
        in_specs=inputs,
        out_specs=(place,) * len(outputs),
        scratch_shapes=scratch,
        compiler_params=pltpu.CompilerParams(vmem_limit_bytes=limit * MIB),
        name=name,
    )(*args)


def _in_hbm(value):
    return pltpu.with_memory_space_constraint(value, pltpu.HBM)


def shards(samples, pair_list, sensor_home):
    tiles = lax.axis_size("tile")
    segments = lax.axis_size("seg")
    local = samples[0]
    sens_dev, seg_len = local.shape
    pair_dev = pair_list.shape[1]
    rows = tiles * CAP
    lags = NLAG // segments
    shape = jax.ShapeDtypeStruct
    home = sensor_home.reshape(-1, LANES)
    want, slot, where = _call(
        functools.partial(request_kernel, tiles),
        "request",
        [ANY] * 2,
        (
            pltpu.VMEM((tiles, CAP, sens_dev), BF16),
            pltpu.VMEM((tiles, sens_dev), F32),
            pltpu.VMEM((2, 2 * pair_dev), jnp.int32),
        ),
        (_in_hbm(pair_list), _in_hbm(home)),
        [
            pltpu.VMEM(pair_list.shape, jnp.int32),
            pltpu.VMEM(home.shape, jnp.int32),
            pltpu.SemaphoreType.DMA((2,)),
        ],
    )
    asked = lax.all_to_all(want, "tile", split_axis=0, concat_axis=0, tiled=True)
    forward, inverse = _upper_halves(_forward_tables(), _inverse_tables(segments))
    forward = np.stack(_split(forward), axis=1).reshape(2 * HALF, LANES, 2 * LANES)
    inverse = jnp.asarray(inverse.astype(BF16))
    pick, inverse = _call(
        position_kernel,
        "position",
        [VMEM] * 2 + [ANY],
        (pltpu.VMEM((2 * pair_dev, rows), BF16), pltpu.VMEM(inverse.shape, BF16)),
        (slot, where, _in_hbm(inverse)),
        [pltpu.SemaphoreType.DMA((1,))],
    )
    asked, pick = lax.optimization_barrier((asked, pick))
    outgoing = jnp.dot(asked.reshape(rows, sens_dev), local, preferred_element_type=F32).astype(BF16)
    arrived = lax.all_to_all(
        outgoing.reshape(tiles, CAP, seg_len), "tile", split_axis=0, concat_axis=0, tiled=True
    )
    lag_block = (pair_dev, lags)
    spectra = pltpu.VMEM((HALF, rows, 2 * LANES), BF16)
    yh, yl, forward = _call(
        transform_kernel,
        "transform",
        [VMEM, ANY],
        (spectra, spectra, pltpu.VMEM(forward.shape, BF16)),
        (arrived.reshape(rows, seg_len), _in_hbm(jnp.asarray(forward))),
        [pltpu.SemaphoreType.DMA((1,))],
        limit=16,
    )
    (blocks,) = _call(
        correlate_kernel,
        "correlate",
        [VMEM] * 5,
        (pltpu.VMEM((segments,) + lag_block, BF16),),
        (yh, yl, forward, inverse, pick),
        [
            pltpu.VMEM((HALF, rows, 2 * LANES), F32),
            pltpu.VMEM((rows, LANES), F32),
            pltpu.VMEM((HALF, pair_dev, 2 * LANES), F32),
            pltpu.VMEM((HALF, pair_dev // 2, 2 * LANES), BF16),
        ],
        limit=24,
    )
    far, ahead, back, ahead1, back1, keep = _call(
        pack_kernel,
        "pack",
        [VMEM],
        tuple(pltpu.VMEM(n + lag_block, BF16) for n in ((), (), (), (), (), (3,))),
        (blocks,),
    )

    def shift(value, steps):
        ring = [
            (s * tiles + t, (s + (-steps if t % 2 else steps)) % segments * tiles + t)
            for s in range(segments)
            for t in range(tiles)
        ]
        return lax.ppermute(value, ("seg", "tile"), ring)

    far, ahead, back = shift(far, 2), shift(ahead, 1), shift(back, -1)
    ahead1, back1 = shift(ahead1, 1), shift(back1, -1)
    ahead2, back2 = _call(
        relay_kernel,
        "relay",
        [VMEM] * 4,
        (pltpu.VMEM(lag_block, BF16),) * 2,
        (keep, far, ahead, back),
    )
    ahead2, back2 = shift(ahead2, 2), shift(back2, -2)
    (out,) = _call(
        sum_kernel,
        "stack",
        [VMEM] * 5,
        (shape((lags, pair_dev), BF16),),
        (keep, ahead1, back1, ahead2, back2),
        [pltpu.VMEM((lags, pair_dev), BF16), pltpu.SemaphoreType.DMA((2,))],
        place=ANY,
    )
    return out


def solution(mesh):
    return jax.shard_map(
        shards,
        mesh=mesh,
        in_specs=(P("seg", "tile", None), P(None, "tile"), P()),
        out_specs=P("seg", "tile"),
        check_vma=False,
    )
```

```python
import functools
import math

import jax
import jax.numpy as jnp
import numpy as np
from jax import lax
from jax.experimental import pallas as pl
from jax.experimental.pallas import tpu as pltpu
from jax.sharding import PartitionSpec as P

NFFT = 4096
NF = 2048
BAND = 64
NLAG = 2048
CAP = 8
RADIX = 32
LANES = 128
HALF = RADIX // 2
F32 = jnp.float32
BF16 = jnp.bfloat16


def _bins():
    k2 = np.arange(NF // RADIX)
    low = [np.arange(HALF), np.concatenate([[HALF], RADIX - np.arange(1, HALF)])]
    return np.concatenate([c[:, None] + RADIX * k2[None, :] for c in low], axis=1)


def _forward_tables():
    bins = _bins()
    n2 = np.arange(LANES)
    half = NF // RADIX
    tables = np.zeros((HALF, 2 * LANES, 2 * LANES))
    for j in range(HALF):
        angle = -2.0 * np.pi * ((n2[:, None] * bins[j][None, :]) % NFFT) / NFFT
        c, s = np.cos(angle), np.sin(angle)
        a, b = slice(0, half), slice(half, LANES)
        top, low = tables[j, :LANES], tables[j, LANES:]
        re, im = slice(0, LANES), slice(LANES, 2 * LANES)
        if j == 0:
            top[:, re][:, a], top[:, im][:, a] = c[:, a], s[:, a]
            low[:, re][:, b], low[:, im][:, b] = c[:, b], s[:, b]
        else:
            sign = np.where(np.arange(LANES) < half, 1.0, -1.0)[None, :]
            top[:, re], top[:, im] = c, s
            low[:, re], low[:, im] = -sign * s, sign * c
    return tables


def _inverse_tables(segments):
    bins = _bins()
    t2 = np.arange(LANES)
    half = NF // RADIX
    tables = np.zeros((HALF, 2 * LANES, 2 * LANES))
    for j in range(HALF):
        weight = np.where(bins[j] == 0, 1.0, 2.0) / math.sqrt(NFFT * segments)
        angle = 2.0 * np.pi * ((bins[j][:, None] * t2[None, :]) % NFFT) / NFFT
        wave = weight[:, None] * np.exp(1j * angle)
        if j == 0:
            for part, cols in ((slice(0, half), slice(0, LANES)), (slice(half, LANES), slice(LANES, 2 * LANES))):
                tables[0, :LANES, cols][part] = wave.real[part]
                tables[0, LANES:, cols][part] = -wave.imag[part]
        else:
            turn = (-1j) ** j
            first = (np.arange(LANES) < half)[:, None]
            of_re = turn * np.where(first, wave, np.conj(wave))
            of_im = turn * np.where(first, 1j * wave, np.conj(1j * wave))
            tables[j, :LANES, :LANES], tables[j, :LANES, LANES:] = of_re.real, of_re.imag
            tables[j, LANES:, :LANES], tables[j, LANES:, LANES:] = of_im.real, of_im.imag
    return tables


def _upper_halves(tables, inverse):
    upper = tables[:, :LANES].copy()
    upper[0] += tables[0, LANES:]
    inverse_upper = inverse[:, :LANES].copy()
    folded = inverse[0, :, :LANES] + inverse[0, :, LANES:]
    inverse_upper[0] = np.concatenate([folded[:LANES], folded[LANES:]], axis=1)
    return upper, inverse_upper


def _forward_whole(j, upper):
    c, s = upper[:, :LANES], upper[:, LANES:]
    first = lax.broadcasted_iota(jnp.int32, c.shape, 1) < NF // RADIX
    none = jnp.zeros_like(c)
    if j == 0:
        above = [jnp.where(first, c, none), jnp.where(first, s, none)]
        below = [jnp.where(first, none, c), jnp.where(first, none, s)]
    else:
        above = [c, s]
        below = [jnp.where(first, -s, s), jnp.where(first, c, -c)]
    return jnp.concatenate([jnp.concatenate(above, axis=1), jnp.concatenate(below, axis=1)], axis=0)


def _inverse_whole(j, upper):
    half = NF // RADIX
    a, b = upper[:, :LANES], upper[:, LANES:]
    none = jnp.zeros_like(a[:half])
    if j == 0:
        parts = [(a[:half], none), (none, a[half:]), (b[:half], none), (none, b[half:])]
    else:
        parts = [(a[:half], b[:half]), (a[half:], b[half:]), (-b[:half], a[:half]), (b[half:], -a[half:])]
    return jnp.concatenate([jnp.concatenate(p, axis=1) for p in parts], axis=0)


def _split(table):
    high = table.astype(BF16)
    low = (table - high.astype(np.float64)).astype(BF16)
    return high, low


def _turn(z, k, n, sign):
    re, im = z
    k = k % n
    if k == 0:
        return z
    if 4 * k == n:
        return (-im, re) if sign > 0 else (im, -re)
    if 2 * k == n:
        return (-re, -im)
    if 8 * k == n:
        r = math.sqrt(0.5)
        return ((re - im) * r, (re + im) * r) if sign > 0 else ((re + im) * r, (im - re) * r)
    c, s = math.cos(2 * math.pi * k / n), sign * math.sin(2 * math.pi * k / n)
    return (re * c - im * s, re * s + im * c)


def _add(a, b):
    return (a[0] + b[0], a[1] + b[1])


def _sub(a, b):
    return (a[0] - b[0], a[1] - b[1])


def _dft(z, sign):
    n = len(z)
    if n == 1:
        return list(z)
    half = n // 2
    even = _dft([_add(z[i], z[i + half]) for i in range(half)], sign)
    odd = _dft([_turn(_sub(z[i], z[i + half]), i, n, sign) for i in range(half)], sign)
    return [v for pair in zip(even, odd) for v in pair]


def _odd_bins(x):
    half = len(x) // 2
    z = [_turn((x[n], -x[n + half]), n, 4 * half, -1) if n else (x[0], -x[half]) for n in range(half)]
    return _dft(z, -1)


def _place_odd(out, d, n):
    for q, v in enumerate(d):
        k = 4 * q + 1
        if 2 * k <= n:
            out[k] = v
        else:
            out[n - k] = (v[0], -v[1])


def _rdft(x):
    n = len(x)
    if n == 2:
        return [(x[0] + x[1], None), (x[0] - x[1], None)]
    half = n // 2
    out = [None] * (half + 1)
    out[::2] = _rdft([x[i] + x[i + half] for i in range(half)])
    if n == 4:
        out[1] = (x[0] - x[2], x[3] - x[1])
    else:
        _place_odd(out, _odd_bins([x[i] - x[i + half] for i in range(half)]), n)
    return out


def _forward32(x):
    out = [None] * (HALF + 1)
    out[::2] = _rdft(x)
    _place_odd(out, _odd_bins(x), RADIX)
    return out


def _odd_adjoint(u, n):
    count = n // 4
    d = []
    for q in range(count):
        k = 4 * q + 1
        d.append(u[k] if 2 * k <= n else (u[n - k][0], -u[n - k][1]))
    z = _dft(d, 1)
    y = [_turn(z[i], i, n, 1) for i in range(count)]
    return [v[0] for v in y] + [-v[1] for v in y]


def _rdft_adjoint(u):
    n = 2 * (len(u) - 1)
    if n == 2:
        return [u[0][0] + u[1][0], u[0][0] - u[1][0]]
    a = _rdft_adjoint(u[::2])
    if n == 4:
        b = [u[1][0], -u[1][1]]
    else:
        b = _odd_adjoint(u, n)
    return [p + q for p, q in zip(a, b)] + [p - q for p, q in zip(a, b)]


def _inverse32(u):
    a = _rdft_adjoint(u[::2])
    b = _odd_adjoint(u, RADIX)
    return [p + q for p, q in zip(a, b)]


def _dot(a, b, dims=((1,), (0,))):
    return lax.dot_general(a, b, (dims, ((), ())), preferred_element_type=F32)


def _band_mean(power):
    row = lax.broadcasted_iota(jnp.int32, (LANES, LANES), 0) % (NF // RADIX) // (BAND // RADIX)
    col = lax.broadcasted_iota(jnp.int32, (LANES, LANES), 1) % (NF // RADIX) // (BAND // RADIX)
    share = jnp.where(row == col, 1.0 / BAND, 0.0).astype(BF16)
    high = power.astype(BF16)
    low = (power - high.astype(F32)).astype(BF16)
    return _dot(high, share) + _dot(low, share)


def _one_hot(index, rows):
    return (lax.broadcasted_iota(jnp.int32, (rows, index.shape[1]), 0) == index).astype(F32)


def request_kernel(
    holders, pair_hbm, home_hbm, table_hbm, want_ref, pick_ref, table_ref, pair_ref, home_ref, sems
):
    copies = [
        pltpu.make_async_copy(src, dst, sems.at[i])
        for i, (src, dst) in enumerate(
            ((pair_hbm, pair_ref), (home_hbm, home_ref), (table_hbm, table_ref))
        )
    ]
    for copy in copies:
        copy.start()
    for copy in copies[:2]:
        copy.wait()
    pairs = jnp.concatenate([pair_ref[0:1, :], pair_ref[1:2, :]], axis=1)
    home = home_ref[...]
    high = _one_hot(pairs // LANES, home.shape[0])
    low = _one_hot(pairs % LANES, LANES).astype(BF16)
    stored = jnp.concatenate([home // LANES, home % LANES], axis=0).astype(F32).astype(BF16)
    columns = _dot(stored, low)
    owner = jnp.sum(columns[: home.shape[0]] * high, axis=0, keepdims=True).astype(jnp.int32)
    place = jnp.sum(columns[home.shape[0] :] * high, axis=0, keepdims=True).astype(jnp.int32)
    owners = _one_hot(owner, holders).astype(BF16)
    places = _one_hot(place, LANES).astype(BF16)
    needed = jnp.minimum(_dot(owners, places, ((1,), (1,))), 1.0)
    row = lax.broadcasted_iota(jnp.int32, (LANES, LANES), 0)
    col = lax.broadcasted_iota(jnp.int32, (LANES, LANES), 1)
    slot = _dot(needed.astype(BF16), (row < col).astype(F32).astype(BF16))
    marked = jnp.where(needed > 0.0, slot, -1.0)
    slots = lax.broadcasted_iota(jnp.int32, (CAP, LANES), 0).astype(F32)
    for holder in range(holders):
        want_ref[holder] = (marked[holder : holder + 1, :] == slots).astype(F32).astype(BF16)
    slot = jnp.minimum(slot, CAP - 1.0)
    of_pair = _dot(slot.astype(BF16), owners, ((0,), (0,)))
    slot = jnp.sum(of_pair * _one_hot(place, LANES), axis=0, keepdims=True)
    position = owner * CAP + slot.astype(jnp.int32)
    pick_ref[...] = _one_hot(position, holders * CAP).T.astype(BF16)
    copies[2].wait()


ROWS = 16


def transform_kernel(x_ref, table_hbm, yh_ref, yl_ref, table_ref, sem):
    copy = pltpu.make_async_copy(table_hbm, table_ref, sem.at[0])
    copy.start()
    row_count = x_ref.shape[0]
    re, im = slice(0, LANES), slice(LANES, 2 * LANES)

    def put(j, rows, cols, value):
        high = value.astype(BF16)
        yh_ref[j, rows, cols] = high
        yl_ref[j, rows, cols] = (value - high.astype(F32)).astype(BF16)

    @pl.loop(0, row_count // ROWS)
    def _(i):
        rows = pl.ds(pl.multiple_of(i * ROWS, ROWS), ROWS)
        x = [x_ref[rows, n * LANES : (n + 1) * LANES].astype(F32) for n in range(HALF)]
        y = _forward32(x)
        put(0, rows, re, y[0][0])
        put(0, rows, im, y[HALF][0])
        for j in range(1, HALF):
            put(j, rows, re, y[j][0])
            put(j, rows, im, y[j][1])

    copy.wait()


def correlate_kernel(yh_ref, yl_ref, table_ref, inverse_ref, pick_ref, lags_ref, spec_ref, power_ref, u_ref, cross_ref):
    pair_count = pick_ref.shape[0] // 2
    re, im = slice(0, LANES), slice(LANES, 2 * LANES)
    for j in range(HALF):
        high, low = _forward_whole(j, table_ref[2 * j]), _forward_whole(j, table_ref[2 * j + 1])
        spec = _dot(yh_ref[j], high) + _dot(yh_ref[j], low) + _dot(yl_ref[j], high)
        spec_ref[j] = spec
        power = spec[:, re] * spec[:, re] + spec[:, im] * spec[:, im]
        power_ref[...] = power if j == 0 else power_ref[...] + power

    power_ref[...] = 1.0 / jnp.sqrt(_band_mean(power_ref[...]) + 1e-05)

    def ends_of(j):
        scale = power_ref[...]
        white = jnp.concatenate(
            [(spec_ref[j, :, re] * scale).astype(BF16), (spec_ref[j, :, im] * scale).astype(BF16)], axis=1
        )
        return _dot(pick_ref[...], white)

    half = pair_count // 2
    queue = [ends_of(0), ends_of(1)]
    for j in range(HALF):
        ends = queue.pop(0)
        if j + 2 < HALF:
            queue.append(ends_of(j + 2))
        a, c = ends[:pair_count], ends[pair_count:]
        cross = jnp.concatenate(
            [
                (a[:, re] * c[:, re] + a[:, im] * c[:, im]).astype(BF16),
                (a[:, im] * c[:, re] - a[:, re] * c[:, im]).astype(BF16),
            ],
            axis=1,
        )
        u_ref[j, :half] = _dot(cross[:half], _inverse_whole(j, inverse_ref[j]))
        cross_ref[j] = cross[half:]

    me = lax.axis_index("seg")
    even = lax.axis_index("tile") % 2 == 0
    blocks = lags_ref.shape[0]
    width = lags_ref.shape[2] // LANES

    def lags_of(rows):
        u = [(u_ref[0, rows, re], None)]
        u += [(u_ref[j, rows, re], u_ref[j, rows, im]) for j in range(1, HALF)]
        u += [(u_ref[0, rows, im], None)]
        lags = _inverse32(u)
        for s in range(blocks):
            place = lax.rem(jnp.where(even, s - me, me - s) + blocks, blocks)
            for h in range(width):
                lags_ref[place, rows, h * LANES : (h + 1) * LANES] = lags[s * width + h].astype(BF16)

    steps = half // ROWS
    for j in range(HALF):
        u_ref[j, half:] = _dot(cross_ref[j], _inverse_whole(j, inverse_ref[j]))
        for i in range(j * steps // HALF, (j + 1) * steps // HALF):
            lags_of(slice(i * ROWS, (i + 1) * ROWS))

    @pl.loop(steps, pair_count // ROWS)
    def _(i):
        lags_of(pl.ds(pl.multiple_of(i * ROWS, ROWS), ROWS))


def pack_kernel(lags_ref, far_ref, ahead_ref, back_ref, ahead1_ref, back1_ref, keep_ref):
    far_ref[...] = lags_ref[4]
    ahead_ref[...], back_ref[...] = lags_ref[3], lags_ref[5]
    ahead1_ref[...], back1_ref[...] = lags_ref[1], lags_ref[7]
    keep_ref[0], keep_ref[1], keep_ref[2] = lags_ref[0], lags_ref[2], lags_ref[6]


def relay_kernel(keep_ref, far_ref, ahead_ref, back_ref, ahead_out_ref, back_out_ref):
    ahead = keep_ref[1].astype(F32) + far_ref[...].astype(F32) + ahead_ref[...].astype(F32)
    back = keep_ref[2].astype(F32) + back_ref[...].astype(F32)
    ahead_out_ref[...] = ahead.astype(BF16)
    back_out_ref[...] = back.astype(BF16)


def sum_kernel(keep_ref, ahead_ref, back_ref, ahead2_ref, back2_ref, out_hbm, out_ref, sems):
    half = out_ref.shape[0] // 2
    copies = []
    for i in range(2):
        part = slice(i * half, (i + 1) * half)
        total = keep_ref[0, :, part].astype(F32) + ahead_ref[:, part].astype(F32) + back_ref[:, part].astype(F32)
        total = total + ahead2_ref[:, part].astype(F32) + back2_ref[:, part].astype(F32)
        out_ref[part] = total.T.astype(BF16)
        copies.append(pltpu.make_async_copy(out_ref.at[part], out_hbm.at[part], sems.at[i]))
        copies[i].start()
    for copy in copies:
        copy.wait()


VMEM = pl.BlockSpec(memory_space=pltpu.VMEM)
ANY = pl.BlockSpec(memory_space=pl.ANY)
MIB = 1024 * 1024


def _call(kernel, name, inputs, outputs, args, scratch=(), limit=4, place=VMEM):
    return pl.pallas_call(
        kernel,
        out_shape=outputs,
        in_specs=inputs,
        out_specs=(place,) * len(outputs),
        scratch_shapes=scratch,
        compiler_params=pltpu.CompilerParams(vmem_limit_bytes=limit * MIB),
        name=name,
    )(*args)


def _in_hbm(value):
    return pltpu.with_memory_space_constraint(value, pltpu.HBM)


def shards(samples, pair_list, sensor_home):
    tiles = lax.axis_size("tile")
    segments = lax.axis_size("seg")
    local = samples[0]
    sens_dev, seg_len = local.shape
    pair_dev = pair_list.shape[1]
    rows = tiles * CAP
    lags = NLAG // segments
    shape = jax.ShapeDtypeStruct
    home = sensor_home.reshape(-1, LANES)
    forward, inverse = _upper_halves(_forward_tables(), _inverse_tables(segments))
    forward = np.stack(_split(forward), axis=1).reshape(2 * HALF, LANES, 2 * LANES)
    inverse = jnp.asarray(inverse.astype(BF16))
    want, pick, inverse = _call(
        functools.partial(request_kernel, tiles),
        "request",
        [ANY] * 3,
        (
            pltpu.VMEM((tiles, CAP, sens_dev), BF16),
            pltpu.VMEM((2 * pair_dev, rows), BF16),
            pltpu.VMEM(inverse.shape, BF16),
        ),
        (_in_hbm(pair_list), _in_hbm(home), _in_hbm(inverse)),
        [
            pltpu.VMEM(pair_list.shape, jnp.int32),
            pltpu.VMEM(home.shape, jnp.int32),
            pltpu.SemaphoreType.DMA((3,)),
        ],
    )
    asked = lax.all_to_all(want, "tile", split_axis=0, concat_axis=0, tiled=True)
    outgoing = jnp.dot(asked.reshape(rows, sens_dev), local, preferred_element_type=F32).astype(BF16)
    arrived = lax.all_to_all(
        outgoing.reshape(tiles, CAP, seg_len), "tile", split_axis=0, concat_axis=0, tiled=True
    )
    lag_block = (pair_dev, lags)
    spectra = pltpu.VMEM((HALF, rows, 2 * LANES), BF16)
    yh, yl, forward = _call(
        transform_kernel,
        "transform",
        [VMEM, ANY],
        (spectra, spectra, pltpu.VMEM(forward.shape, BF16)),
        (arrived.reshape(rows, seg_len), _in_hbm(jnp.asarray(forward))),
        [pltpu.SemaphoreType.DMA((1,))],
        limit=16,
    )
    (blocks,) = _call(
        correlate_kernel,
        "correlate",
        [VMEM] * 5,
        (pltpu.VMEM((segments,) + lag_block, BF16),),
        (yh, yl, forward, inverse, pick),
        [
            pltpu.VMEM((HALF, rows, 2 * LANES), F32),
            pltpu.VMEM((rows, LANES), F32),
            pltpu.VMEM((HALF, pair_dev, 2 * LANES), F32),
            pltpu.VMEM((HALF, pair_dev // 2, 2 * LANES), BF16),
        ],
        limit=24,
    )
    far, ahead, back, ahead1, back1, keep = _call(
        pack_kernel,
        "pack",
        [VMEM],
        tuple(pltpu.VMEM(n + lag_block, BF16) for n in ((), (), (), (), (), (3,))),
        (blocks,),
    )

    def shift(value, steps):
        ring = [
            (s * tiles + t, (s + (-steps if t % 2 else steps)) % segments * tiles + t)
            for s in range(segments)
            for t in range(tiles)
        ]
        return lax.ppermute(value, ("seg", "tile"), ring)

    far, ahead, back = shift(far, 2), shift(ahead, 1), shift(back, -1)
    ahead1, back1 = shift(ahead1, 1), shift(back1, -1)
    ahead2, back2 = _call(
        relay_kernel,
        "relay",
        [VMEM] * 4,
        (pltpu.VMEM(lag_block, BF16),) * 2,
        (keep, far, ahead, back),
    )
    ahead2, back2 = shift(ahead2, 2), shift(back2, -2)
    (out,) = _call(
        sum_kernel,
        "stack",
        [VMEM] * 5,
        (shape((lags, pair_dev), BF16),),
        (keep, ahead1, back1, ahead2, back2),
        [pltpu.VMEM((lags, pair_dev), BF16), pltpu.SemaphoreType.DMA((2,))],
        place=ANY,
    )
    return out


def solution(mesh):
    return jax.shard_map(
        shards,
        mesh=mesh,
        in_specs=(P("seg", "tile", None), P(None, "tile"), P()),
        out_specs=P("seg", "tile"),
        check_vma=False,
    )
```

```python
import functools
import math

import jax
import jax.numpy as jnp
import numpy as np
from jax import lax
from jax.experimental import pallas as pl
from jax.experimental.pallas import tpu as pltpu
from jax.sharding import PartitionSpec as P

NFFT = 4096
NF = 2048
BAND = 64
NLAG = 2048
CAP = 8
RADIX = 32
LANES = 128
HALF = RADIX // 2
F32 = jnp.float32
BF16 = jnp.bfloat16


def _bins():
    k2 = np.arange(NF // RADIX)
    low = [np.arange(HALF), np.concatenate([[HALF], RADIX - np.arange(1, HALF)])]
    return np.concatenate([c[:, None] + RADIX * k2[None, :] for c in low], axis=1)


def _forward_tables():
    bins = _bins()
    n2 = np.arange(LANES)
    half = NF // RADIX
    tables = np.zeros((HALF, 2 * LANES, 2 * LANES))
    for j in range(HALF):
        angle = -2.0 * np.pi * ((n2[:, None] * bins[j][None, :]) % NFFT) / NFFT
        c, s = np.cos(angle), np.sin(angle)
        a, b = slice(0, half), slice(half, LANES)
        top, low = tables[j, :LANES], tables[j, LANES:]
        re, im = slice(0, LANES), slice(LANES, 2 * LANES)
        if j == 0:
            top[:, re][:, a], top[:, im][:, a] = c[:, a], s[:, a]
            low[:, re][:, b], low[:, im][:, b] = c[:, b], s[:, b]
        else:
            sign = np.where(np.arange(LANES) < half, 1.0, -1.0)[None, :]
            top[:, re], top[:, im] = c, s
            low[:, re], low[:, im] = -sign * s, sign * c
    return tables


def _inverse_tables(segments):
    bins = _bins()
    t2 = np.arange(LANES)
    half = NF // RADIX
    tables = np.zeros((HALF, 2 * LANES, 2 * LANES))
    for j in range(HALF):
        weight = np.where(bins[j] == 0, 1.0, 2.0) / math.sqrt(NFFT * segments)
        angle = 2.0 * np.pi * ((bins[j][:, None] * t2[None, :]) % NFFT) / NFFT
        wave = weight[:, None] * np.exp(1j * angle)
        if j == 0:
            for part, cols in ((slice(0, half), slice(0, LANES)), (slice(half, LANES), slice(LANES, 2 * LANES))):
                tables[0, :LANES, cols][part] = wave.real[part]
                tables[0, LANES:, cols][part] = -wave.imag[part]
        else:
            turn = (-1j) ** j
            first = (np.arange(LANES) < half)[:, None]
            of_re = turn * np.where(first, wave, np.conj(wave))
            of_im = turn * np.where(first, 1j * wave, np.conj(1j * wave))
            tables[j, :LANES, :LANES], tables[j, :LANES, LANES:] = of_re.real, of_re.imag
            tables[j, LANES:, :LANES], tables[j, LANES:, LANES:] = of_im.real, of_im.imag
    return tables


def _upper_halves(tables, inverse):
    upper = tables[:, :LANES].copy()
    upper[0] += tables[0, LANES:]
    inverse_upper = inverse[:, :LANES].copy()
    folded = inverse[0, :, :LANES] + inverse[0, :, LANES:]
    inverse_upper[0] = np.concatenate([folded[:LANES], folded[LANES:]], axis=1)
    return upper, inverse_upper


def _forward_whole(j, upper):
    c, s = upper[:, :LANES], upper[:, LANES:]
    first = lax.broadcasted_iota(jnp.int32, c.shape, 1) < NF // RADIX
    none = jnp.zeros_like(c)
    if j == 0:
        above = [jnp.where(first, c, none), jnp.where(first, s, none)]
        below = [jnp.where(first, none, c), jnp.where(first, none, s)]
    else:
        above = [c, s]
        below = [jnp.where(first, -s, s), jnp.where(first, c, -c)]
    return jnp.concatenate([jnp.concatenate(above, axis=1), jnp.concatenate(below, axis=1)], axis=0)


def _inverse_whole(j, upper):
    half = NF // RADIX
    a, b = upper[:, :LANES], upper[:, LANES:]
    none = jnp.zeros_like(a[:half])
    if j == 0:
        parts = [(a[:half], none), (none, a[half:]), (b[:half], none), (none, b[half:])]
    else:
        parts = [(a[:half], b[:half]), (a[half:], b[half:]), (-b[:half], a[:half]), (b[half:], -a[half:])]
    return jnp.concatenate([jnp.concatenate(p, axis=1) for p in parts], axis=0)


def _split(table):
    high = table.astype(BF16)
    low = (table - high.astype(np.float64)).astype(BF16)
    return high, low


def _turn(z, k, n, sign):
    re, im = z
    k = k % n
    if k == 0:
        return z
    if 4 * k == n:
        return (-im, re) if sign > 0 else (im, -re)
    if 2 * k == n:
        return (-re, -im)
    if 8 * k == n:
        r = math.sqrt(0.5)
        return ((re - im) * r, (re + im) * r) if sign > 0 else ((re + im) * r, (im - re) * r)
    c, s = math.cos(2 * math.pi * k / n), sign * math.sin(2 * math.pi * k / n)
    return (re * c - im * s, re * s + im * c)


def _add(a, b):
    return (a[0] + b[0], a[1] + b[1])


def _sub(a, b):
    return (a[0] - b[0], a[1] - b[1])


def _dft(z, sign):
    n = len(z)
    if n == 1:
        return list(z)
    half = n // 2
    even = _dft([_add(z[i], z[i + half]) for i in range(half)], sign)
    odd = _dft([_turn(_sub(z[i], z[i + half]), i, n, sign) for i in range(half)], sign)
    return [v for pair in zip(even, odd) for v in pair]


def _odd_bins(x):
    half = len(x) // 2
    z = [_turn((x[n], -x[n + half]), n, 4 * half, -1) if n else (x[0], -x[half]) for n in range(half)]
    return _dft(z, -1)


def _place_odd(out, d, n):
    for q, v in enumerate(d):
        k = 4 * q + 1
        if 2 * k <= n:
            out[k] = v
        else:
            out[n - k] = (v[0], -v[1])


def _rdft(x):
    n = len(x)
    if n == 2:
        return [(x[0] + x[1], None), (x[0] - x[1], None)]
    half = n // 2
    out = [None] * (half + 1)
    out[::2] = _rdft([x[i] + x[i + half] for i in range(half)])
    if n == 4:
        out[1] = (x[0] - x[2], x[3] - x[1])
    else:
        _place_odd(out, _odd_bins([x[i] - x[i + half] for i in range(half)]), n)
    return out


def _forward32(x):
    out = [None] * (HALF + 1)
    out[::2] = _rdft(x)
    _place_odd(out, _odd_bins(x), RADIX)
    return out


def _odd_adjoint(u, n):
    count = n // 4
    d = []
    for q in range(count):
        k = 4 * q + 1
        d.append(u[k] if 2 * k <= n else (u[n - k][0], -u[n - k][1]))
    z = _dft(d, 1)
    y = [_turn(z[i], i, n, 1) for i in range(count)]
    return [v[0] for v in y] + [-v[1] for v in y]


def _rdft_adjoint(u):
    n = 2 * (len(u) - 1)
    if n == 2:
        return [u[0][0] + u[1][0], u[0][0] - u[1][0]]
    a = _rdft_adjoint(u[::2])
    if n == 4:
        b = [u[1][0], -u[1][1]]
    else:
        b = _odd_adjoint(u, n)
    return [p + q for p, q in zip(a, b)] + [p - q for p, q in zip(a, b)]


def _inverse32(u):
    a = _rdft_adjoint(u[::2])
    b = _odd_adjoint(u, RADIX)
    return [p + q for p, q in zip(a, b)]


def _dot(a, b, dims=((1,), (0,))):
    return lax.dot_general(a, b, (dims, ((), ())), preferred_element_type=F32)


def _band_mean(power):
    row = lax.broadcasted_iota(jnp.int32, (LANES, LANES), 0) % (NF // RADIX) // (BAND // RADIX)
    col = lax.broadcasted_iota(jnp.int32, (LANES, LANES), 1) % (NF // RADIX) // (BAND // RADIX)
    share = jnp.where(row == col, 1.0 / BAND, 0.0).astype(BF16)
    high = power.astype(BF16)
    low = (power - high.astype(F32)).astype(BF16)
    return _dot(high, share) + _dot(low, share)


def _one_hot(index, rows):
    return (lax.broadcasted_iota(jnp.int32, (rows, index.shape[1]), 0) == index).astype(F32)


def request_kernel(
    holders, pair_hbm, home_hbm, table_hbm, want_ref, pick_ref, table_ref, pair_ref, home_ref, sems
):
    copies = [
        pltpu.make_async_copy(src, dst, sems.at[i])
        for i, (src, dst) in enumerate(
            ((pair_hbm, pair_ref), (home_hbm, home_ref), (table_hbm, table_ref))
        )
    ]
    for copy in copies:
        copy.start()
    for copy in copies[:2]:
        copy.wait()
    pairs = jnp.concatenate([pair_ref[0:1, :], pair_ref[1:2, :]], axis=1)
    home = home_ref[...]
    high = _one_hot(pairs // LANES, home.shape[0])
    low = _one_hot(pairs % LANES, LANES).astype(BF16)
    stored = jnp.concatenate([home // LANES, home % LANES], axis=0).astype(F32).astype(BF16)
    columns = _dot(stored, low)
    owner = jnp.sum(columns[: home.shape[0]] * high, axis=0, keepdims=True).astype(jnp.int32)
    place = jnp.sum(columns[home.shape[0] :] * high, axis=0, keepdims=True).astype(jnp.int32)
    owners = _one_hot(owner, holders).astype(BF16)
    places = _one_hot(place, LANES).astype(BF16)
    needed = jnp.minimum(_dot(owners, places, ((1,), (1,))), 1.0)
    row = lax.broadcasted_iota(jnp.int32, (LANES, LANES), 0)
    col = lax.broadcasted_iota(jnp.int32, (LANES, LANES), 1)
    slot = _dot(needed.astype(BF16), (row < col).astype(F32).astype(BF16))
    marked = jnp.where(needed > 0.0, slot, -1.0)
    slots = lax.broadcasted_iota(jnp.int32, (CAP, LANES), 0).astype(F32)
    for holder in range(holders):
        want_ref[holder] = (marked[holder : holder + 1, :] == slots).astype(F32).astype(BF16)
    slot = jnp.minimum(slot, CAP - 1.0)
    of_pair = _dot(slot.astype(BF16), owners, ((0,), (0,)))
    slot = jnp.sum(of_pair * _one_hot(place, LANES), axis=0, keepdims=True)
    position = owner * CAP + slot.astype(jnp.int32)
    pick_ref[...] = _one_hot(position, holders * CAP).T.astype(BF16)
    copies[2].wait()


ROWS = 16


def transform_kernel(x_ref, table_hbm, yh_ref, yl_ref, table_ref, sem):
    copy = pltpu.make_async_copy(table_hbm, table_ref, sem.at[0])
    copy.start()
    row_count = x_ref.shape[0]
    re, im = slice(0, LANES), slice(LANES, 2 * LANES)

    def put(j, rows, cols, value):
        high = value.astype(BF16)
        yh_ref[j, rows, cols] = high
        yl_ref[j, rows, cols] = (value - high.astype(F32)).astype(BF16)

    @pl.loop(0, row_count // ROWS)
    def _(i):
        rows = pl.ds(pl.multiple_of(i * ROWS, ROWS), ROWS)
        x = [x_ref[rows, n * LANES : (n + 1) * LANES].astype(F32) for n in range(HALF)]
        y = _forward32(x)
        put(0, rows, re, y[0][0])
        put(0, rows, im, y[HALF][0])
        for j in range(1, HALF):
            put(j, rows, re, y[j][0])
            put(j, rows, im, y[j][1])

    copy.wait()


def correlate_kernel(yh_ref, yl_ref, table_ref, inverse_ref, pick_ref, lags_ref, spec_ref, power_ref, u_ref, cross_ref):
    pair_count = pick_ref.shape[0] // 2
    re, im = slice(0, LANES), slice(LANES, 2 * LANES)
    for j in range(HALF):
        high, low = _forward_whole(j, table_ref[2 * j]), _forward_whole(j, table_ref[2 * j + 1])
        spec = _dot(yh_ref[j], high) + _dot(yh_ref[j], low) + _dot(yl_ref[j], high)
        spec_ref[j] = spec
        power = spec[:, re] * spec[:, re] + spec[:, im] * spec[:, im]
        power_ref[...] = power if j == 0 else power_ref[...] + power

    power_ref[...] = 1.0 / jnp.sqrt(_band_mean(power_ref[...]) + 1e-05)

    def ends_of(j):
        scale = power_ref[...]
        white = jnp.concatenate(
            [(spec_ref[j, :, re] * scale).astype(BF16), (spec_ref[j, :, im] * scale).astype(BF16)], axis=1
        )
        return _dot(pick_ref[...], white)

    half = pair_count // 2
    queue = [ends_of(0), ends_of(1)]
    for j in range(HALF):
        ends = queue.pop(0)
        if j + 2 < HALF:
            queue.append(ends_of(j + 2))
        a, c = ends[:pair_count], ends[pair_count:]
        cross = jnp.concatenate(
            [
                (a[:, re] * c[:, re] + a[:, im] * c[:, im]).astype(BF16),
                (a[:, im] * c[:, re] - a[:, re] * c[:, im]).astype(BF16),
            ],
            axis=1,
        )
        u_ref[j, :half] = _dot(cross[:half], _inverse_whole(j, inverse_ref[j]))
        cross_ref[j] = cross[half:]

    me = lax.axis_index("seg")
    even = lax.axis_index("tile") % 2 == 0
    blocks = lags_ref.shape[0]
    width = lags_ref.shape[2] // LANES

    def lags_of(rows):
        u = [(u_ref[0, rows, re], None)]
        u += [(u_ref[j, rows, re], u_ref[j, rows, im]) for j in range(1, HALF)]
        u += [(u_ref[0, rows, im], None)]
        lags = _inverse32(u)
        for s in range(blocks):
            place = lax.rem(jnp.where(even, s - me, me - s) + blocks, blocks)
            for h in range(width):
                lags_ref[place, rows, h * LANES : (h + 1) * LANES] = lags[s * width + h].astype(BF16)

    steps = half // ROWS
    for j in range(HALF):
        u_ref[j, half:] = _dot(cross_ref[j], _inverse_whole(j, inverse_ref[j]))
        for i in range(j * steps // HALF, (j + 1) * steps // HALF):
            lags_of(slice(i * ROWS, (i + 1) * ROWS))

    @pl.loop(steps, pair_count // ROWS)
    def _(i):
        lags_of(pl.ds(pl.multiple_of(i * ROWS, ROWS), ROWS))


def pack_kernel(lags_ref, far_ref, ahead_ref, back_ref, ahead1_ref, back1_ref, keep_ref):
    far_ref[...] = lags_ref[4]
    ahead_ref[...], back_ref[...] = lags_ref[3], lags_ref[5]
    ahead1_ref[...], back1_ref[...] = lags_ref[1], lags_ref[7]
    keep_ref[0], keep_ref[1], keep_ref[2] = lags_ref[0], lags_ref[2], lags_ref[6]


def relay_kernel(keep_ref, far_ref, ahead_ref, back_ref, ahead_out_ref, back_out_ref):
    ahead = keep_ref[1].astype(F32) + far_ref[...].astype(F32) + ahead_ref[...].astype(F32)
    back = keep_ref[2].astype(F32) + back_ref[...].astype(F32)
    ahead_out_ref[...] = ahead.astype(BF16)
    back_out_ref[...] = back.astype(BF16)


def sum_kernel(keep_ref, ahead_ref, back_ref, back2_ref, ahead2_ref, out_hbm, out_ref, sems):
    half = out_ref.shape[0] // 2
    copies = []
    for i in range(2):
        part = slice(i * half, (i + 1) * half)
        total = keep_ref[0, :, part].astype(F32) + ahead_ref[:, part].astype(F32) + back_ref[:, part].astype(F32)
        total = total + ahead2_ref[:, part].astype(F32) + back2_ref[:, part].astype(F32)
        out_ref[part] = total.T.astype(BF16)
        copies.append(pltpu.make_async_copy(out_ref.at[part], out_hbm.at[part], sems.at[i]))
        copies[i].start()
    for copy in copies:
        copy.wait()


VMEM = pl.BlockSpec(memory_space=pltpu.VMEM)
ANY = pl.BlockSpec(memory_space=pl.ANY)
MIB = 1024 * 1024


def _call(kernel, name, inputs, outputs, args, scratch=(), limit=4, place=VMEM):
    return pl.pallas_call(
        kernel,
        out_shape=outputs,
        in_specs=inputs,
        out_specs=(place,) * len(outputs),
        scratch_shapes=scratch,
        compiler_params=pltpu.CompilerParams(vmem_limit_bytes=limit * MIB),
        name=name,
    )(*args)


def _in_hbm(value):
    return pltpu.with_memory_space_constraint(value, pltpu.HBM)


def shards(samples, pair_list, sensor_home):
    tiles = lax.axis_size("tile")
    segments = lax.axis_size("seg")
    local = samples[0]
    sens_dev, seg_len = local.shape
    pair_dev = pair_list.shape[1]
    rows = tiles * CAP
    lags = NLAG // segments
    shape = jax.ShapeDtypeStruct
    home = sensor_home.reshape(-1, LANES)
    forward, inverse = _upper_halves(_forward_tables(), _inverse_tables(segments))
    forward = np.stack(_split(forward), axis=1).reshape(2 * HALF, LANES, 2 * LANES)
    inverse = jnp.asarray(inverse.astype(BF16))
    want, pick, inverse = _call(
        functools.partial(request_kernel, tiles),
        "request",
        [ANY] * 3,
        (
            pltpu.VMEM((tiles, CAP, sens_dev), BF16),
            pltpu.VMEM((2 * pair_dev, rows), BF16),
            pltpu.VMEM(inverse.shape, BF16),
        ),
        (_in_hbm(pair_list), _in_hbm(home), _in_hbm(inverse)),
        [
            pltpu.VMEM(pair_list.shape, jnp.int32),
            pltpu.VMEM(home.shape, jnp.int32),
            pltpu.SemaphoreType.DMA((3,)),
        ],
    )
    asked = lax.all_to_all(want, "tile", split_axis=0, concat_axis=0, tiled=True)
    outgoing = jnp.dot(asked.reshape(rows, sens_dev), local, preferred_element_type=F32).astype(BF16)
    arrived = lax.all_to_all(
        outgoing.reshape(tiles, CAP, seg_len), "tile", split_axis=0, concat_axis=0, tiled=True
    )
    lag_block = (pair_dev, lags)
    spectra = pltpu.VMEM((HALF, rows, 2 * LANES), BF16)
    yh, yl, forward = _call(
        transform_kernel,
        "transform",
        [VMEM, ANY],
        (spectra, spectra, pltpu.VMEM(forward.shape, BF16)),
        (arrived.reshape(rows, seg_len), _in_hbm(jnp.asarray(forward))),
        [pltpu.SemaphoreType.DMA((1,))],
        limit=16,
    )
    (blocks,) = _call(
        correlate_kernel,
        "correlate",
        [VMEM] * 5,
        (pltpu.VMEM((segments,) + lag_block, BF16),),
        (yh, yl, forward, inverse, pick),
        [
            pltpu.VMEM((HALF, rows, 2 * LANES), F32),
            pltpu.VMEM((rows, LANES), F32),
            pltpu.VMEM((HALF, pair_dev, 2 * LANES), F32),
            pltpu.VMEM((HALF, pair_dev // 2, 2 * LANES), BF16),
        ],
        limit=24,
    )
    far, ahead, back, ahead1, back1, keep = _call(
        pack_kernel,
        "pack",
        [VMEM],
        tuple(pltpu.VMEM(n + lag_block, BF16) for n in ((), (), (), (), (), (3,))),
        (blocks,),
    )

    def shift(value, steps):
        ring = [
            (s * tiles + t, (s + (-steps if t % 2 else steps)) % segments * tiles + t)
            for s in range(segments)
            for t in range(tiles)
        ]
        return lax.ppermute(value, ("seg", "tile"), ring)

    far, ahead, back = shift(far, 2), shift(ahead, 1), shift(back, -1)
    ahead1, back1 = shift(ahead1, 1), shift(back1, -1)
    ahead2, back2 = _call(
        relay_kernel,
        "relay",
        [VMEM] * 4,
        (pltpu.VMEM(lag_block, BF16),) * 2,
        (keep, far, ahead, back),
    )
    ahead2, back2 = shift(ahead2, 2), shift(back2, -2)
    (out,) = _call(
        sum_kernel,
        "stack",
        [VMEM] * 5,
        (shape((lags, pair_dev), BF16),),
        (keep, ahead1, back1, back2, ahead2),
        [pltpu.VMEM((lags, pair_dev), BF16), pltpu.SemaphoreType.DMA((2,))],
        place=ANY,
    )
    return out


def solution(mesh):
    return jax.shard_map(
        shards,
        mesh=mesh,
        in_specs=(P("seg", "tile", None), P(None, "tile"), P()),
        out_specs=P("seg", "tile"),
        check_vma=False,
    )
```

```python
import functools
import math

import jax
import jax.numpy as jnp
import numpy as np
from jax import lax
from jax.experimental import pallas as pl
from jax.experimental.pallas import tpu as pltpu
from jax.sharding import PartitionSpec as P

NFFT = 4096
NF = 2048
BAND = 64
NLAG = 2048
CAP = 8
RADIX = 32
LANES = 128
HALF = RADIX // 2
F32 = jnp.float32
BF16 = jnp.bfloat16


def _bins():
    k2 = np.arange(NF // RADIX)
    low = [np.arange(HALF), np.concatenate([[HALF], RADIX - np.arange(1, HALF)])]
    return np.concatenate([c[:, None] + RADIX * k2[None, :] for c in low], axis=1)


def _forward_tables():
    bins = _bins()
    n2 = np.arange(LANES)
    half = NF // RADIX
    tables = np.zeros((HALF, 2 * LANES, 2 * LANES))
    for j in range(HALF):
        angle = -2.0 * np.pi * ((n2[:, None] * bins[j][None, :]) % NFFT) / NFFT
        c, s = np.cos(angle), np.sin(angle)
        a, b = slice(0, half), slice(half, LANES)
        top, low = tables[j, :LANES], tables[j, LANES:]
        re, im = slice(0, LANES), slice(LANES, 2 * LANES)
        if j == 0:
            top[:, re][:, a], top[:, im][:, a] = c[:, a], s[:, a]
            low[:, re][:, b], low[:, im][:, b] = c[:, b], s[:, b]
        else:
            sign = np.where(np.arange(LANES) < half, 1.0, -1.0)[None, :]
            top[:, re], top[:, im] = c, s
            low[:, re], low[:, im] = -sign * s, sign * c
    return tables


def _inverse_tables(segments):
    bins = _bins()
    t2 = np.arange(LANES)
    half = NF // RADIX
    tables = np.zeros((HALF, 2 * LANES, 2 * LANES))
    for j in range(HALF):
        weight = np.where(bins[j] == 0, 1.0, 2.0) / math.sqrt(NFFT * segments)
        angle = 2.0 * np.pi * ((bins[j][:, None] * t2[None, :]) % NFFT) / NFFT
        wave = weight[:, None] * np.exp(1j * angle)
        if j == 0:
            for part, cols in ((slice(0, half), slice(0, LANES)), (slice(half, LANES), slice(LANES, 2 * LANES))):
                tables[0, :LANES, cols][part] = wave.real[part]
                tables[0, LANES:, cols][part] = -wave.imag[part]
        else:
            turn = (-1j) ** j
            first = (np.arange(LANES) < half)[:, None]
            of_re = turn * np.where(first, wave, np.conj(wave))
            of_im = turn * np.where(first, 1j * wave, np.conj(1j * wave))
            tables[j, :LANES, :LANES], tables[j, :LANES, LANES:] = of_re.real, of_re.imag
            tables[j, LANES:, :LANES], tables[j, LANES:, LANES:] = of_im.real, of_im.imag
    return tables


def _upper_halves(tables, inverse):
    upper = tables[:, :LANES].copy()
    upper[0] += tables[0, LANES:]
    inverse_upper = inverse[:, :LANES].copy()
    folded = inverse[0, :, :LANES] + inverse[0, :, LANES:]
    inverse_upper[0] = np.concatenate([folded[:LANES], folded[LANES:]], axis=1)
    return upper, inverse_upper


def _forward_whole(j, upper):
    c, s = upper[:, :LANES], upper[:, LANES:]
    first = lax.broadcasted_iota(jnp.int32, c.shape, 1) < NF // RADIX
    none = jnp.zeros_like(c)
    if j == 0:
        above = [jnp.where(first, c, none), jnp.where(first, s, none)]
        below = [jnp.where(first, none, c), jnp.where(first, none, s)]
    else:
        above = [c, s]
        below = [jnp.where(first, -s, s), jnp.where(first, c, -c)]
    return jnp.concatenate([jnp.concatenate(above, axis=1), jnp.concatenate(below, axis=1)], axis=0)


def _inverse_whole(j, upper):
    half = NF // RADIX
    a, b = upper[:, :LANES], upper[:, LANES:]
    none = jnp.zeros_like(a[:half])
    if j == 0:
        parts = [(a[:half], none), (none, a[half:]), (b[:half], none), (none, b[half:])]
    else:
        parts = [(a[:half], b[:half]), (a[half:], b[half:]), (-b[:half], a[:half]), (b[half:], -a[half:])]
    return jnp.concatenate([jnp.concatenate(p, axis=1) for p in parts], axis=0)


def _split(table):
    high = table.astype(BF16)
    low = (table - high.astype(np.float64)).astype(BF16)
    return high, low


def _turn(z, k, n, sign):
    re, im = z
    k = k % n
    if k == 0:
        return z
    if 4 * k == n:
        return (-im, re) if sign > 0 else (im, -re)
    if 2 * k == n:
        return (-re, -im)
    if 8 * k == n:
        r = math.sqrt(0.5)
        return ((re - im) * r, (re + im) * r) if sign > 0 else ((re + im) * r, (im - re) * r)
    c, s = math.cos(2 * math.pi * k / n), sign * math.sin(2 * math.pi * k / n)
    return (re * c - im * s, re * s + im * c)


def _add(a, b):
    return (a[0] + b[0], a[1] + b[1])


def _sub(a, b):
    return (a[0] - b[0], a[1] - b[1])


def _dft(z, sign):
    n = len(z)
    if n == 1:
        return list(z)
    half = n // 2
    even = _dft([_add(z[i], z[i + half]) for i in range(half)], sign)
    odd = _dft([_turn(_sub(z[i], z[i + half]), i, n, sign) for i in range(half)], sign)
    return [v for pair in zip(even, odd) for v in pair]


def _odd_bins(x):
    half = len(x) // 2
    z = [_turn((x[n], -x[n + half]), n, 4 * half, -1) if n else (x[0], -x[half]) for n in range(half)]
    return _dft(z, -1)


def _place_odd(out, d, n):
    for q, v in enumerate(d):
        k = 4 * q + 1
        if 2 * k <= n:
            out[k] = v
        else:
            out[n - k] = (v[0], -v[1])


def _rdft(x):
    n = len(x)
    if n == 2:
        return [(x[0] + x[1], None), (x[0] - x[1], None)]
    half = n // 2
    out = [None] * (half + 1)
    out[::2] = _rdft([x[i] + x[i + half] for i in range(half)])
    if n == 4:
        out[1] = (x[0] - x[2], x[3] - x[1])
    else:
        _place_odd(out, _odd_bins([x[i] - x[i + half] for i in range(half)]), n)
    return out


def _forward32(x):
    out = [None] * (HALF + 1)
    out[::2] = _rdft(x)
    _place_odd(out, _odd_bins(x), RADIX)
    return out


def _odd_adjoint(u, n):
    count = n // 4
    d = []
    for q in range(count):
        k = 4 * q + 1
        d.append(u[k] if 2 * k <= n else (u[n - k][0], -u[n - k][1]))
    z = _dft(d, 1)
    y = [_turn(z[i], i, n, 1) for i in range(count)]
    return [v[0] for v in y] + [-v[1] for v in y]


def _rdft_adjoint(u):
    n = 2 * (len(u) - 1)
    if n == 2:
        return [u[0][0] + u[1][0], u[0][0] - u[1][0]]
    a = _rdft_adjoint(u[::2])
    if n == 4:
        b = [u[1][0], -u[1][1]]
    else:
        b = _odd_adjoint(u, n)
    return [p + q for p, q in zip(a, b)] + [p - q for p, q in zip(a, b)]


def _inverse32(u):
    a = _rdft_adjoint(u[::2])
    b = _odd_adjoint(u, RADIX)
    return [p + q for p, q in zip(a, b)]


def _dot(a, b, dims=((1,), (0,))):
    return lax.dot_general(a, b, (dims, ((), ())), preferred_element_type=F32)


def _band_mean(power):
    row = lax.broadcasted_iota(jnp.int32, (LANES, LANES), 0) % (NF // RADIX) // (BAND // RADIX)
    col = lax.broadcasted_iota(jnp.int32, (LANES, LANES), 1) % (NF // RADIX) // (BAND // RADIX)
    share = jnp.where(row == col, 1.0 / BAND, 0.0).astype(BF16)
    high = power.astype(BF16)
    low = (power - high.astype(F32)).astype(BF16)
    return _dot(high, share) + _dot(low, share)


def _one_hot(index, rows):
    return (lax.broadcasted_iota(jnp.int32, (rows, index.shape[1]), 0) == index).astype(F32)


def request_kernel(
    holders, pair_hbm, home_hbm, table_hbm, want_ref, pick_ref, table_ref, pair_ref, home_ref, sems
):
    copies = [
        pltpu.make_async_copy(src, dst, sems.at[i])
        for i, (src, dst) in enumerate(
            ((pair_hbm, pair_ref), (home_hbm, home_ref), (table_hbm, table_ref))
        )
    ]
    for copy in copies:
        copy.start()
    for copy in copies[:2]:
        copy.wait()
    pairs = jnp.concatenate([pair_ref[0:1, :], pair_ref[1:2, :]], axis=1)
    home = home_ref[...]
    high = _one_hot(pairs // LANES, home.shape[0])
    low = _one_hot(pairs % LANES, LANES).astype(BF16)
    stored = jnp.concatenate([home // LANES, home % LANES], axis=0).astype(F32).astype(BF16)
    columns = _dot(stored, low)
    owner = jnp.sum(columns[: home.shape[0]] * high, axis=0, keepdims=True).astype(jnp.int32)
    place = jnp.sum(columns[home.shape[0] :] * high, axis=0, keepdims=True).astype(jnp.int32)
    owners = _one_hot(owner, holders).astype(BF16)
    places = _one_hot(place, LANES).astype(BF16)
    needed = jnp.minimum(_dot(owners, places, ((1,), (1,))), 1.0)
    row = lax.broadcasted_iota(jnp.int32, (LANES, LANES), 0)
    col = lax.broadcasted_iota(jnp.int32, (LANES, LANES), 1)
    slot = _dot(needed.astype(BF16), (row < col).astype(F32).astype(BF16))
    marked = jnp.where(needed > 0.0, slot, -1.0)
    slots = lax.broadcasted_iota(jnp.int32, (CAP, LANES), 0).astype(F32)
    for holder in range(holders):
        want_ref[holder] = (marked[holder : holder + 1, :] == slots).astype(F32).astype(BF16)
    slot = jnp.minimum(slot, CAP - 1.0)
    of_pair = _dot(slot.astype(BF16), owners, ((0,), (0,)))
    slot = jnp.sum(of_pair * _one_hot(place, LANES), axis=0, keepdims=True)
    position = owner * CAP + slot.astype(jnp.int32)
    pick_ref[...] = _one_hot(position, holders * CAP).T.astype(BF16)
    copies[2].wait()


ROWS = 16


def transform_kernel(x_ref, table_hbm, yh_ref, yl_ref, table_ref, sem):
    copy = pltpu.make_async_copy(table_hbm, table_ref, sem.at[0])
    copy.start()
    row_count = x_ref.shape[0]
    re, im = slice(0, LANES), slice(LANES, 2 * LANES)

    def put(j, rows, cols, value):
        high = value.astype(BF16)
        yh_ref[j, rows, cols] = high
        yl_ref[j, rows, cols] = (value - high.astype(F32)).astype(BF16)

    @pl.loop(0, row_count // ROWS)
    def _(i):
        rows = pl.ds(pl.multiple_of(i * ROWS, ROWS), ROWS)
        x = [x_ref[rows, n * LANES : (n + 1) * LANES].astype(F32) for n in range(HALF)]
        y = _forward32(x)
        put(0, rows, re, y[0][0])
        put(0, rows, im, y[HALF][0])
        for j in range(1, HALF):
            put(j, rows, re, y[j][0])
            put(j, rows, im, y[j][1])

    copy.wait()


def correlate_kernel(yh_ref, yl_ref, table_ref, inverse_ref, pick_ref, lags_ref, spec_ref, power_ref, u_ref, cross_ref):
    pair_count = pick_ref.shape[0] // 2
    re, im = slice(0, LANES), slice(LANES, 2 * LANES)
    for j in range(HALF):
        high, low = _forward_whole(j, table_ref[2 * j]), _forward_whole(j, table_ref[2 * j + 1])
        spec = _dot(yh_ref[j], high) + _dot(yh_ref[j], low) + _dot(yl_ref[j], high)
        spec_ref[j] = spec
        power = spec[:, re] * spec[:, re] + spec[:, im] * spec[:, im]
        power_ref[...] = power if j == 0 else power_ref[...] + power

    power_ref[...] = 1.0 / jnp.sqrt(_band_mean(power_ref[...]) + 1e-05)

    def ends_of(j):
        scale = power_ref[...]
        white = jnp.concatenate(
            [(spec_ref[j, :, re] * scale).astype(BF16), (spec_ref[j, :, im] * scale).astype(BF16)], axis=1
        )
        return _dot(pick_ref[...], white)

    half = pair_count // 2
    queue = [ends_of(0), ends_of(1)]
    for j in range(HALF):
        ends = queue.pop(0)
        if j + 2 < HALF:
            queue.append(ends_of(j + 2))
        a, c = ends[:pair_count], ends[pair_count:]
        cross = jnp.concatenate(
            [
                (a[:, re] * c[:, re] + a[:, im] * c[:, im]).astype(BF16),
                (a[:, im] * c[:, re] - a[:, re] * c[:, im]).astype(BF16),
            ],
            axis=1,
        )
        u_ref[j, :half] = _dot(cross[:half], _inverse_whole(j, inverse_ref[j]))
        cross_ref[j] = cross[half:]

    me = lax.axis_index("seg")
    even = lax.axis_index("tile") % 2 == 0
    blocks = lags_ref.shape[0]
    width = lags_ref.shape[2] // LANES

    def lags_of(rows):
        u = [(u_ref[0, rows, re], None)]
        u += [(u_ref[j, rows, re], u_ref[j, rows, im]) for j in range(1, HALF)]
        u += [(u_ref[0, rows, im], None)]
        lags = _inverse32(u)
        for s in range(blocks):
            place = lax.rem(jnp.where(even, s - me, me - s) + blocks, blocks)
            for h in range(width):
                lags_ref[place, rows, h * LANES : (h + 1) * LANES] = lags[s * width + h].astype(BF16)

    steps = half // ROWS
    for j in range(HALF):
        u_ref[j, half:] = _dot(cross_ref[j], _inverse_whole(j, inverse_ref[j]))
        for i in range(j * steps // HALF, (j + 1) * steps // HALF):
            lags_of(slice(i * ROWS, (i + 1) * ROWS))

    @pl.loop(steps, pair_count // ROWS)
    def _(i):
        lags_of(pl.ds(pl.multiple_of(i * ROWS, ROWS), ROWS))


def pack_kernel(lags_ref, far_ref, ahead_ref, back_ref, ahead1_ref, back1_ref, keep_ref):
    far_ref[...] = lags_ref[4]
    ahead_ref[...], back_ref[...] = lags_ref[3], lags_ref[5]
    ahead1_ref[...], back1_ref[...] = lags_ref[1], lags_ref[7]
    keep_ref[0], keep_ref[1], keep_ref[2] = lags_ref[0], lags_ref[2], lags_ref[6]


def relay_kernel(keep_ref, far_ref, ahead_ref, back_ref, ahead_out_ref, back_out_ref):
    ahead = keep_ref[1].astype(F32) + far_ref[...].astype(F32) + ahead_ref[...].astype(F32)
    back = keep_ref[2].astype(F32) + back_ref[...].astype(F32)
    ahead_out_ref[...] = ahead.astype(BF16)
    back_out_ref[...] = back.astype(BF16)


def sum_kernel(keep_ref, back_ref, ahead_ref, back2_ref, ahead2_ref, out_hbm, out_ref, sems):
    half = out_ref.shape[0] // 2
    copies = []
    for i in range(2):
        part = slice(i * half, (i + 1) * half)
        total = keep_ref[0, :, part].astype(F32) + ahead_ref[:, part].astype(F32) + back_ref[:, part].astype(F32)
        total = total + ahead2_ref[:, part].astype(F32) + back2_ref[:, part].astype(F32)
        out_ref[part] = total.T.astype(BF16)
        copies.append(pltpu.make_async_copy(out_ref.at[part], out_hbm.at[part], sems.at[i]))
        copies[i].start()
    for copy in copies:
        copy.wait()


VMEM = pl.BlockSpec(memory_space=pltpu.VMEM)
ANY = pl.BlockSpec(memory_space=pl.ANY)
MIB = 1024 * 1024


def _call(kernel, name, inputs, outputs, args, scratch=(), limit=4, place=VMEM):
    return pl.pallas_call(
        kernel,
        out_shape=outputs,
        in_specs=inputs,
        out_specs=(place,) * len(outputs),
        scratch_shapes=scratch,
        compiler_params=pltpu.CompilerParams(vmem_limit_bytes=limit * MIB),
        name=name,
    )(*args)


def _in_hbm(value):
    return pltpu.with_memory_space_constraint(value, pltpu.HBM)


def shards(samples, pair_list, sensor_home):
    tiles = lax.axis_size("tile")
    segments = lax.axis_size("seg")
    local = samples[0]
    sens_dev, seg_len = local.shape
    pair_dev = pair_list.shape[1]
    rows = tiles * CAP
    lags = NLAG // segments
    shape = jax.ShapeDtypeStruct
    home = sensor_home.reshape(-1, LANES)
    forward, inverse = _upper_halves(_forward_tables(), _inverse_tables(segments))
    forward = np.stack(_split(forward), axis=1).reshape(2 * HALF, LANES, 2 * LANES)
    inverse = jnp.asarray(inverse.astype(BF16))
    want, pick, inverse = _call(
        functools.partial(request_kernel, tiles),
        "request",
        [ANY] * 3,
        (
            pltpu.VMEM((tiles, CAP, sens_dev), BF16),
            pltpu.VMEM((2 * pair_dev, rows), BF16),
            pltpu.VMEM(inverse.shape, BF16),
        ),
        (_in_hbm(pair_list), _in_hbm(home), _in_hbm(inverse)),
        [
            pltpu.VMEM(pair_list.shape, jnp.int32),
            pltpu.VMEM(home.shape, jnp.int32),
            pltpu.SemaphoreType.DMA((3,)),
        ],
    )
    asked = lax.all_to_all(want, "tile", split_axis=0, concat_axis=0, tiled=True)
    outgoing = jnp.dot(asked.reshape(rows, sens_dev), local, preferred_element_type=F32).astype(BF16)
    arrived = lax.all_to_all(
        outgoing.reshape(tiles, CAP, seg_len), "tile", split_axis=0, concat_axis=0, tiled=True
    )
    lag_block = (pair_dev, lags)
    spectra = pltpu.VMEM((HALF, rows, 2 * LANES), BF16)
    yh, yl, forward = _call(
        transform_kernel,
        "transform",
        [VMEM, ANY],
        (spectra, spectra, pltpu.VMEM(forward.shape, BF16)),
        (arrived.reshape(rows, seg_len), _in_hbm(jnp.asarray(forward))),
        [pltpu.SemaphoreType.DMA((1,))],
        limit=16,
    )
    (blocks,) = _call(
        correlate_kernel,
        "correlate",
        [VMEM] * 5,
        (pltpu.VMEM((segments,) + lag_block, BF16),),
        (yh, yl, forward, inverse, pick),
        [
            pltpu.VMEM((HALF, rows, 2 * LANES), F32),
            pltpu.VMEM((rows, LANES), F32),
            pltpu.VMEM((HALF, pair_dev, 2 * LANES), F32),
            pltpu.VMEM((HALF, pair_dev // 2, 2 * LANES), BF16),
        ],
        limit=24,
    )
    far, ahead, back, ahead1, back1, keep = _call(
        pack_kernel,
        "pack",
        [VMEM],
        tuple(pltpu.VMEM(n + lag_block, BF16) for n in ((), (), (), (), (), (3,))),
        (blocks,),
    )

    def shift(value, steps):
        ring = [
            (s * tiles + t, (s + (-steps if t % 2 else steps)) % segments * tiles + t)
            for s in range(segments)
            for t in range(tiles)
        ]
        return lax.ppermute(value, ("seg", "tile"), ring)

    far, ahead, back = shift(far, 2), shift(ahead, 1), shift(back, -1)
    ahead1, back1 = shift(ahead1, 1), shift(back1, -1)
    ahead2, back2 = _call(
        relay_kernel,
        "relay",
        [VMEM] * 4,
        (pltpu.VMEM(lag_block, BF16),) * 2,
        (keep, far, ahead, back),
    )
    ahead2, back2 = shift(ahead2, 2), shift(back2, -2)
    (out,) = _call(
        sum_kernel,
        "stack",
        [VMEM] * 5,
        (shape((lags, pair_dev), BF16),),
        (keep, back1, ahead1, back2, ahead2),
        [pltpu.VMEM((lags, pair_dev), BF16), pltpu.SemaphoreType.DMA((2,))],
        place=ANY,
    )
    return out


def solution(mesh):
    return jax.shard_map(
        shards,
        mesh=mesh,
        in_specs=(P("seg", "tile", None), P(None, "tile"), P()),
        out_specs=P("seg", "tile"),
        check_vma=False,
    )
```

```python
import functools
import math

import jax
import jax.numpy as jnp
import numpy as np
from jax import lax
from jax.experimental import pallas as pl
from jax.experimental.pallas import tpu as pltpu
from jax.sharding import PartitionSpec as P

NFFT = 4096
NF = 2048
BAND = 64
NLAG = 2048
CAP = 8
RADIX = 32
LANES = 128
HALF = RADIX // 2
F32 = jnp.float32
BF16 = jnp.bfloat16


def _bins():
    k2 = np.arange(NF // RADIX)
    low = [np.arange(HALF), np.concatenate([[HALF], RADIX - np.arange(1, HALF)])]
    return np.concatenate([c[:, None] + RADIX * k2[None, :] for c in low], axis=1)


def _forward_tables():
    bins = _bins()
    n2 = np.arange(LANES)
    half = NF // RADIX
    tables = np.zeros((HALF, 2 * LANES, 2 * LANES))
    for j in range(HALF):
        angle = -2.0 * np.pi * ((n2[:, None] * bins[j][None, :]) % NFFT) / NFFT
        c, s = np.cos(angle), np.sin(angle)
        a, b = slice(0, half), slice(half, LANES)
        top, low = tables[j, :LANES], tables[j, LANES:]
        re, im = slice(0, LANES), slice(LANES, 2 * LANES)
        if j == 0:
            top[:, re][:, a], top[:, im][:, a] = c[:, a], s[:, a]
            low[:, re][:, b], low[:, im][:, b] = c[:, b], s[:, b]
        else:
            sign = np.where(np.arange(LANES) < half, 1.0, -1.0)[None, :]
            top[:, re], top[:, im] = c, s
            low[:, re], low[:, im] = -sign * s, sign * c
    return tables


def _inverse_tables(segments):
    bins = _bins()
    t2 = np.arange(LANES)
    half = NF // RADIX
    tables = np.zeros((HALF, 2 * LANES, 2 * LANES))
    for j in range(HALF):
        weight = np.where(bins[j] == 0, 1.0, 2.0) / math.sqrt(NFFT * segments)
        angle = 2.0 * np.pi * ((bins[j][:, None] * t2[None, :]) % NFFT) / NFFT
        wave = weight[:, None] * np.exp(1j * angle)
        if j == 0:
            for part, cols in ((slice(0, half), slice(0, LANES)), (slice(half, LANES), slice(LANES, 2 * LANES))):
                tables[0, :LANES, cols][part] = wave.real[part]
                tables[0, LANES:, cols][part] = -wave.imag[part]
        else:
            turn = (-1j) ** j
            first = (np.arange(LANES) < half)[:, None]
            of_re = turn * np.where(first, wave, np.conj(wave))
            of_im = turn * np.where(first, 1j * wave, np.conj(1j * wave))
            tables[j, :LANES, :LANES], tables[j, :LANES, LANES:] = of_re.real, of_re.imag
            tables[j, LANES:, :LANES], tables[j, LANES:, LANES:] = of_im.real, of_im.imag
    return tables


def _upper_halves(tables, inverse):
    upper = tables[:, :LANES].copy()
    upper[0] += tables[0, LANES:]
    inverse_upper = inverse[:, :LANES].copy()
    folded = inverse[0, :, :LANES] + inverse[0, :, LANES:]
    inverse_upper[0] = np.concatenate([folded[:LANES], folded[LANES:]], axis=1)
    return upper, inverse_upper


def _forward_whole(j, upper):
    c, s = upper[:, :LANES], upper[:, LANES:]
    first = lax.broadcasted_iota(jnp.int32, c.shape, 1) < NF // RADIX
    none = jnp.zeros_like(c)
    if j == 0:
        above = [jnp.where(first, c, none), jnp.where(first, s, none)]
        below = [jnp.where(first, none, c), jnp.where(first, none, s)]
    else:
        above = [c, s]
        below = [jnp.where(first, -s, s), jnp.where(first, c, -c)]
    return jnp.concatenate([jnp.concatenate(above, axis=1), jnp.concatenate(below, axis=1)], axis=0)


def _inverse_whole(j, upper):
    half = NF // RADIX
    a, b = upper[:, :LANES], upper[:, LANES:]
    none = jnp.zeros_like(a[:half])
    if j == 0:
        parts = [(a[:half], none), (none, a[half:]), (b[:half], none), (none, b[half:])]
    else:
        parts = [(a[:half], b[:half]), (a[half:], b[half:]), (-b[:half], a[:half]), (b[half:], -a[half:])]
    return jnp.concatenate([jnp.concatenate(p, axis=1) for p in parts], axis=0)


def _split(table):
    high = table.astype(BF16)
    low = (table - high.astype(np.float64)).astype(BF16)
    return high, low


def _turn(z, k, n, sign):
    re, im = z
    k = k % n
    if k == 0:
        return z
    if 4 * k == n:
        return (-im, re) if sign > 0 else (im, -re)
    if 2 * k == n:
        return (-re, -im)
    if 8 * k == n:
        r = math.sqrt(0.5)
        return ((re - im) * r, (re + im) * r) if sign > 0 else ((re + im) * r, (im - re) * r)
    c, s = math.cos(2 * math.pi * k / n), sign * math.sin(2 * math.pi * k / n)
    return (re * c - im * s, re * s + im * c)


def _add(a, b):
    return (a[0] + b[0], a[1] + b[1])


def _sub(a, b):
    return (a[0] - b[0], a[1] - b[1])


def _dft(z, sign):
    n = len(z)
    if n == 1:
        return list(z)
    half = n // 2
    even = _dft([_add(z[i], z[i + half]) for i in range(half)], sign)
    odd = _dft([_turn(_sub(z[i], z[i + half]), i, n, sign) for i in range(half)], sign)
    return [v for pair in zip(even, odd) for v in pair]


def _odd_bins(x):
    half = len(x) // 2
    z = [_turn((x[n], -x[n + half]), n, 4 * half, -1) if n else (x[0], -x[half]) for n in range(half)]
    return _dft(z, -1)


def _place_odd(out, d, n):
    for q, v in enumerate(d):
        k = 4 * q + 1
        if 2 * k <= n:
            out[k] = v
        else:
            out[n - k] = (v[0], -v[1])


def _rdft(x):
    n = len(x)
    if n == 2:
        return [(x[0] + x[1], None), (x[0] - x[1], None)]
    half = n // 2
    out = [None] * (half + 1)
    out[::2] = _rdft([x[i] + x[i + half] for i in range(half)])
    if n == 4:
        out[1] = (x[0] - x[2], x[3] - x[1])
    else:
        _place_odd(out, _odd_bins([x[i] - x[i + half] for i in range(half)]), n)
    return out


def _forward32(x):
    out = [None] * (HALF + 1)
    out[::2] = _rdft(x)
    _place_odd(out, _odd_bins(x), RADIX)
    return out


def _odd_adjoint(u, n):
    count = n // 4
    d = []
    for q in range(count):
        k = 4 * q + 1
        d.append(u[k] if 2 * k <= n else (u[n - k][0], -u[n - k][1]))
    z = _dft(d, 1)
    y = [_turn(z[i], i, n, 1) for i in range(count)]
    return [v[0] for v in y] + [-v[1] for v in y]


def _rdft_adjoint(u):
    n = 2 * (len(u) - 1)
    if n == 2:
        return [u[0][0] + u[1][0], u[0][0] - u[1][0]]
    a = _rdft_adjoint(u[::2])
    if n == 4:
        b = [u[1][0], -u[1][1]]
    else:
        b = _odd_adjoint(u, n)
    return [p + q for p, q in zip(a, b)] + [p - q for p, q in zip(a, b)]


def _inverse32(u):
    a = _rdft_adjoint(u[::2])
    b = _odd_adjoint(u, RADIX)
    return [p + q for p, q in zip(a, b)]


def _dot(a, b, dims=((1,), (0,))):
    return lax.dot_general(a, b, (dims, ((), ())), preferred_element_type=F32)


def _band_mean(power):
    row = lax.broadcasted_iota(jnp.int32, (LANES, LANES), 0) % (NF // RADIX) // (BAND // RADIX)
    col = lax.broadcasted_iota(jnp.int32, (LANES, LANES), 1) % (NF // RADIX) // (BAND // RADIX)
    share = jnp.where(row == col, 1.0 / BAND, 0.0).astype(BF16)
    high = power.astype(BF16)
    low = (power - high.astype(F32)).astype(BF16)
    return _dot(high, share) + _dot(low, share)


def _one_hot(index, rows):
    return (lax.broadcasted_iota(jnp.int32, (rows, index.shape[1]), 0) == index).astype(F32)


def request_kernel(
    holders, pair_hbm, home_hbm, table_hbm, want_ref, pick_ref, table_ref, pair_ref, home_ref, sems
):
    copies = [
        pltpu.make_async_copy(src, dst, sems.at[i])
        for i, (src, dst) in enumerate(
            ((pair_hbm, pair_ref), (home_hbm, home_ref), (table_hbm, table_ref))
        )
    ]
    for copy in copies:
        copy.start()
    for copy in copies[:2]:
        copy.wait()
    pairs = jnp.concatenate([pair_ref[0:1, :], pair_ref[1:2, :]], axis=1)
    home = home_ref[...]
    high = _one_hot(pairs // LANES, home.shape[0])
    low = _one_hot(pairs % LANES, LANES).astype(BF16)
    stored = jnp.concatenate([home // LANES, home % LANES], axis=0).astype(F32).astype(BF16)
    columns = _dot(stored, low)
    owner = jnp.sum(columns[: home.shape[0]] * high, axis=0, keepdims=True).astype(jnp.int32)
    place = jnp.sum(columns[home.shape[0] :] * high, axis=0, keepdims=True).astype(jnp.int32)
    owners = _one_hot(owner, holders).astype(BF16)
    places = _one_hot(place, LANES).astype(BF16)
    needed = jnp.minimum(_dot(owners, places, ((1,), (1,))), 1.0)
    row = lax.broadcasted_iota(jnp.int32, (LANES, LANES), 0)
    col = lax.broadcasted_iota(jnp.int32, (LANES, LANES), 1)
    slot = _dot(needed.astype(BF16), (row < col).astype(F32).astype(BF16))
    marked = jnp.where(needed > 0.0, slot, -1.0)
    slots = lax.broadcasted_iota(jnp.int32, (CAP, LANES), 0).astype(F32)
    for holder in range(holders):
        want_ref[holder] = (marked[holder : holder + 1, :] == slots).astype(F32).astype(BF16)
    slot = jnp.minimum(slot, CAP - 1.0)
    of_pair = _dot(slot.astype(BF16), owners, ((0,), (0,)))
    slot = jnp.sum(of_pair * _one_hot(place, LANES), axis=0, keepdims=True)
    position = owner * CAP + slot.astype(jnp.int32)
    position = jnp.broadcast_to(position.astype(F32), (LANES, position.shape[1])).T
    lane = lax.broadcasted_iota(jnp.int32, position.shape, 1).astype(F32)
    for start in range(0, holders * CAP, LANES):
        pick_ref[:, start : start + LANES] = (position - start == lane).astype(F32).astype(BF16)
    copies[2].wait()


ROWS = 16


def transform_kernel(x_ref, table_hbm, yh_ref, yl_ref, table_ref, sem):
    copy = pltpu.make_async_copy(table_hbm, table_ref, sem.at[0])
    copy.start()
    row_count = x_ref.shape[0]
    re, im = slice(0, LANES), slice(LANES, 2 * LANES)

    def put(j, rows, cols, value):
        high = value.astype(BF16)
        yh_ref[j, rows, cols] = high
        yl_ref[j, rows, cols] = (value - high.astype(F32)).astype(BF16)

    @pl.loop(0, row_count // ROWS)
    def _(i):
        rows = pl.ds(pl.multiple_of(i * ROWS, ROWS), ROWS)
        x = [x_ref[rows, n * LANES : (n + 1) * LANES].astype(F32) for n in range(HALF)]
        y = _forward32(x)
        put(0, rows, re, y[0][0])
        put(0, rows, im, y[HALF][0])
        for j in range(1, HALF):
            put(j, rows, re, y[j][0])
            put(j, rows, im, y[j][1])

    copy.wait()


def correlate_kernel(yh_ref, yl_ref, table_ref, inverse_ref, pick_ref, lags_ref, spec_ref, power_ref, u_ref, cross_ref):
    pair_count = pick_ref.shape[0] // 2
    re, im = slice(0, LANES), slice(LANES, 2 * LANES)
    for j in range(HALF):
        high, low = _forward_whole(j, table_ref[2 * j]), _forward_whole(j, table_ref[2 * j + 1])
        spec = _dot(yh_ref[j], high) + _dot(yh_ref[j], low) + _dot(yl_ref[j], high)
        spec_ref[j] = spec
        power = spec[:, re] * spec[:, re] + spec[:, im] * spec[:, im]
        power_ref[...] = power if j == 0 else power_ref[...] + power

    power_ref[...] = 1.0 / jnp.sqrt(_band_mean(power_ref[...]) + 1e-05)

    def ends_of(j):
        scale = power_ref[...]
        white = jnp.concatenate(
            [(spec_ref[j, :, re] * scale).astype(BF16), (spec_ref[j, :, im] * scale).astype(BF16)], axis=1
        )
        return _dot(pick_ref[...], white)

    half = pair_count // 2
    queue = [ends_of(0), ends_of(1)]
    for j in range(HALF):
        ends = queue.pop(0)
        if j + 2 < HALF:
            queue.append(ends_of(j + 2))
        a, c = ends[:pair_count], ends[pair_count:]
        cross = jnp.concatenate(
            [
                (a[:, re] * c[:, re] + a[:, im] * c[:, im]).astype(BF16),
                (a[:, im] * c[:, re] - a[:, re] * c[:, im]).astype(BF16),
            ],
            axis=1,
        )
        u_ref[j, :half] = _dot(cross[:half], _inverse_whole(j, inverse_ref[j]))
        cross_ref[j] = cross[half:]

    me = lax.axis_index("seg")
    even = lax.axis_index("tile") % 2 == 0
    blocks = lags_ref.shape[0]
    width = lags_ref.shape[2] // LANES

    def lags_of(rows):
        u = [(u_ref[0, rows, re], None)]
        u += [(u_ref[j, rows, re], u_ref[j, rows, im]) for j in range(1, HALF)]
        u += [(u_ref[0, rows, im], None)]
        lags = _inverse32(u)
        for s in range(blocks):
            place = lax.rem(jnp.where(even, s - me, me - s) + blocks, blocks)
            for h in range(width):
                lags_ref[place, rows, h * LANES : (h + 1) * LANES] = lags[s * width + h].astype(BF16)

    steps = half // ROWS
    for j in range(HALF):
        u_ref[j, half:] = _dot(cross_ref[j], _inverse_whole(j, inverse_ref[j]))
        for i in range(j * steps // HALF, (j + 1) * steps // HALF):
            lags_of(slice(i * ROWS, (i + 1) * ROWS))

    @pl.loop(steps, pair_count // ROWS)
    def _(i):
        lags_of(pl.ds(pl.multiple_of(i * ROWS, ROWS), ROWS))


def pack_kernel(lags_ref, far_ref, ahead_ref, back_ref, ahead1_ref, back1_ref, keep_ref):
    far_ref[...] = lags_ref[4]
    ahead_ref[...], back_ref[...] = lags_ref[3], lags_ref[5]
    ahead1_ref[...], back1_ref[...] = lags_ref[1], lags_ref[7]
    keep_ref[0], keep_ref[1], keep_ref[2] = lags_ref[0], lags_ref[2], lags_ref[6]


def relay_kernel(keep_ref, far_ref, ahead_ref, back_ref, ahead_out_ref, back_out_ref):
    ahead = keep_ref[1].astype(F32) + far_ref[...].astype(F32) + ahead_ref[...].astype(F32)
    back = keep_ref[2].astype(F32) + back_ref[...].astype(F32)
    ahead_out_ref[...] = ahead.astype(BF16)
    back_out_ref[...] = back.astype(BF16)


def sum_kernel(keep_ref, back_ref, ahead_ref, back2_ref, ahead2_ref, out_hbm, out_ref, sems):
    half = out_ref.shape[0] // 2
    copies = []
    for i in range(2):
        part = slice(i * half, (i + 1) * half)
        total = keep_ref[0, :, part].astype(F32) + ahead_ref[:, part].astype(F32) + back_ref[:, part].astype(F32)
        total = total + ahead2_ref[:, part].astype(F32) + back2_ref[:, part].astype(F32)
        out_ref[part] = total.T.astype(BF16)
        copies.append(pltpu.make_async_copy(out_ref.at[part], out_hbm.at[part], sems.at[i]))
        copies[i].start()
    for copy in copies:
        copy.wait()


VMEM = pl.BlockSpec(memory_space=pltpu.VMEM)
ANY = pl.BlockSpec(memory_space=pl.ANY)
MIB = 1024 * 1024


def _call(kernel, name, inputs, outputs, args, scratch=(), limit=4, place=VMEM):
    return pl.pallas_call(
        kernel,
        out_shape=outputs,
        in_specs=inputs,
        out_specs=(place,) * len(outputs),
        scratch_shapes=scratch,
        compiler_params=pltpu.CompilerParams(vmem_limit_bytes=limit * MIB),
        name=name,
    )(*args)


def _in_hbm(value):
    return pltpu.with_memory_space_constraint(value, pltpu.HBM)


def shards(samples, pair_list, sensor_home):
    tiles = lax.axis_size("tile")
    segments = lax.axis_size("seg")
    local = samples[0]
    sens_dev, seg_len = local.shape
    pair_dev = pair_list.shape[1]
    rows = tiles * CAP
    lags = NLAG // segments
    shape = jax.ShapeDtypeStruct
    home = sensor_home.reshape(-1, LANES)
    forward, inverse = _upper_halves(_forward_tables(), _inverse_tables(segments))
    forward = np.stack(_split(forward), axis=1).reshape(2 * HALF, LANES, 2 * LANES)
    inverse = jnp.asarray(inverse.astype(BF16))
    want, pick, inverse = _call(
        functools.partial(request_kernel, tiles),
        "request",
        [ANY] * 3,
        (
            pltpu.VMEM((tiles, CAP, sens_dev), BF16),
            pltpu.VMEM((2 * pair_dev, rows), BF16),
            pltpu.VMEM(inverse.shape, BF16),
        ),
        (_in_hbm(pair_list), _in_hbm(home), _in_hbm(inverse)),
        [
            pltpu.VMEM(pair_list.shape, jnp.int32),
            pltpu.VMEM(home.shape, jnp.int32),
            pltpu.SemaphoreType.DMA((3,)),
        ],
    )
    asked = lax.all_to_all(want, "tile", split_axis=0, concat_axis=0, tiled=True)
    outgoing = jnp.dot(asked.reshape(rows, sens_dev), local, preferred_element_type=F32).astype(BF16)
    arrived = lax.all_to_all(
        outgoing.reshape(tiles, CAP, seg_len), "tile", split_axis=0, concat_axis=0, tiled=True
    )
    lag_block = (pair_dev, lags)
    spectra = pltpu.VMEM((HALF, rows, 2 * LANES), BF16)
    yh, yl, forward = _call(
        transform_kernel,
        "transform",
        [VMEM, ANY],
        (spectra, spectra, pltpu.VMEM(forward.shape, BF16)),
        (arrived.reshape(rows, seg_len), _in_hbm(jnp.asarray(forward))),
        [pltpu.SemaphoreType.DMA((1,))],
        limit=16,
    )
    (blocks,) = _call(
        correlate_kernel,
        "correlate",
        [VMEM] * 5,
        (pltpu.VMEM((segments,) + lag_block, BF16),),
        (yh, yl, forward, inverse, pick),
        [
            pltpu.VMEM((HALF, rows, 2 * LANES), F32),
            pltpu.VMEM((rows, LANES), F32),
            pltpu.VMEM((HALF, pair_dev, 2 * LANES), F32),
            pltpu.VMEM((HALF, pair_dev // 2, 2 * LANES), BF16),
        ],
        limit=24,
    )
    far, ahead, back, ahead1, back1, keep = _call(
        pack_kernel,
        "pack",
        [VMEM],
        tuple(pltpu.VMEM(n + lag_block, BF16) for n in ((), (), (), (), (), (3,))),
        (blocks,),
    )

    def shift(value, steps):
        ring = [
            (s * tiles + t, (s + (-steps if t % 2 else steps)) % segments * tiles + t)
            for s in range(segments)
            for t in range(tiles)
        ]
        return lax.ppermute(value, ("seg", "tile"), ring)

    far, ahead, back = shift(far, 2), shift(ahead, 1), shift(back, -1)
    ahead1, back1 = shift(ahead1, 1), shift(back1, -1)
    ahead2, back2 = _call(
        relay_kernel,
        "relay",
        [VMEM] * 4,
        (pltpu.VMEM(lag_block, BF16),) * 2,
        (keep, far, ahead, back),
    )
    ahead2, back2 = shift(ahead2, 2), shift(back2, -2)
    (out,) = _call(
        sum_kernel,
        "stack",
        [VMEM] * 5,
        (shape((lags, pair_dev), BF16),),
        (keep, back1, ahead1, back2, ahead2),
        [pltpu.VMEM((lags, pair_dev), BF16), pltpu.SemaphoreType.DMA((2,))],
        place=ANY,
    )
    return out


def solution(mesh):
    return jax.shard_map(
        shards,
        mesh=mesh,
        in_specs=(P("seg", "tile", None), P(None, "tile"), P()),
        out_specs=P("seg", "tile"),
        check_vma=False,
    )
```

```python
import functools
import math

import jax
import jax.numpy as jnp
import numpy as np
from jax import lax
from jax.experimental import pallas as pl
from jax.experimental.pallas import tpu as pltpu
from jax.sharding import PartitionSpec as P

NFFT = 4096
NF = 2048
BAND = 64
NLAG = 2048
CAP = 8
RADIX = 32
LANES = 128
HALF = RADIX // 2
F32 = jnp.float32
BF16 = jnp.bfloat16


def _bins():
    k2 = np.arange(NF // RADIX)
    low = [np.arange(HALF), np.concatenate([[HALF], RADIX - np.arange(1, HALF)])]
    return np.concatenate([c[:, None] + RADIX * k2[None, :] for c in low], axis=1)


def _forward_tables():
    bins = _bins()
    n2 = np.arange(LANES)
    half = NF // RADIX
    tables = np.zeros((HALF, 2 * LANES, 2 * LANES))
    for j in range(HALF):
        angle = -2.0 * np.pi * ((n2[:, None] * bins[j][None, :]) % NFFT) / NFFT
        c, s = np.cos(angle), np.sin(angle)
        a, b = slice(0, half), slice(half, LANES)
        top, low = tables[j, :LANES], tables[j, LANES:]
        re, im = slice(0, LANES), slice(LANES, 2 * LANES)
        if j == 0:
            top[:, re][:, a], top[:, im][:, a] = c[:, a], s[:, a]
            low[:, re][:, b], low[:, im][:, b] = c[:, b], s[:, b]
        else:
            sign = np.where(np.arange(LANES) < half, 1.0, -1.0)[None, :]
            top[:, re], top[:, im] = c, s
            low[:, re], low[:, im] = -sign * s, sign * c
    return tables


def _inverse_tables(segments):
    bins = _bins()
    t2 = np.arange(LANES)
    half = NF // RADIX
    tables = np.zeros((HALF, 2 * LANES, 2 * LANES))
    for j in range(HALF):
        weight = np.where(bins[j] == 0, 1.0, 2.0) / math.sqrt(NFFT * segments)
        angle = 2.0 * np.pi * ((bins[j][:, None] * t2[None, :]) % NFFT) / NFFT
        wave = weight[:, None] * np.exp(1j * angle)
        if j == 0:
            for part, cols in ((slice(0, half), slice(0, LANES)), (slice(half, LANES), slice(LANES, 2 * LANES))):
                tables[0, :LANES, cols][part] = wave.real[part]
                tables[0, LANES:, cols][part] = -wave.imag[part]
        else:
            turn = (-1j) ** j
            first = (np.arange(LANES) < half)[:, None]
            of_re = turn * np.where(first, wave, np.conj(wave))
            of_im = turn * np.where(first, 1j * wave, np.conj(1j * wave))
            tables[j, :LANES, :LANES], tables[j, :LANES, LANES:] = of_re.real, of_re.imag
            tables[j, LANES:, :LANES], tables[j, LANES:, LANES:] = of_im.real, of_im.imag
    return tables


def _upper_halves(tables, inverse):
    upper = tables[:, :LANES].copy()
    upper[0] += tables[0, LANES:]
    inverse_upper = inverse[:, :LANES].copy()
    folded = inverse[0, :, :LANES] + inverse[0, :, LANES:]
    inverse_upper[0] = np.concatenate([folded[:LANES], folded[LANES:]], axis=1)
    return upper, inverse_upper


def _forward_whole(j, upper):
    c, s = upper[:, :LANES], upper[:, LANES:]
    first = lax.broadcasted_iota(jnp.int32, c.shape, 1) < NF // RADIX
    none = jnp.zeros_like(c)
    if j == 0:
        above = [jnp.where(first, c, none), jnp.where(first, s, none)]
        below = [jnp.where(first, none, c), jnp.where(first, none, s)]
    else:
        above = [c, s]
        below = [jnp.where(first, -s, s), jnp.where(first, c, -c)]
    return jnp.concatenate([jnp.concatenate(above, axis=1), jnp.concatenate(below, axis=1)], axis=0)


def _inverse_whole(j, upper):
    half = NF // RADIX
    a, b = upper[:, :LANES], upper[:, LANES:]
    none = jnp.zeros_like(a[:half])
    if j == 0:
        parts = [(a[:half], none), (none, a[half:]), (b[:half], none), (none, b[half:])]
    else:
        parts = [(a[:half], b[:half]), (a[half:], b[half:]), (-b[:half], a[:half]), (b[half:], -a[half:])]
    return jnp.concatenate([jnp.concatenate(p, axis=1) for p in parts], axis=0)


def _split(table):
    high = table.astype(BF16)
    low = (table - high.astype(np.float64)).astype(BF16)
    return high, low


def _turn(z, k, n, sign):
    re, im = z
    k = k % n
    if k == 0:
        return z
    if 4 * k == n:
        return (-im, re) if sign > 0 else (im, -re)
    if 2 * k == n:
        return (-re, -im)
    if 8 * k == n:
        r = math.sqrt(0.5)
        return ((re - im) * r, (re + im) * r) if sign > 0 else ((re + im) * r, (im - re) * r)
    c, s = math.cos(2 * math.pi * k / n), sign * math.sin(2 * math.pi * k / n)
    return (re * c - im * s, re * s + im * c)


def _add(a, b):
    return (a[0] + b[0], a[1] + b[1])


def _sub(a, b):
    return (a[0] - b[0], a[1] - b[1])


def _dft(z, sign):
    n = len(z)
    if n == 1:
        return list(z)
    half = n // 2
    even = _dft([_add(z[i], z[i + half]) for i in range(half)], sign)
    odd = _dft([_turn(_sub(z[i], z[i + half]), i, n, sign) for i in range(half)], sign)
    return [v for pair in zip(even, odd) for v in pair]


def _odd_bins(x):
    half = len(x) // 2
    z = [_turn((x[n], -x[n + half]), n, 4 * half, -1) if n else (x[0], -x[half]) for n in range(half)]
    return _dft(z, -1)


def _place_odd(out, d, n):
    for q, v in enumerate(d):
        k = 4 * q + 1
        if 2 * k <= n:
            out[k] = v
        else:
            out[n - k] = (v[0], -v[1])


def _rdft(x):
    n = len(x)
    if n == 2:
        return [(x[0] + x[1], None), (x[0] - x[1], None)]
    half = n // 2
    out = [None] * (half + 1)
    out[::2] = _rdft([x[i] + x[i + half] for i in range(half)])
    if n == 4:
        out[1] = (x[0] - x[2], x[3] - x[1])
    else:
        _place_odd(out, _odd_bins([x[i] - x[i + half] for i in range(half)]), n)
    return out


def _forward32(x):
    out = [None] * (HALF + 1)
    out[::2] = _rdft(x)
    _place_odd(out, _odd_bins(x), RADIX)
    return out


def _odd_adjoint(u, n):
    count = n // 4
    d = []
    for q in range(count):
        k = 4 * q + 1
        d.append(u[k] if 2 * k <= n else (u[n - k][0], -u[n - k][1]))
    z = _dft(d, 1)
    y = [_turn(z[i], i, n, 1) for i in range(count)]
    return [v[0] for v in y] + [-v[1] for v in y]


def _rdft_adjoint(u):
    n = 2 * (len(u) - 1)
    if n == 2:
        return [u[0][0] + u[1][0], u[0][0] - u[1][0]]
    a = _rdft_adjoint(u[::2])
    if n == 4:
        b = [u[1][0], -u[1][1]]
    else:
        b = _odd_adjoint(u, n)
    return [p + q for p, q in zip(a, b)] + [p - q for p, q in zip(a, b)]


def _inverse32(u):
    a = _rdft_adjoint(u[::2])
    b = _odd_adjoint(u, RADIX)
    return [p + q for p, q in zip(a, b)]


def _dot(a, b, dims=((1,), (0,))):
    return lax.dot_general(a, b, (dims, ((), ())), preferred_element_type=F32)


def _band_mean(power):
    row = lax.broadcasted_iota(jnp.int32, (LANES, LANES), 0) % (NF // RADIX) // (BAND // RADIX)
    col = lax.broadcasted_iota(jnp.int32, (LANES, LANES), 1) % (NF // RADIX) // (BAND // RADIX)
    share = jnp.where(row == col, 1.0 / BAND, 0.0).astype(BF16)
    high = power.astype(BF16)
    low = (power - high.astype(F32)).astype(BF16)
    return _dot(high, share) + _dot(low, share)


def _one_hot(index, rows):
    return (lax.broadcasted_iota(jnp.int32, (rows, index.shape[1]), 0) == index).astype(F32)


def request_kernel(
    holders, pair_hbm, home_hbm, table_hbm, want_ref, pick_ref, table_ref, pair_ref, home_ref, sems
):
    copies = [
        pltpu.make_async_copy(src, dst, sems.at[i])
        for i, (src, dst) in enumerate(
            ((pair_hbm, pair_ref), (home_hbm, home_ref), (table_hbm, table_ref))
        )
    ]
    for copy in copies:
        copy.start()
    for copy in copies[:2]:
        copy.wait()
    pairs = jnp.concatenate([pair_ref[0:1, :], pair_ref[1:2, :]], axis=1)
    home = home_ref[...]
    high = _one_hot(pairs // LANES, home.shape[0])
    low = _one_hot(pairs % LANES, LANES).astype(BF16)
    stored = jnp.concatenate([home // LANES, home % LANES], axis=0).astype(F32).astype(BF16)
    columns = _dot(stored, low)
    owner = jnp.sum(columns[: home.shape[0]] * high, axis=0, keepdims=True).astype(jnp.int32)
    place = jnp.sum(columns[home.shape[0] :] * high, axis=0, keepdims=True).astype(jnp.int32)
    owners = _one_hot(owner, holders).astype(BF16)
    places = _one_hot(place, LANES).astype(BF16)
    needed = jnp.minimum(_dot(owners, places, ((1,), (1,))), 1.0)
    row = lax.broadcasted_iota(jnp.int32, (LANES, LANES), 0)
    col = lax.broadcasted_iota(jnp.int32, (LANES, LANES), 1)
    slot = _dot(needed.astype(BF16), (row < col).astype(F32).astype(BF16))
    marked = jnp.where(needed > 0.0, slot, -1.0)
    slots = lax.broadcasted_iota(jnp.int32, (CAP, LANES), 0).astype(F32)
    for holder in range(holders):
        want_ref[holder] = (marked[holder : holder + 1, :] == slots).astype(F32).astype(BF16)
    slot = jnp.minimum(slot, CAP - 1.0)
    of_pair = _dot(slot.astype(BF16), owners, ((0,), (0,)))
    slot = jnp.sum(of_pair * _one_hot(place, LANES), axis=0, keepdims=True)
    position = owner * CAP + slot.astype(jnp.int32)
    position = jnp.broadcast_to(position.astype(F32), (LANES, position.shape[1])).T
    lane = lax.broadcasted_iota(jnp.int32, position.shape, 1).astype(F32)
    for start in range(0, holders * CAP, LANES):
        pick_ref[:, start : start + LANES] = (position - start == lane).astype(F32).astype(BF16)
    copies[2].wait()


ROWS = 16


def transform_kernel(x_ref, table_hbm, yh_ref, yl_ref, table_ref, sem):
    copy = pltpu.make_async_copy(table_hbm, table_ref, sem.at[0])
    copy.start()
    row_count = x_ref.shape[0]
    re, im = slice(0, LANES), slice(LANES, 2 * LANES)

    def put(j, rows, cols, value):
        high = value.astype(BF16)
        yh_ref[j, rows, cols] = high
        yl_ref[j, rows, cols] = (value - high.astype(F32)).astype(BF16)

    @pl.loop(0, row_count // ROWS)
    def _(i):
        rows = pl.ds(pl.multiple_of(i * ROWS, ROWS), ROWS)
        x = [x_ref[rows, n * LANES : (n + 1) * LANES].astype(F32) for n in range(HALF)]
        y = _forward32(x)
        put(0, rows, re, y[0][0])
        put(0, rows, im, y[HALF][0])
        for j in range(1, HALF):
            put(j, rows, re, y[j][0])
            put(j, rows, im, y[j][1])

    copy.wait()


def correlate_kernel(yh_ref, yl_ref, table_ref, inverse_ref, pick_ref, lags_ref, spec_ref, power_ref, u_ref, cross_ref):
    pair_count = pick_ref.shape[0] // 2
    re, im = slice(0, LANES), slice(LANES, 2 * LANES)
    for j in range(HALF):
        high, low = _forward_whole(j, table_ref[2 * j]), _forward_whole(j, table_ref[2 * j + 1])
        spec = _dot(yh_ref[j], high) + _dot(yh_ref[j], low) + _dot(yl_ref[j], high)
        spec_ref[j] = spec
        power = spec[:, re] * spec[:, re] + spec[:, im] * spec[:, im]
        power_ref[...] = power if j == 0 else power_ref[...] + power

    power_ref[...] = 1.0 / jnp.sqrt(_band_mean(power_ref[...]) + 1e-05)

    def ends_of(j):
        scale = power_ref[...]
        white = jnp.concatenate(
            [(spec_ref[j, :, re] * scale).astype(BF16), (spec_ref[j, :, im] * scale).astype(BF16)], axis=1
        )
        return _dot(pick_ref[...], white)

    half = pair_count // 2
    queue = [ends_of(0), ends_of(1)]
    for j in range(HALF):
        ends = queue.pop(0)
        if j + 2 < HALF:
            queue.append(ends_of(j + 2))
        a, c = ends[:pair_count], ends[pair_count:]
        cross = jnp.concatenate(
            [
                (a[:, re] * c[:, re] + a[:, im] * c[:, im]).astype(BF16),
                (a[:, im] * c[:, re] - a[:, re] * c[:, im]).astype(BF16),
            ],
            axis=1,
        )
        u_ref[j, :half] = _dot(cross[:half], _inverse_whole(j, inverse_ref[j]))
        cross_ref[j] = cross[half:]

    me = lax.axis_index("seg")
    even = lax.axis_index("tile") % 2 == 0
    blocks = lags_ref.shape[0]
    width = lags_ref.shape[2] // LANES

    def lags_of(rows):
        u = [(u_ref[0, rows, re], None)]
        u += [(u_ref[j, rows, re], u_ref[j, rows, im]) for j in range(1, HALF)]
        u += [(u_ref[0, rows, im], None)]
        lags = _inverse32(u)
        for s in range(blocks):
            place = lax.rem(jnp.where(even, s - me, me - s) + blocks, blocks)
            for h in range(width):
                lags_ref[place, rows, h * LANES : (h + 1) * LANES] = lags[s * width + h].astype(BF16)

    steps = half // ROWS
    for j in range(HALF):
        u_ref[j, half:] = _dot(cross_ref[j], _inverse_whole(j, inverse_ref[j]))
        for i in range(j * steps // HALF, (j + 1) * steps // HALF):
            lags_of(slice(i * ROWS, (i + 1) * ROWS))

    @pl.loop(steps, pair_count // ROWS)
    def _(i):
        lags_of(pl.ds(pl.multiple_of(i * ROWS, ROWS), ROWS))


def pack_kernel(lags_ref, far_ref, ahead_ref, back_ref, ahead1_ref, back1_ref, keep_ref):
    far_ref[...] = lags_ref[4]
    ahead_ref[...], back_ref[...] = lags_ref[3], lags_ref[5]
    ahead1_ref[...], back1_ref[...] = lags_ref[1], lags_ref[7]
    keep_ref[0], keep_ref[1], keep_ref[2] = lags_ref[0], lags_ref[2], lags_ref[6]


def relay_kernel(keep_ref, far_ref, ahead_ref, back_ref, ahead_out_ref, back_out_ref):
    ahead = keep_ref[1].astype(F32) + far_ref[...].astype(F32) + ahead_ref[...].astype(F32)
    back = keep_ref[2].astype(F32) + back_ref[...].astype(F32)
    ahead_out_ref[...] = ahead.astype(BF16)
    back_out_ref[...] = back.astype(BF16)


def early_kernel(keep_ref, back_ref, ahead_ref, out_ref):
    total = keep_ref[0].astype(F32) + back_ref[...].astype(F32) + ahead_ref[...].astype(F32)
    out_ref[...] = total.T


def sum_kernel(back2_ref, ahead2_ref, early_ref, out_ref):
    late = back2_ref[...].astype(F32) + ahead2_ref[...].astype(F32)
    out_ref[...] = (early_ref[...] + late.T).astype(BF16)


VMEM = pl.BlockSpec(memory_space=pltpu.VMEM)
ANY = pl.BlockSpec(memory_space=pl.ANY)
MIB = 1024 * 1024


def _call(kernel, name, inputs, outputs, args, scratch=(), limit=4):
    return pl.pallas_call(
        kernel,
        out_shape=outputs,
        in_specs=inputs,
        out_specs=(VMEM,) * len(outputs),
        scratch_shapes=scratch,
        compiler_params=pltpu.CompilerParams(vmem_limit_bytes=limit * MIB),
        name=name,
    )(*args)


def _in_hbm(value):
    return pltpu.with_memory_space_constraint(value, pltpu.HBM)


def shards(samples, pair_list, sensor_home):
    tiles = lax.axis_size("tile")
    segments = lax.axis_size("seg")
    local = samples[0]
    sens_dev, seg_len = local.shape
    pair_dev = pair_list.shape[1]
    rows = tiles * CAP
    lags = NLAG // segments
    shape = jax.ShapeDtypeStruct
    home = sensor_home.reshape(-1, LANES)
    forward, inverse = _upper_halves(_forward_tables(), _inverse_tables(segments))
    forward = np.stack(_split(forward), axis=1).reshape(2 * HALF, LANES, 2 * LANES)
    inverse = jnp.asarray(inverse.astype(BF16))
    want, pick, inverse = _call(
        functools.partial(request_kernel, tiles),
        "request",
        [ANY] * 3,
        (
            pltpu.VMEM((tiles, CAP, sens_dev), BF16),
            pltpu.VMEM((2 * pair_dev, rows), BF16),
            pltpu.VMEM(inverse.shape, BF16),
        ),
        (_in_hbm(pair_list), _in_hbm(home), _in_hbm(inverse)),
        [
            pltpu.VMEM(pair_list.shape, jnp.int32),
            pltpu.VMEM(home.shape, jnp.int32),
            pltpu.SemaphoreType.DMA((3,)),
        ],
    )
    asked = lax.all_to_all(want, "tile", split_axis=0, concat_axis=0, tiled=True)
    outgoing = jnp.dot(asked.reshape(rows, sens_dev), local, preferred_element_type=F32).astype(BF16)
    arrived = lax.all_to_all(
        outgoing.reshape(tiles, CAP, seg_len), "tile", split_axis=0, concat_axis=0, tiled=True
    )
    lag_block = (pair_dev, lags)
    spectra = pltpu.VMEM((HALF, rows, 2 * LANES), BF16)
    yh, yl, forward = _call(
        transform_kernel,
        "transform",
        [VMEM, ANY],
        (spectra, spectra, pltpu.VMEM(forward.shape, BF16)),
        (arrived.reshape(rows, seg_len), _in_hbm(jnp.asarray(forward))),
        [pltpu.SemaphoreType.DMA((1,))],
        limit=16,
    )
    (blocks,) = _call(
        correlate_kernel,
        "correlate",
        [VMEM] * 5,
        (pltpu.VMEM((segments,) + lag_block, BF16),),
        (yh, yl, forward, inverse, pick),
        [
            pltpu.VMEM((HALF, rows, 2 * LANES), F32),
            pltpu.VMEM((rows, LANES), F32),
            pltpu.VMEM((HALF, pair_dev, 2 * LANES), F32),
            pltpu.VMEM((HALF, pair_dev // 2, 2 * LANES), BF16),
        ],
        limit=24,
    )
    far, ahead, back, ahead1, back1, keep = _call(
        pack_kernel,
        "pack",
        [VMEM],
        tuple(pltpu.VMEM(n + lag_block, BF16) for n in ((), (), (), (), (), (3,))),
        (blocks,),
    )

    def shift(value, steps):
        ring = [
            (s * tiles + t, (s + (-steps if t % 2 else steps)) % segments * tiles + t)
            for s in range(segments)
            for t in range(tiles)
        ]
        return lax.ppermute(value, ("seg", "tile"), ring)

    far, ahead, back = shift(far, 2), shift(ahead, 1), shift(back, -1)
    ahead1, back1 = shift(ahead1, 1), shift(back1, -1)
    ahead2, back2 = _call(
        relay_kernel,
        "relay",
        [VMEM] * 4,
        (pltpu.VMEM(lag_block, BF16),) * 2,
        (keep, far, ahead, back),
    )
    ahead2, back2 = shift(ahead2, 2), shift(back2, -2)
    (early,) = _call(
        early_kernel, "early", [VMEM] * 3, (pltpu.VMEM((lags, pair_dev), F32),), (keep, back1, ahead1)
    )
    (out,) = _call(
        sum_kernel, "stack", [VMEM] * 3, (shape((lags, pair_dev), BF16),), (back2, ahead2, early)
    )
    return out


def solution(mesh):
    return jax.shard_map(
        shards,
        mesh=mesh,
        in_specs=(P("seg", "tile", None), P(None, "tile"), P()),
        out_specs=P("seg", "tile"),
        check_vma=False,
    )
```
